32 devices in a mesh: rng: 4 (over y, x), azi: 8 (over z, core).
Axes of the slice: x: 2, y: 2, z: 4, core: 2. Of those that a mesh axis runs over, the one named last changes fastest.
Arguments:
- observed: float32 [512, 2048], P('rng', 'azi'), may hold values from -6 to 6
- psf_tiles: float32 [4, 16, 121], P('rng', 'azi'), may hold values from 0.002 to 0.02
Outputs:
- estimate: float32 [512, 2048], P('rng', 'azi')
- residual: float32 [512, 2048], P('rng', 'azi')
The draws below stay inside these ranges and needn't reach their ends.
All inputs are finite; a program needn't handle non-finite values.
Results may differ from the reference program's by a relative error of at most 0.00035.
Values sent between devices are 32-bit elements; how exact they have to be, the bound alone decides.
No kernel may reach another device: no remote copies, remote signals or barrier semaphores. Data moves between devices by JAX's collectives and lax.ppermute only.
A program may use at most 64 MiB of HBM per device.

```python
import math
import jax
import jax.numpy as jnp
from jax import lax

TILE = 128
KSIZE = 11
ITERS = 2
RADIUS = 5
IMG_ROWS = 512
IMG_COLS = 2048


def level_of(rng, extent, split, low, high):
    factor_of, own = 1.0, jax.random.fold_in(rng, 6)
    for position, parts in split:
        draws = jnp.exp(jax.random.uniform(jax.random.fold_in(own, position), (parts,), jnp.float32, low / len(split), high / len(split)))
        factor_of = factor_of * jnp.repeat(draws, extent[position] // parts).reshape([-1 if axis == position else 1 for axis in range(len(extent))])
    return factor_of


def centred(rng, shape, deviation, limit, cuts=(), dtype=jnp.bfloat16):
    result = jax.random.normal(rng, shape, jnp.float32) * deviation
    if len(cuts) > 0:
        result = level_of(rng, shape, cuts, -0.22, 0.18) * result
    return jnp.clip(result, min=-limit, max=limit).astype(dtype)


def setup_inputs(seed: int = 0) -> dict:
    key_list = jax.random.split(jax.random.key(seed), 3)
    observed = centred(key_list[0], (IMG_ROWS, IMG_COLS), 1.0, 6.0, ((0, 4), (1, 8)), jnp.float32)
    psf_tiles = jnp.clip(jnp.exp(math.log(0.02) - 2.30258502 * jax.random.uniform(key_list[1], (IMG_ROWS // TILE, IMG_COLS // TILE, KSIZE * KSIZE), jnp.float32) ** level_of(key_list[1], (IMG_ROWS // TILE, IMG_COLS // TILE, KSIZE * KSIZE), ((0, 4), (1, 8)), -0.2, 0.2)), 0.002, 0.02)
    return {"observed": observed, "psf_tiles": psf_tiles}


def blur(field, psf_tiles):
    tiles_r = IMG_ROWS // TILE
    tiles_c = IMG_COLS // TILE
    padded = jnp.pad(field, RADIUS)

    def add_tap(tap, summed):
        tap_index = jnp.asarray(tap).astype(jnp.int32)
        row_off = tap_index // KSIZE
        col_off = tap_index % KSIZE
        piece = lax.dynamic_slice(padded, (row_off, col_off), (IMG_ROWS, IMG_COLS))
        weight = lax.dynamic_index_in_dim(psf_tiles, tap_index, 2, keepdims=False)
        return summed + piece.reshape(tiles_r, TILE, tiles_c, TILE) * weight[:, None, :, None]

    start = jnp.zeros((tiles_r, TILE, tiles_c, TILE), jnp.float32)
    summed = lax.fori_loop(0, KSIZE * KSIZE, add_tap, start)
    return summed.reshape(IMG_ROWS, IMG_COLS)


def blur_adjoint(field, psf_tiles):
    tiles_r = IMG_ROWS // TILE
    tiles_c = IMG_COLS // TILE
    shaped = field.reshape(tiles_r, TILE, tiles_c, TILE)

    def add_tap(tap, extended):
        tap_index = jnp.asarray(tap).astype(jnp.int32)
        row_off = tap_index // KSIZE
        col_off = tap_index % KSIZE
        weight = lax.dynamic_index_in_dim(psf_tiles, tap_index, 2, keepdims=False)
        term = (shaped * weight[:, None, :, None]).reshape(IMG_ROWS, IMG_COLS)
        current = lax.dynamic_slice(extended, (row_off, col_off), (IMG_ROWS, IMG_COLS))
        return lax.dynamic_update_slice(extended, current + term, (row_off, col_off))

    start = jnp.zeros((IMG_ROWS + 2 * RADIUS, IMG_COLS + 2 * RADIUS), jnp.float32)
    extended = lax.fori_loop(0, KSIZE * KSIZE, add_tap, start)
    return extended[RADIUS:RADIUS + IMG_ROWS, RADIUS:RADIUS + IMG_COLS]


def reference(observed, psf_tiles):
    estimate = jnp.zeros_like(observed)
    residual = observed
    gradient = blur_adjoint(residual, psf_tiles)
    direction = gradient
    gamma = jnp.sum(gradient * gradient)
    for step in range(ITERS):
        image = blur(direction, psf_tiles)
        delta = jnp.sum(image * image)
        alpha = gamma / delta
        estimate = estimate + alpha * direction
        residual = residual - alpha * image
        if step + 1 < ITERS:
            gradient = blur_adjoint(residual, psf_tiles)
            gamma_new = jnp.sum(gradient * gradient)
            direction = gradient + (gamma_new / gamma) * direction
            gamma = gamma_new
    return estimate, residual
```

```python
import jax
import jax.numpy as jnp
from jax import lax
from jax.experimental import pallas as pl
from jax.experimental.pallas import tpu as pltpu
from jax.sharding import PartitionSpec as P

TILE = 128
KSIZE = 11
RADIUS = 5
TAPS = KSIZE * KSIZE
LANES = 128
HALO = 24
REACH = 20
WINDOWS = 3
ROWS = TILE + 2 * HALO
SLOTS = (KSIZE + 1) // 2
DEPTH = SLOTS * LANES
MAIN = 144
REGIONS = ((0, 1, 24), (1, 2, 64), (2, 3, 104))
VMEM = pl.BlockSpec(memory_space=pltpu.VMEM)


def call(kernel, out_shape, scratch=(), limit=4):
    single = isinstance(out_shape, jax.ShapeDtypeStruct)
    return pl.pallas_call(
        kernel,
        out_shape=out_shape,
        out_specs=VMEM if single else [VMEM] * len(out_shape),
        scratch_shapes=list(scratch),
        compiler_params=pltpu.CompilerParams(vmem_limit_bytes=limit * 2**20),
    )


def f32(*shape):
    return jax.ShapeDtypeStruct(shape, jnp.float32)


def lanes_of(shape):
    return lax.broadcasted_iota(jnp.int32, shape, len(shape) - 1)


def is_odd(axis):
    return lax.axis_index(axis) % 2 == 1


def columns_kernel(block_ref, psf_ref, near_ref, far_ref):
    lane = lanes_of((32, LANES))

    def packed(half, first):
        out = jnp.zeros((32, LANES), jnp.float32)
        for part in range(4):
            rows = block_ref[32 * part : 32 * part + 32, LANES * half : LANES * half + LANES]
            moved = pltpu.roll(rows, (32 * part - first) % LANES, 1)
            out = jnp.where((lane >= 32 * part) & (lane < 32 * part + HALO), moved, out)
        return out

    left, right = packed(0, 0), packed(1, LANES - HALO)
    odd = is_odd("azi")
    near_ref[:32] = jnp.where(odd, left, right)
    far_ref[:32] = jnp.where(odd, right, left)
    near_ref[32:] = jnp.zeros((8, LANES), jnp.float32)
    far_ref[32:] = jnp.zeros((8, LANES), jnp.float32)
    near_ref[32:33, :TAPS] = jnp.where(odd, psf_ref[0:1], psf_ref[1:2])
    far_ref[32:33, :TAPS] = jnp.where(odd, psf_ref[1:2], psf_ref[0:1])


def rows_kernel(block_ref, psf_ref, near_ref, far_ref, wide_ref, taps_ref, one_ref, two_ref, top, low):
    odd = is_odd("azi")
    lane = lanes_of((32, LANES))
    near, far = near_ref[:32], far_ref[:32]
    left = jnp.where(odd, near, far)
    right = jnp.where(odd, far, near)
    for part in range(4):
        rows = slice(32 * part, 32 * part + 32)
        first = block_ref[rows, :LANES]
        second = block_ref[rows, LANES:]
        halo_left = pltpu.roll(left, (-32 * part) % LANES, 1)
        halo_right = pltpu.roll(right, (LANES - HALO - 32 * part) % LANES, 1)
        wide_ref[rows, :LANES] = jnp.where(lane < HALO, halo_left, pltpu.roll(first, HALO, 1))
        wide_ref[rows, LANES : 2 * LANES] = jnp.where(
            lane < 64, pltpu.roll(first, 64, 1), pltpu.roll(second, 64, 1)
        )
        wide_ref[rows, 2 * LANES :] = jnp.where(
            lane < LANES - HALO, pltpu.roll(second, LANES - HALO, 1), halo_right
        )
    taps_ref[...] = jnp.zeros((8, LANES), jnp.float32)
    near_taps, far_taps = near_ref[32:33], far_ref[32:33]
    taps_ref[0:1] = jnp.where(odd, near_taps, far_taps)
    taps_ref[1:3, :TAPS] = psf_ref[...]
    taps_ref[3:4] = jnp.where(odd, far_taps, near_taps)
    top[...] = wide_ref[:HALO]
    low[...] = wide_ref[TILE - HALO :]
    top[REACH:, :LANES] = taps_ref[0:4]
    low[: HALO - REACH, :LANES] = taps_ref[0:4]
    odd_row = is_odd("rng")
    one_ref[...] = jnp.where(odd_row, top[...], low[...])
    two_ref[...] = jnp.where(odd_row, low[...], top[...])


def split(value):
    high = value.astype(jnp.bfloat16)
    return high, (value - high.astype(jnp.float32)).astype(jnp.bfloat16)


def product(parts, high, low, dims):
    rows = parts[0].shape[0]

    def dot(a, b):
        return lax.dot_general(a, b, (dims, ((), ())), preferred_element_type=jnp.float32)

    both = dot(jnp.concatenate(parts, axis=0), high)
    return both[:rows] + both[rows:] + dot(parts[0], low)


def shifted(load, offsets):
    pieces = [split(load(offset)) for offset in offsets]
    return [jnp.concatenate([piece[part] for piece in pieces], axis=1) for part in range(2)]


def adjoint_main(padded_ref, window, high_ref, low_ref, pair_ref):
    cols = pl.ds(window * LANES, LANES)
    offsets = [RADIUS - 2 * slot for slot in range(SLOTS)]
    parts = shifted(lambda o: padded_ref[pl.ds(8 + o, MAIN), cols], offsets)
    both = product(parts, high_ref[window], low_ref[window], ((1,), (0,)))
    pair_ref[8:, :] = both[:, LANES:]
    return both[:, :LANES] + pair_ref[pl.ds(7, MAIN), :]


def forward_main(field_ref, window, high_ref, low_ref, pair_ref):
    cols = pl.ds(window * LANES, LANES)
    offsets = [2 * slot - RADIUS for slot in range(SLOTS)]
    parts = shifted(lambda o: field_ref[pl.ds(HALO + o, MAIN), cols], offsets)

    def turned(ref):
        return jnp.concatenate(
            [
                jnp.concatenate(
                    [ref[window, s * LANES : (s + 1) * LANES, e * LANES : (e + 1) * LANES] for s in range(SLOTS)],
                    axis=1,
                )
                for e in range(2)
            ],
            axis=0,
        )

    both = product(parts, turned(high_ref), turned(low_ref), ((1,), (1,)))
    pair_ref[:MAIN, :] = both[:, LANES:]
    return both[:TILE, :LANES] + pair_ref[pl.ds(1, TILE), :]


def start_kernel(wide_ref, taps_ref, high_ref, low_ref, main_ref, padded, pair):
    row = lax.broadcasted_iota(jnp.int32, (LANES, LANES), 0)
    lane8 = lanes_of((8, LANES))
    taps = taps_ref[...]
    for offset in range(2 * SLOTS):
        slot, half = offset // 2, offset % 2
        place = (slice(slot * LANES, (slot + 1) * LANES), slice(half * LANES, (half + 1) * LANES))
        if offset >= KSIZE:
            for window in range(WINDOWS):
                high_ref[(window, *place)] = jnp.zeros((LANES, LANES), jnp.bfloat16)
                low_ref[(window, *place)] = jnp.zeros((LANES, LANES), jnp.bfloat16)
            continue
        line = pltpu.roll(taps, (-KSIZE * offset) % LANES, 1)
        line = pltpu.roll(jnp.where(lane8 < KSIZE, line, 0.0), LANES - RADIUS, 1)
        for window, (before, after, bound) in enumerate(REGIONS):
            base = jnp.where(
                row < bound,
                jnp.broadcast_to(line[before : before + 1], (LANES, LANES)),
                jnp.broadcast_to(line[after : after + 1], (LANES, LANES)),
            )
            band = pltpu.roll(base, 0, 1, stride=1, stride_axis=0)
            high, low = split(band)
            high_ref[(window, *place)] = high
            low_ref[(window, *place)] = low
    padded[:16] = jnp.zeros((16, WINDOWS * LANES), jnp.float32)
    padded[16 + TILE :] = jnp.zeros((16, WINDOWS * LANES), jnp.float32)
    padded[16 : 16 + TILE] = wide_ref[...]
    pair[:8] = jnp.zeros((8, LANES), jnp.float32)
    for window in range(WINDOWS):
        main_ref[:, window * LANES : (window + 1) * LANES] = adjoint_main(
            padded, window, high_ref, low_ref, pair
        )


def strip(load, table, band, window, sign):
    sums = [None] * KSIZE
    for u in range(KSIZE):
        rows = load(u)
        for v in range(KSIZE):
            term = table[band, window, pl.ds(u * KSIZE + v, 1), :] * rows
            sums[v] = term if u == 0 else sums[v] + term
    total = sums[RADIUS]
    for v in range(KSIZE):
        if v != RADIUS:
            total = total + pltpu.roll(sums[v], (sign * (v - RADIUS)) % LANES, 1)
    return total


def finish_kernel(
    wide_ref,
    high_ref,
    low_ref,
    main_ref,
    one_ref,
    two_ref,
    grad_ref,
    image_ref,
    grad2_ref,
    image2_ref,
    record_ref,
    gather_table,
    spread_table,
    edges,
    field,
    padded,
    pair,
):
    odd_row = is_odd("rng")
    one, two = one_ref[...], two_ref[...]
    above = jnp.where(odd_row, one, two)
    below = jnp.where(odd_row, two, one)
    zero = jnp.zeros((1, 1), jnp.float32)
    row24 = lax.broadcasted_iota(jnp.int32, (HALO, 1), 0)
    wide = WINDOWS * LANES
    lane = lanes_of((1, LANES))

    tap_row = lax.broadcasted_iota(jnp.int32, (LANES, LANES), 0)
    tap_lane = lanes_of((LANES, LANES))
    reach = tap_lane - (tap_row % KSIZE - RADIUS)
    for band, taps in enumerate((above[:8, :LANES], below[REACH - 4 :, :LANES])):
        columns = jnp.transpose(taps)
        skip = 0 if band == 0 else 4
        filled = [
            jnp.broadcast_to(columns[:, skip + tile : skip + tile + 1], (LANES, LANES)) for tile in range(4)
        ]
        for window, (before, after, bound) in enumerate(REGIONS):
            spread_table[band, window] = jnp.where(tap_lane < bound, filled[before], filled[after])
            gather_table[band, window] = jnp.where(reach < bound, filled[before], filled[after])

    has_left = lax.axis_index("azi") > 0
    has_right = lax.axis_index("azi") < lax.axis_size("azi") - 1
    has_above = lax.axis_index("rng") > 0
    has_below = lax.axis_index("rng") < lax.axis_size("rng") - 1
    inside = [
        (lane >= HALO) | has_left,
        lane >= 0,
        (lane < LANES - HALO) | has_right,
    ]

    edges[...] = jnp.zeros((2, 40, wide), jnp.float32)
    edges[0, :HALO] = jnp.where(row24 < HALO - REACH, 0.0, above)
    edges[1, 16:] = jnp.where(row24 >= REACH, 0.0, below)
    field[:16] = jnp.zeros((16, wide), jnp.float32)
    field[ROWS - 16 :] = jnp.zeros((16, wide), jnp.float32)
    padded[:16] = jnp.zeros((16, wide), jnp.float32)
    padded[16 + TILE :] = jnp.zeros((16, wide), jnp.float32)
    pair[:8] = jnp.zeros((8, LANES), jnp.float32)

    def cols(window):
        return pl.ds(window * LANES, LANES)

    def put_field(main, window, first, count):
        up = strip(
            lambda u: edges[0, pl.ds(first + 29 - u, count), cols(window)], spread_table, 0, window, 1
        )
        down = strip(lambda u: edges[1, pl.ds(13 - u, count), cols(window)], spread_table, 1, window, 1)
        up_main = main[:16]
        if first < -8:
            up_main = jnp.concatenate([jnp.zeros((-8 - first, LANES), jnp.float32), up_main], axis=0)
        down_main = main[128:]
        if count > 16:
            down_main = jnp.concatenate([down_main, jnp.zeros((count - 16, LANES), jnp.float32)], axis=0)
        up = up + up_main
        down = down + down_main
        keep = inside[window]
        outer = -first
        up_keep = keep & (has_above | (lax.broadcasted_iota(jnp.int32, (count, LANES), 0) >= outer))
        down_keep = keep & (has_below | (lax.broadcasted_iota(jnp.int32, (count, LANES), 0) < 8))
        field[pl.ds(HALO + first, count), cols(window)] = jnp.where(up_keep, up, 0.0)
        field[32:144, cols(window)] = jnp.where(keep, main[16:128], 0.0)
        field[pl.ds(144, count), cols(window)] = jnp.where(down_keep, down, 0.0)

    for window in range(WINDOWS):
        put_field(main_ref[:, window * LANES : (window + 1) * LANES], window, -16, 24)
    grad_ref[...] = field[HALO : HALO + TILE]

    for window in range(WINDOWS):
        image = forward_main(field, window, high_ref, low_ref, pair)
        up = strip(lambda u: field[pl.ds(3 + u, 16), cols(window)], gather_table, 0, window, -1)
        down = strip(lambda u: field[pl.ds(147 + u, 16), cols(window)], gather_table, 1, window, -1)
        padded[16 : 16 + TILE, cols(window)] = image
        edges[0, 8:24, cols(window)] = up
        edges[1, 16:32, cols(window)] = down
    edges[0, :8] = jnp.zeros((8, wide), jnp.float32)
    edges[1, 32:] = jnp.zeros((8, wide), jnp.float32)
    image_ref[...] = padded[16 : 16 + TILE]

    pair[:8] = jnp.zeros((8, LANES), jnp.float32)
    for window in range(WINDOWS):
        main = adjoint_main(padded, window, high_ref, low_ref, pair)
        put_field(main, window, -8, 16)
    grad2_ref[...] = field[HALO : HALO + TILE]

    for window in range(WINDOWS):
        image2_ref[:, window * LANES : (window + 1) * LANES] = forward_main(
            field, window, high_ref, low_ref, pair
        )

    bounds = ((24, 108), (20, 108), (20, 104))
    own = jnp.concatenate([(lane >= low) & (lane < high) for low, high in bounds], axis=1)

    def total(value):
        return jnp.sum(jnp.where(own, jnp.sum(value, axis=0, keepdims=True), 0.0), axis=1, keepdims=True)

    def best(first, second):
        size = total(second * second)
        cross = total(first * second)
        ratio = jnp.where(size > 0.0, cross / jnp.where(size > 0.0, size, 1.0), 0.0)
        rest = first - ratio * second
        return total(first * first), size, ratio, total(rest * rest)

    record = best(grad_ref[...], grad2_ref[...]) + best(image_ref[...], image2_ref[...])
    line = jnp.zeros((1, LANES), jnp.float32)
    for position, value in enumerate(record):
        line = jnp.where(lane == position, value, line)
    record_ref[...] = jnp.broadcast_to(line[None], record_ref.shape)


def combine_kernel(records_ref, block_ref, grad_ref, image_ref, grad2_ref, image2_ref, estimate_ref, residual_ref):
    records = records_ref[:, 0, :]

    def item(position):
        return records[:, position : position + 1]

    def total(value):
        return jnp.sum(value, axis=0, keepdims=True)

    gamma = total(item(0))
    delta = total(item(4))
    alpha = gamma / delta
    gamma_new = total(item(3) + (alpha - item(2)) ** 2 * item(1))
    bent = total(item(7) + (alpha - item(6)) ** 2 * item(5))
    factor = gamma_new / gamma
    delta_new = bent - factor * factor * delta
    alpha_new = gamma_new / delta_new
    first = alpha + alpha_new * (1.0 + factor)
    second = -alpha_new * alpha
    lane = lanes_of((TILE, LANES))

    def own(a_ref, b_ref):
        parts = [
            first * a_ref[:, w * LANES : (w + 1) * LANES] + second * b_ref[:, w * LANES : (w + 1) * LANES]
            for w in range(WINDOWS)
        ]
        middle = pltpu.roll(parts[1], 64, 1)
        left = jnp.where(lane < 84, pltpu.roll(parts[0], LANES - HALO, 1), middle)
        right = jnp.where(lane < 44, middle, pltpu.roll(parts[2], HALO, 1))
        return left, right

    left, right = own(grad_ref, grad2_ref)
    estimate_ref[:, :LANES] = left
    estimate_ref[:, LANES:] = right
    left, right = own(image_ref, image2_ref)
    residual_ref[:, :LANES] = block_ref[:, :LANES] - left
    residual_ref[:, LANES:] = block_ref[:, LANES:] - right


def neighbours(axis):
    count = lax.axis_size(axis)
    near = [(i, i + 1) for i in range(0, count - 1, 2)]
    far = [(i, i + 1) for i in range(1, count - 1, 2)]
    return [pairs + [(b, a) for a, b in pairs] for pairs in (near, far)]


def body(observed, psf_tiles):
    psf = psf_tiles.reshape(2, TAPS)
    devices = lax.axis_size("rng") * lax.axis_size("azi")
    wide = WINDOWS * LANES
    near, far = call(columns_kernel, [f32(40, LANES), f32(40, LANES)])(observed, psf)
    near_pairs, far_pairs = neighbours("azi")
    near = lax.ppermute(near, "azi", near_pairs)
    far = lax.ppermute(far, "azi", far_pairs)
    block, taps, one, two = call(
        rows_kernel,
        [f32(TILE, wide), f32(8, LANES), f32(HALO, wide), f32(HALO, wide)],
        [pltpu.VMEM((HALO, wide), jnp.float32)] * 2,
    )(observed, psf, near, far)
    one_pairs, two_pairs = neighbours("rng")
    one = lax.ppermute(one, "rng", one_pairs)
    two = lax.ppermute(two, "rng", two_pairs)
    matrix = jax.ShapeDtypeStruct((WINDOWS, DEPTH, 2 * LANES), jnp.bfloat16)
    high, low, main = call(
        start_kernel,
        [matrix, matrix, f32(MAIN, wide)],
        [pltpu.VMEM((160, wide), jnp.float32), pltpu.VMEM((152, LANES), jnp.float32)],
        limit=8,
    )(block, taps)
    table = pltpu.VMEM((2, WINDOWS, LANES, LANES), jnp.float32)
    grad, image, grad2, image2, record = call(
        finish_kernel,
        [f32(TILE, wide)] * 4 + [f32(devices, 1, LANES)],
        [
            table,
            table,
            pltpu.VMEM((2, 40, wide), jnp.float32),
            pltpu.VMEM((ROWS, wide), jnp.float32),
            pltpu.VMEM((160, wide), jnp.float32),
            pltpu.VMEM((152, LANES), jnp.float32),
        ],
        limit=12,
    )(block, high, low, main, one, two)
    records = lax.all_to_all(record, ("rng", "azi"), 0, 0, tiled=True)
    estimate, residual = call(combine_kernel, [f32(TILE, 2 * LANES)] * 2)(
        records, observed, grad, image, grad2, image2
    )
    return estimate, residual


def solution(mesh):
    return jax.shard_map(
        body,
        mesh=mesh,
        in_specs=(P("rng", "azi"), P("rng", "azi", None)),
        out_specs=(P("rng", "azi"), P("rng", "azi")),
        check_vma=False,
    )
```

```python
import jax
import jax.numpy as jnp
from jax import lax
from jax.experimental import pallas as pl
from jax.experimental.pallas import tpu as pltpu
from jax.sharding import PartitionSpec as P

TILE = 128
KSIZE = 11
RADIUS = 5
TAPS = KSIZE * KSIZE
LANES = 128
HALO = 24
REACH = 20
WINDOWS = 3
ROWS = TILE + 2 * HALO
SLOTS = (KSIZE + 1) // 2
DEPTH = SLOTS * LANES
MAIN = 144
REGIONS = ((0, 1, 24), (1, 2, 64), (2, 3, 104))
VMEM = pl.BlockSpec(memory_space=pltpu.VMEM)


def call(kernel, out_shape, scratch=(), limit=4):
    single = isinstance(out_shape, jax.ShapeDtypeStruct)
    return pl.pallas_call(
        kernel,
        out_shape=out_shape,
        out_specs=VMEM if single else [VMEM] * len(out_shape),
        scratch_shapes=list(scratch),
        compiler_params=pltpu.CompilerParams(vmem_limit_bytes=limit * 2**20),
    )


def f32(*shape):
    return jax.ShapeDtypeStruct(shape, jnp.float32)


def lanes_of(shape):
    return lax.broadcasted_iota(jnp.int32, shape, len(shape) - 1)


def is_odd(axis):
    return lax.axis_index(axis) % 2 == 1


def columns_kernel(block_ref, psf_ref, near_ref, far_ref):
    lane = lanes_of((32, LANES))

    def packed(half, first):
        out = jnp.zeros((32, LANES), jnp.float32)
        for part in range(4):
            rows = block_ref[32 * part : 32 * part + 32, LANES * half : LANES * half + LANES]
            moved = pltpu.roll(rows, (32 * part - first) % LANES, 1)
            out = jnp.where((lane >= 32 * part) & (lane < 32 * part + HALO), moved, out)
        return out

    left, right = packed(0, 0), packed(1, LANES - HALO)
    odd = is_odd("azi")
    near_ref[:32] = jnp.where(odd, left, right)
    far_ref[:32] = jnp.where(odd, right, left)
    near_ref[32:] = jnp.zeros((8, LANES), jnp.float32)
    far_ref[32:] = jnp.zeros((8, LANES), jnp.float32)
    near_ref[32:33, :TAPS] = jnp.where(odd, psf_ref[0:1], psf_ref[1:2])
    far_ref[32:33, :TAPS] = jnp.where(odd, psf_ref[1:2], psf_ref[0:1])


def rows_kernel(block_ref, psf_ref, near_ref, far_ref, wide_ref, taps_ref, one_ref, two_ref, top, low):
    odd = is_odd("azi")
    lane = lanes_of((32, LANES))
    near, far = near_ref[:32], far_ref[:32]
    left = jnp.where(odd, near, far)
    right = jnp.where(odd, far, near)
    for part in range(4):
        rows = slice(32 * part, 32 * part + 32)
        first = block_ref[rows, :LANES]
        second = block_ref[rows, LANES:]
        halo_left = pltpu.roll(left, (-32 * part) % LANES, 1)
        halo_right = pltpu.roll(right, (LANES - HALO - 32 * part) % LANES, 1)
        wide_ref[rows, :LANES] = jnp.where(lane < HALO, halo_left, pltpu.roll(first, HALO, 1))
        wide_ref[rows, LANES : 2 * LANES] = jnp.where(
            lane < 64, pltpu.roll(first, 64, 1), pltpu.roll(second, 64, 1)
        )
        wide_ref[rows, 2 * LANES :] = jnp.where(
            lane < LANES - HALO, pltpu.roll(second, LANES - HALO, 1), halo_right
        )
    taps_ref[...] = jnp.zeros((8, LANES), jnp.float32)
    near_taps, far_taps = near_ref[32:33], far_ref[32:33]
    taps_ref[0:1] = jnp.where(odd, near_taps, far_taps)
    taps_ref[1:3, :TAPS] = psf_ref[...]
    taps_ref[3:4] = jnp.where(odd, far_taps, near_taps)
    top[...] = wide_ref[:HALO]
    low[...] = wide_ref[TILE - HALO :]
    top[REACH:, :LANES] = taps_ref[0:4]
    low[: HALO - REACH, :LANES] = taps_ref[0:4]
    odd_row = is_odd("rng")
    one_ref[...] = jnp.where(odd_row, top[...], low[...])
    two_ref[...] = jnp.where(odd_row, low[...], top[...])


def split(value):
    high = value.astype(jnp.bfloat16)
    return high, (value - high.astype(jnp.float32)).astype(jnp.bfloat16)


def product(parts, high, low, dims):
    rows = parts[0].shape[0]

    def dot(a, b):
        return lax.dot_general(a, b, (dims, ((), ())), preferred_element_type=jnp.float32)

    both = dot(jnp.concatenate(parts, axis=0), high)
    return both[:rows] + both[rows:] + dot(parts[0], low)


def shifted(load, offsets):
    pieces = [split(load(offset)) for offset in offsets]
    return [jnp.concatenate([piece[part] for piece in pieces], axis=1) for part in range(2)]


def adjoint_main(padded_ref, window, high_ref, low_ref, pair_ref):
    cols = pl.ds(window * LANES, LANES)
    offsets = [RADIUS - 2 * slot for slot in range(SLOTS)]
    parts = shifted(lambda o: padded_ref[pl.ds(8 + o, MAIN), cols], offsets)
    both = product(parts, high_ref[window], low_ref[window], ((1,), (0,)))
    pair_ref[8:, :] = both[:, LANES:]
    return both[:, :LANES] + pair_ref[pl.ds(7, MAIN), :]


def forward_main(field_ref, window, high_ref, low_ref, pair_ref):
    cols = pl.ds(window * LANES, LANES)
    offsets = [2 * slot - RADIUS for slot in range(SLOTS)]
    parts = shifted(lambda o: field_ref[pl.ds(HALO + o, MAIN), cols], offsets)

    def turned(ref):
        return jnp.concatenate(
            [
                jnp.concatenate(
                    [ref[window, s * LANES : (s + 1) * LANES, e * LANES : (e + 1) * LANES] for s in range(SLOTS)],
                    axis=1,
                )
                for e in range(2)
            ],
            axis=0,
        )

    both = product(parts, turned(high_ref), turned(low_ref), ((1,), (1,)))
    pair_ref[:MAIN, :] = both[:, LANES:]
    return both[:TILE, :LANES] + pair_ref[pl.ds(1, TILE), :]


def start_kernel(wide_ref, taps_ref, high_ref, low_ref, main_ref, padded, pair):
    row = lax.broadcasted_iota(jnp.int32, (LANES, LANES), 0)
    lane8 = lanes_of((8, LANES))
    taps = taps_ref[...]
    for offset in range(2 * SLOTS):
        slot, half = offset // 2, offset % 2
        place = (slice(slot * LANES, (slot + 1) * LANES), slice(half * LANES, (half + 1) * LANES))
        if offset >= KSIZE:
            for window in range(WINDOWS):
                high_ref[(window, *place)] = jnp.zeros((LANES, LANES), jnp.bfloat16)
                low_ref[(window, *place)] = jnp.zeros((LANES, LANES), jnp.bfloat16)
            continue
        line = pltpu.roll(taps, (-KSIZE * offset) % LANES, 1)
        line = pltpu.roll(jnp.where(lane8 < KSIZE, line, 0.0), LANES - RADIUS, 1)
        for window, (before, after, bound) in enumerate(REGIONS):
            base = jnp.where(
                row < bound,
                jnp.broadcast_to(line[before : before + 1], (LANES, LANES)),
                jnp.broadcast_to(line[after : after + 1], (LANES, LANES)),
            )
            band = pltpu.roll(base, 0, 1, stride=1, stride_axis=0)
            high, low = split(band)
            high_ref[(window, *place)] = high
            low_ref[(window, *place)] = low
    padded[:16] = jnp.zeros((16, WINDOWS * LANES), jnp.float32)
    padded[16 + TILE :] = jnp.zeros((16, WINDOWS * LANES), jnp.float32)
    padded[16 : 16 + TILE] = wide_ref[...]
    pair[:8] = jnp.zeros((8, LANES), jnp.float32)
    for window in range(WINDOWS):
        main_ref[:, window * LANES : (window + 1) * LANES] = adjoint_main(
            padded, window, high_ref, low_ref, pair
        )


GROUP = 32
GROUPS = 3 * LANES // GROUP


def strip_weights(taps, count, place, keep):
    lane = lanes_of((8, LANES))
    row = lax.broadcasted_iota(jnp.int32, (count, LANES), 0)
    wide_lane = lanes_of((count, LANES))
    pieces = [[] for _ in range(8)]
    for part in range(3):
        u, group = place(lane)
        v = part * (LANES // GROUP) + group
        index = jnp.clip(u * KSIZE + v, 0, LANES - 1)
        base = jnp.take_along_axis(taps, index, axis=1)
        base = jnp.where((u >= 0) & (u < KSIZE) & (v < KSIZE), base, 0.0)
        for tile in range(8):
            moved = pltpu.roll(
                jnp.broadcast_to(base[tile : tile + 1], (count, LANES)), 0, 1, stride=1, stride_axis=0
            )
            pieces[tile].append(jnp.where(keep(wide_lane % GROUP - row), moved, 0.0))
    return [jnp.concatenate(piece, axis=1) for piece in pieces]


def row_product(weights, field):
    high, low = split(field)
    parts = split(weights)
    return product(parts, high, low, ((1,), (0,)))


def spread(rows, sign):
    moved = [rows if v == RADIUS else pltpu.roll(rows, (sign * (v - RADIUS)) % LANES, 1) for v in range(KSIZE)]
    moved.append(jnp.zeros((GROUP * (GROUPS - KSIZE), LANES), jnp.float32))
    return jnp.concatenate(moved, axis=0)


def forward_strips(windows, weights):
    lane = lanes_of((16, LANES))
    stacked = jnp.concatenate([spread(rows, -1) for rows in windows], axis=1)
    result = row_product(jnp.concatenate(weights, axis=0), stacked)
    out = []
    for window, (before, after, bound) in enumerate(REGIONS):
        cols = slice(window * LANES, (window + 1) * LANES)
        out.append(
            jnp.where(lane < bound, result[16 * before : 16 * before + 16, cols], result[16 * after : 16 * after + 16, cols])
        )
    return out


def adjoint_strip(rows, window, weights, count):
    before, after, bound = REGIONS[window]
    lane = lanes_of((GROUP, LANES))
    stacked = jnp.concatenate(
        [spread(jnp.where(lane < bound, rows, 0.0), 1), spread(jnp.where(lane < bound, 0.0, rows), 1)], axis=0
    )
    both = jnp.concatenate([weights[before][:count], weights[after][:count]], axis=1)
    return row_product(both, stacked)


def finish_kernel(
    wide_ref,
    high_ref,
    low_ref,
    main_ref,
    one_ref,
    two_ref,
    grad_ref,
    image_ref,
    grad2_ref,
    image2_ref,
    record_ref,
    edges,
    field,
    padded,
    pair,
):
    odd_row = is_odd("rng")
    one, two = one_ref[...], two_ref[...]
    above = jnp.where(odd_row, one, two)
    below = jnp.where(odd_row, two, one)
    row24 = lax.broadcasted_iota(jnp.int32, (HALO, 1), 0)
    wide = WINDOWS * LANES
    lane = lanes_of((1, LANES))

    row8 = lax.broadcasted_iota(jnp.int32, (8, LANES), 0)
    taps = jnp.where(row8 < 4, above[:8, :LANES], below[HALO - 8 :, :LANES])
    forward_weights = strip_weights(taps, 16, lambda l: (l % GROUP - 3, l // GROUP), lambda d: d >= 3)
    above_weights = strip_weights(taps, 24, lambda l: (13 - l % GROUP, l // GROUP), lambda d: d >= 3)[:4]
    below_weights = strip_weights(
        taps,
        24,
        lambda l: (10 - (l + 13) % LANES % GROUP, (l + 13) % LANES // GROUP),
        lambda d: d <= -3,
    )[4:]

    has_left = lax.axis_index("azi") > 0
    has_right = lax.axis_index("azi") < lax.axis_size("azi") - 1
    has_above = lax.axis_index("rng") > 0
    has_below = lax.axis_index("rng") < lax.axis_size("rng") - 1
    inside = [
        (lane >= HALO) | has_left,
        lane >= 0,
        (lane < LANES - HALO) | has_right,
    ]

    edges[...] = jnp.zeros((2, 48, wide), jnp.float32)
    edges[0, :HALO] = jnp.where(row24 < HALO - REACH, 0.0, above)
    edges[1, 16:40] = jnp.where(row24 >= REACH, 0.0, below)
    field[:16] = jnp.zeros((16, wide), jnp.float32)
    field[ROWS - 16 :] = jnp.zeros((16, wide), jnp.float32)
    padded[:16] = jnp.zeros((16, wide), jnp.float32)
    padded[16 + TILE :] = jnp.zeros((16, wide), jnp.float32)
    pair[:8] = jnp.zeros((8, LANES), jnp.float32)

    def cols(window):
        return pl.ds(window * LANES, LANES)

    def put_field(main, window, first, count):
        up = adjoint_strip(edges[0, pl.ds(first + 16, GROUP), cols(window)], window, above_weights, count)
        down = adjoint_strip(edges[1, 16:48, cols(window)], window, below_weights, count)
        up_main = main[:16]
        if first < -8:
            up_main = jnp.concatenate([jnp.zeros((-8 - first, LANES), jnp.float32), up_main], axis=0)
        down_main = main[128:]
        if count > 16:
            down_main = jnp.concatenate([down_main, jnp.zeros((count - 16, LANES), jnp.float32)], axis=0)
        up = up + up_main
        down = down + down_main
        keep = inside[window]
        outer = -first
        up_keep = keep & (has_above | (lax.broadcasted_iota(jnp.int32, (count, LANES), 0) >= outer))
        down_keep = keep & (has_below | (lax.broadcasted_iota(jnp.int32, (count, LANES), 0) < 8))
        field[pl.ds(HALO + first, count), cols(window)] = jnp.where(up_keep, up, 0.0)
        field[32:144, cols(window)] = jnp.where(keep, main[16:128], 0.0)
        field[pl.ds(144, count), cols(window)] = jnp.where(down_keep, down, 0.0)

    for window in range(WINDOWS):
        put_field(main_ref[:, window * LANES : (window + 1) * LANES], window, -16, 24)
    grad_ref[...] = field[HALO : HALO + TILE]

    for window in range(WINDOWS):
        image = forward_main(field, window, high_ref, low_ref, pair)
        padded[16 : 16 + TILE, cols(window)] = image
    ups = forward_strips([field[:GROUP, cols(w)] for w in range(WINDOWS)], forward_weights[:4])
    downs = forward_strips([field[ROWS - GROUP :, cols(w)] for w in range(WINDOWS)], forward_weights[4:])
    for window in range(WINDOWS):
        edges[0, 8:24, cols(window)] = ups[window]
        edges[1, 16:32, cols(window)] = downs[window]
    edges[0, :8] = jnp.zeros((8, wide), jnp.float32)
    edges[1, 32:40] = jnp.zeros((8, wide), jnp.float32)
    image_ref[...] = padded[16 : 16 + TILE]

    pair[:8] = jnp.zeros((8, LANES), jnp.float32)
    for window in range(WINDOWS):
        main = adjoint_main(padded, window, high_ref, low_ref, pair)
        put_field(main, window, -8, 16)
    grad2_ref[...] = field[HALO : HALO + TILE]

    for window in range(WINDOWS):
        image2_ref[:, window * LANES : (window + 1) * LANES] = forward_main(
            field, window, high_ref, low_ref, pair
        )

    bounds = ((24, 108), (20, 108), (20, 104))
    own = jnp.concatenate([(lane >= low) & (lane < high) for low, high in bounds], axis=1)

    def total(value):
        return jnp.sum(jnp.where(own, jnp.sum(value, axis=0, keepdims=True), 0.0), axis=1, keepdims=True)

    def best(first, second):
        size = total(second * second)
        cross = total(first * second)
        ratio = jnp.where(size > 0.0, cross / jnp.where(size > 0.0, size, 1.0), 0.0)
        rest = first - ratio * second
        return total(first * first), size, ratio, total(rest * rest)

    record = best(grad_ref[...], grad2_ref[...]) + best(image_ref[...], image2_ref[...])
    line = jnp.zeros((1, LANES), jnp.float32)
    for position, value in enumerate(record):
        line = jnp.where(lane == position, value, line)
    record_ref[...] = jnp.broadcast_to(line[None], record_ref.shape)


def combine_kernel(records_ref, block_ref, grad_ref, image_ref, grad2_ref, image2_ref, estimate_ref, residual_ref):
    records = records_ref[:, 0, :]

    def item(position):
        return records[:, position : position + 1]

    def total(value):
        return jnp.sum(value, axis=0, keepdims=True)

    gamma = total(item(0))
    delta = total(item(4))
    alpha = gamma / delta
    gamma_new = total(item(3) + (alpha - item(2)) ** 2 * item(1))
    bent = total(item(7) + (alpha - item(6)) ** 2 * item(5))
    factor = gamma_new / gamma
    delta_new = bent - factor * factor * delta
    alpha_new = gamma_new / delta_new
    first = alpha + alpha_new * (1.0 + factor)
    second = -alpha_new * alpha
    lane = lanes_of((TILE, LANES))

    def own(a_ref, b_ref):
        parts = [
            first * a_ref[:, w * LANES : (w + 1) * LANES] + second * b_ref[:, w * LANES : (w + 1) * LANES]
            for w in range(WINDOWS)
        ]
        middle = pltpu.roll(parts[1], 64, 1)
        left = jnp.where(lane < 84, pltpu.roll(parts[0], LANES - HALO, 1), middle)
        right = jnp.where(lane < 44, middle, pltpu.roll(parts[2], HALO, 1))
        return left, right

    left, right = own(grad_ref, grad2_ref)
    estimate_ref[:, :LANES] = left
    estimate_ref[:, LANES:] = right
    left, right = own(image_ref, image2_ref)
    residual_ref[:, :LANES] = block_ref[:, :LANES] - left
    residual_ref[:, LANES:] = block_ref[:, LANES:] - right


def neighbours(axis):
    count = lax.axis_size(axis)
    near = [(i, i + 1) for i in range(0, count - 1, 2)]
    far = [(i, i + 1) for i in range(1, count - 1, 2)]
    return [pairs + [(b, a) for a, b in pairs] for pairs in (near, far)]


def body(observed, psf_tiles):
    psf = psf_tiles.reshape(2, TAPS)
    devices = lax.axis_size("rng") * lax.axis_size("azi")
    wide = WINDOWS * LANES
    near, far = call(columns_kernel, [f32(40, LANES), f32(40, LANES)])(observed, psf)
    near_pairs, far_pairs = neighbours("azi")
    near = lax.ppermute(near, "azi", near_pairs)
    far = lax.ppermute(far, "azi", far_pairs)
    block, taps, one, two = call(
        rows_kernel,
        [f32(TILE, wide), f32(8, LANES), f32(HALO, wide), f32(HALO, wide)],
        [pltpu.VMEM((HALO, wide), jnp.float32)] * 2,
    )(observed, psf, near, far)
    one_pairs, two_pairs = neighbours("rng")
    one = lax.ppermute(one, "rng", one_pairs)
    two = lax.ppermute(two, "rng", two_pairs)
    matrix = jax.ShapeDtypeStruct((WINDOWS, DEPTH, 2 * LANES), jnp.bfloat16)
    high, low, main = call(
        start_kernel,
        [matrix, matrix, f32(MAIN, wide)],
        [pltpu.VMEM((160, wide), jnp.float32), pltpu.VMEM((152, LANES), jnp.float32)],
        limit=8,
    )(block, taps)
    grad, image, grad2, image2, record = call(
        finish_kernel,
        [f32(TILE, wide)] * 4 + [f32(devices, 1, LANES)],
        [
            pltpu.VMEM((2, 48, wide), jnp.float32),
            pltpu.VMEM((ROWS, wide), jnp.float32),
            pltpu.VMEM((160, wide), jnp.float32),
            pltpu.VMEM((152, LANES), jnp.float32),
        ],
        limit=12,
    )(block, high, low, main, one, two)
    records = lax.all_to_all(record, ("rng", "azi"), 0, 0, tiled=True)
    estimate, residual = call(combine_kernel, [f32(TILE, 2 * LANES)] * 2)(
        records, observed, grad, image, grad2, image2
    )
    return estimate, residual


def solution(mesh):
    return jax.shard_map(
        body,
        mesh=mesh,
        in_specs=(P("rng", "azi"), P("rng", "azi", None)),
        out_specs=(P("rng", "azi"), P("rng", "azi")),
        check_vma=False,
    )
```

```python
import jax
import jax.numpy as jnp
from jax import lax
from jax.experimental import pallas as pl
from jax.experimental.pallas import tpu as pltpu
from jax.sharding import PartitionSpec as P

TILE = 128
KSIZE = 11
RADIUS = 5
TAPS = KSIZE * KSIZE
LANES = 128
HALO = 24
REACH = 20
WINDOWS = 3
ROWS = TILE + 2 * HALO
SLOTS = (KSIZE + 1) // 2
DEPTH = SLOTS * LANES
MAIN = 144
REGIONS = ((0, 1, 24), (1, 2, 64), (2, 3, 104))
VMEM = pl.BlockSpec(memory_space=pltpu.VMEM)


def call(kernel, out_shape, scratch=(), limit=4, inputs=None):
    given = {} if inputs is None else {"in_specs": inputs}
    return pl.pallas_call(
        kernel,
        out_shape=out_shape,
        out_specs=[VMEM] * len(out_shape),
        **given,
        scratch_shapes=list(scratch),
        compiler_params=pltpu.CompilerParams(vmem_limit_bytes=limit * 2**20),
    )


def f32(*shape):
    return jax.ShapeDtypeStruct(shape, jnp.float32)


def lanes_of(shape):
    return lax.broadcasted_iota(jnp.int32, shape, len(shape) - 1)


def is_odd(axis):
    return lax.axis_index(axis) % 2 == 1


def load_kernel(observed_ref, psf_ref, block_ref, taps_ref, far_ref, near_ref, psf, sems):
    half = TILE // 2
    loads = [
        pltpu.make_async_copy(observed_ref.at[pl.ds(half * i, half)], block_ref.at[pl.ds(half * i, half)], sems.at[i])
        for i in range(2)
    ]
    loads.append(pltpu.make_async_copy(psf_ref, psf, sems.at[2]))
    for load in loads:
        load.start()
    taps_ref[...] = jnp.zeros((8, LANES), jnp.float32)
    for load in loads:
        load.wait()
    taps_ref[1:2, :TAPS] = psf[0, 0:1, :]
    taps_ref[2:3, :TAPS] = psf[0, 1:2, :]
    columns_kernel(block_ref, taps_ref, far_ref, near_ref)


def columns_kernel(block_ref, taps_ref, far_ref, near_ref):
    lane = lanes_of((32, LANES))

    def packed(side, first):
        out = jnp.zeros((32, LANES), jnp.float32)
        for part in range(4):
            rows = block_ref[32 * part : 32 * part + 32, LANES * side : LANES * side + LANES]
            moved = pltpu.roll(rows, (32 * part - first) % LANES, 1)
            out = jnp.where((lane >= 32 * part) & (lane < 32 * part + HALO), moved, out)
        return out

    left, right = packed(0, 0), packed(1, LANES - HALO)
    odd = is_odd("azi")
    near_ref[:32] = jnp.where(odd, left, right)
    far_ref[:32] = jnp.where(odd, right, left)
    first, second = taps_ref[...], pltpu.roll(taps_ref[...], 7, 0)
    near_ref[32:] = jnp.where(odd, first, second)
    far_ref[32:] = jnp.where(odd, second, first)


def rows_kernel(block_ref, own_ref, far_ref, near_ref, _, wide_ref, taps_ref, two_ref, one_ref, top, low):
    odd = is_odd("azi")
    lane = lanes_of((32, LANES))
    near, far = near_ref[:32], far_ref[:32]
    left = jnp.where(odd, near, far)
    right = jnp.where(odd, far, near)
    for part in range(4):
        rows = slice(32 * part, 32 * part + 32)
        first = block_ref[rows, :LANES]
        second = block_ref[rows, LANES:]
        halo_left = pltpu.roll(left, (-32 * part) % LANES, 1)
        halo_right = pltpu.roll(right, (LANES - HALO - 32 * part) % LANES, 1)
        wide_ref[rows, :LANES] = jnp.where(lane < HALO, halo_left, pltpu.roll(first, HALO, 1))
        wide_ref[rows, LANES : 2 * LANES] = middle_window(first, second)
        wide_ref[rows, 2 * LANES :] = jnp.where(
            lane < LANES - HALO, pltpu.roll(second, LANES - HALO, 1), halo_right
        )
    near_taps, far_taps = near_ref[33:34], far_ref[33:34]
    taps_ref[...] = own_ref[...]
    taps_ref[0:1] = jnp.where(odd, near_taps, far_taps)
    taps_ref[3:4] = jnp.where(odd, far_taps, near_taps)
    top[...] = wide_ref[:HALO]
    low[...] = wide_ref[TILE - HALO :]
    top[REACH:, :LANES] = taps_ref[0:4]
    low[: HALO - REACH, :LANES] = taps_ref[0:4]
    odd_row = is_odd("rng")
    one_ref[...] = jnp.where(odd_row, top[...], low[...])
    two_ref[...] = jnp.where(odd_row, low[...], top[...])


def middle_window(first, second):
    lane = lanes_of(first.shape)
    return jnp.where(lane < 64, pltpu.roll(first, 64, 1), pltpu.roll(second, 64, 1))


def split(value):
    high = value.astype(jnp.bfloat16)
    return high, (value - high.astype(jnp.float32)).astype(jnp.bfloat16)


def product(parts, high, low, dims):
    rows = parts[0].shape[0]

    def dot(a, b):
        return lax.dot_general(a, b, (dims, ((), ())), preferred_element_type=jnp.float32)

    both = dot(jnp.concatenate(parts, axis=0), high)
    return both[:rows] + both[rows:] + dot(parts[0], low)


def stacked_rows(field_ref, first, count, offsets):
    pieces = [split(field_ref[pl.ds(HALO + first + offset, count), :]) for offset in offsets]
    return [jnp.concatenate([piece[part] for piece in pieces], axis=1) for part in range(2)]


def adjoint_rows(field_ref, block, pair, first, count, lead):
    offsets = [RADIUS - 2 * slot for slot in range(SLOTS)]
    parts = stacked_rows(field_ref, first - lead, count + lead, offsets)
    high, low = [jnp.concatenate([block(part, slot) for slot in range(SLOTS)], axis=0) for part in range(2)]
    both = product(parts, high, low, ((1,), (0,)))
    if lead == 0:
        pair[:8, :] = jnp.zeros((8, LANES), jnp.float32)
    pair[pl.ds(8 if lead == 0 else 0, count + lead), :] = both[:, LANES:]
    return both[lead:, :LANES] + pair[pl.ds(7 if lead == 0 else lead - 1, count), :]


def forward_rows(field_ref, block, pair):
    offsets = [2 * slot - RADIUS for slot in range(SLOTS)]
    parts = stacked_rows(field_ref, 0, MAIN, offsets)

    def turned(part):
        blocks = [block(part, slot) for slot in range(SLOTS)]
        halves = [
            jnp.concatenate([value[:, half * LANES : (half + 1) * LANES] for value in blocks], axis=1)
            for half in range(2)
        ]
        return jnp.concatenate(halves, axis=0)

    both = product(parts, turned(0), turned(1), ((1,), (1,)))
    pair[:MAIN, :] = both[:, LANES:]
    return both[:TILE, :LANES] + pair[pl.ds(1, TILE), :]


def tap_lines(taps):
    spot = (lanes_of((8, LANES)) + RADIUS) % LANES
    return [
        jnp.where(spot < KSIZE, jnp.take_along_axis(taps, jnp.minimum(KSIZE * u + spot, LANES - 1), axis=1), 0.0)
        for u in range(KSIZE)
    ]


def put_band(lines, offset, window, first, count, refs):
    slot, half = offset // 2, offset % 2
    place = (slice(slot * count, (slot + 1) * count), slice(half * LANES, (half + 1) * LANES))
    if offset >= KSIZE:
        for ref in refs:
            ref[place] = jnp.zeros((count, LANES), jnp.bfloat16)
        return
    before, after, bound = REGIONS[window]
    row = first + lax.broadcasted_iota(jnp.int32, (count, LANES), 0)
    left, right = [jnp.broadcast_to(lines[offset][tile : tile + 1], (count, LANES)) for tile in (before, after)]
    base = left if first + count <= bound else right if first >= bound else jnp.where(row < bound, left, right)
    refs[0][place], refs[1][place] = split(pltpu.roll(base, first, 1, stride=1, stride_axis=0))


def inside(window):
    lane = lanes_of((1, LANES))
    if window == 0:
        return (lane >= HALO) | (lax.axis_index("azi") > 0)
    if window == 2:
        return (lane < LANES - HALO) | (lax.axis_index("azi") < lax.axis_size("azi") - 1)
    return lane >= 0


def early_rows(rows, windows, blocks, outs, fields, pairs, between=lambda stage: None):
    own = slice(HALO, HALO + TILE)
    each = range(len(windows))
    keep = [inside(window) for window in windows]
    for i in each:
        for stage in range(4):
            fields[i, stage, :HALO] = jnp.zeros((HALO, LANES), jnp.float32)
            fields[i, stage, HALO + TILE :] = jnp.zeros((HALO, LANES), jnp.float32)
        fields[i, 0, own] = rows[i]
    for i in each:
        main = adjoint_rows(fields.at[i, 0], blocks[i], pairs.at[i, 0], -8, MAIN, 0)
        main = jnp.where(keep[i], main, 0.0)
        outs[i][0][...] = main
        fields[i, 1, HALO - 8 : HALO + TILE + 8] = main
    between(0)
    for i in each:
        image = forward_rows(fields.at[i, 1], blocks[i], pairs.at[i, 1])
        outs[i][1][...] = image
        fields[i, 2, own] = image
    between(1)
    for i in each:
        grad = adjoint_rows(fields.at[i, 2], blocks[i], pairs.at[i, 2], 0, TILE, 16)
        grad = jnp.where(keep[i], grad, 0.0)
        outs[i][2][...] = grad
        fields[i, 3, own] = grad
    between(2)
    for i in each:
        outs[i][3][...] = forward_rows(fields.at[i, 3], blocks[i], pairs.at[i, 3])
    between(3)


PATCH = 32
REST = LANES - PATCH


def middle_kernel(block_ref, taps_ref, *refs):
    outs, sides = refs[:4], (refs[4:6], refs[6:8])
    high, low, fields, pairs = refs[8:]
    lines = tap_lines(taps_ref[...])
    for offset in range(2 * SLOTS):
        put_band(lines, offset, 1, 0, LANES, (high, low))

    def between(stage):
        for offset in range(3 * stage, 3 * stage + 3):
            put_band(lines, offset, 0, PATCH, REST, sides[0])
            put_band(lines, offset, 2, 0, REST, sides[1])

    def block(part, slot):
        return (high, low)[part][slot * LANES : (slot + 1) * LANES, :]

    rows = middle_window(block_ref[:, :LANES], block_ref[:, LANES:])
    early_rows([rows], (1,), [block], [outs], fields, pairs, between)


def sides_kernel(wide_ref, taps_ref, *refs):
    rest, middle = (refs[:2], refs[2:4]), refs[4:8]
    outs, refs = (refs[8:12], refs[12:16]), refs[16:]
    plain_ref, turned_ref, inner_ref, patches, fields, pairs = refs
    taps = taps_ref[...]
    lines = tap_lines(taps)
    for offset in range(2 * SLOTS):
        put_band(lines, offset, 0, 0, PATCH, (patches.at[0, 0], patches.at[0, 1]))
        put_band(lines, offset, 2, REST, PATCH, (patches.at[1, 0], patches.at[1, 1]))

    def piece(side, part, slot):
        whole = rest[side][part][slot * REST : (slot + 1) * REST, :]
        patch = patches[side, part, slot * PATCH : (slot + 1) * PATCH, :]
        return jnp.concatenate([patch, whole] if side == 0 else [whole, patch], axis=0)

    blocks = [lambda part, slot: piece(0, part, slot), lambda part, slot: piece(1, part, slot)]

    def between(stage):
        if stage == 0:
            plain_ref[...] = jnp.concatenate(row_weights(taps, range(4), False), axis=0)
        if stage == 1:
            turned_ref[...] = jnp.concatenate(row_weights(taps, range(4), True), axis=0)

    rows = [wide_ref[:, :LANES], wide_ref[:, 2 * LANES :]]
    early_rows(rows, (0, 2), blocks, outs, fields, pairs, between)
    early = (outs[0], middle, outs[1])
    inner = [[window[0][8 + INNER.start : 8 + INNER.stop] for window in early]]
    inner += [[window[i][INNER] for window in early] for i in range(1, 4)]
    inner_ref[...] = jnp.broadcast_to(record_of(inner, 0), (8, LANES))


GROUP = 32
GROUPS = 3 * LANES // GROUP
EDGE = 4 * RADIUS
COUNT = 24


def row_weights(taps, tiles, turned):
    lane = lanes_of((8, LANES))
    pieces = [[] for _ in tiles]
    for part in range(3):
        u = lane % GROUP
        if turned:
            u = KSIZE - 1 - u
        v = part * (LANES // GROUP) + lane // GROUP
        base = jnp.take_along_axis(taps, jnp.clip(u * KSIZE + v, 0, LANES - 1), axis=1)
        base = jnp.where((u >= 0) & (u < KSIZE) & (v < KSIZE), base, 0.0)
        for piece, tile in zip(pieces, tiles):
            row = jnp.broadcast_to(base[tile : tile + 1], (COUNT, LANES))
            piece.append(pltpu.roll(row, 0, 1, stride=1, stride_axis=0))
    return [jnp.concatenate(piece, axis=1) for piece in pieces]


def spread(rows, sign):
    moved = [rows if v == RADIUS else pltpu.roll(rows, (sign * (v - RADIUS)) % LANES, 1) for v in range(KSIZE)]
    moved.append(jnp.zeros((GROUP * (GROUPS - KSIZE), LANES), rows.dtype))
    return jnp.concatenate(moved, axis=0)


def forward_edge(rows, weights):
    lane = lanes_of((COUNT, LANES))
    parts = [split(value) for value in rows]
    high, low = [jnp.concatenate([spread(part[i], -1) for part in parts], axis=1) for i in range(2)]
    result = product(split(weights), high, low, ((1,), (0,)))
    out = []
    for window, (before, after, bound) in enumerate(REGIONS):
        cols = slice(window * LANES, (window + 1) * LANES)
        left, right = [result[COUNT * tile : COUNT * tile + COUNT, cols] for tile in (before, after)]
        out.append(jnp.where(lane < bound, left, right))
    return out


def adjoint_edge(rows, window, weights):
    before, after, bound = REGIONS[window]
    lane = lanes_of((GROUP, LANES))
    high, low = [
        jnp.concatenate(
            [
                spread(jnp.where(lane < bound, part, jnp.zeros_like(part)), 1),
                spread(jnp.where(lane < bound, jnp.zeros_like(part), part), 1),
            ],
            axis=0,
        )
        for part in split(rows)
    ]
    both = [weights[COUNT * tile : COUNT * tile + COUNT] for tile in (before, after)]
    return product(split(jnp.concatenate(both, axis=1)), high, low, ((1,), (0,)))


def edge_rows(side, message, plain_ref, turned_ref, early, outs, edge, fields):
    wide = WINDOWS * LANES
    each = range(WINDOWS)
    base = 16 if side == 0 else -80
    near = slice(16, 64) if side == 0 else slice(0, 48)
    own = slice(0, 48) if side == 0 else slice(80, 128)
    out = slice(16, 40) if side == 0 else slice(24, 48)
    start = (-15, -10, -5, 0) if side == 0 else (123, 118, 113, 108)
    beyond = lax.axis_index("rng") > 0 if side == 0 else lax.axis_index("rng") < lax.axis_size("rng") - 1
    keep = [inside(window) for window in each]
    row = lax.broadcasted_iota(jnp.int32, (EDGE, LANES), 0)
    half = EDGE // 2

    def cols(window):
        return pl.ds(window * LANES, LANES)

    def spot(stage, reach=0, count=EDGE):
        return pl.ds(start[stage] - reach + base, count)

    def in_image(stage, window):
        inner = row >= -start[stage] if side == 0 else row < TILE - start[stage]
        return keep[window] & (beyond | inner)

    tiles = range(4) if side == 0 else range(4, 8)
    taps = message[:8, :LANES] if side == 0 else message[HALO - 8 :, :LANES]
    turned = jnp.concatenate(row_weights(taps, tiles, True), axis=0)
    plain = jnp.concatenate(row_weights(taps, tiles, False), axis=0)

    row24 = lax.broadcasted_iota(jnp.int32, (HALO, 1), 0)
    if side == 0:
        edge[:HALO] = jnp.where(row24 < HALO - REACH, 0.0, message)
        edge[HALO:] = jnp.zeros((16, wide), jnp.float32)
        strip = slice(4, 36)
    else:
        edge[:16] = jnp.zeros((16, wide), jnp.float32)
        edge[16:] = jnp.where(row24 >= REACH, 0.0, message)
        strip = slice(6, 38)
    for window in each:
        main = early[window][0]
        field = fields.at[0, window]
        if side == 0:
            field[:8] = jnp.zeros((8, LANES), jnp.float32)
            field[8:16] = jnp.where(beyond, main[:8], 0.0)
            field[16:64] = main[8:56]
        else:
            field[:48] = main[88:136]
            field[48:56] = jnp.where(beyond, main[136:], 0.0)
            field[56:] = jnp.zeros((16, LANES), jnp.float32)
        result = adjoint_edge(edge[strip, cols(window)], window, turned)
        field[spot(0), :] += jnp.where(in_image(0, window), result[:EDGE], 0.0)
        outs[0][:, cols(window)] = field[out]

    yield
    out_row = lax.broadcasted_iota(jnp.int32, (4 * COUNT, wide), 0) % COUNT
    mixed = (plain, plain_ref[...]) if side == 0 else (plain_ref[...], plain)
    results = forward_edge(
        [fields[0, window, spot(1, RADIUS, GROUP), :] for window in each], jnp.where(out_row < half, *mixed)
    )
    for window in each:
        field = fields.at[1, window]
        if side == 0:
            field[:16] = jnp.zeros((16, LANES), jnp.float32)
        else:
            field[48:] = jnp.zeros((24, LANES), jnp.float32)
        field[near] = early[window][1][own]
        field[spot(1), :] = results[window][:EDGE]
        outs[1][:, cols(window)] = field[out]

    yield
    in_row = lanes_of((4 * COUNT, wide)) % GROUP
    if side == 0:
        mixed = jnp.where(in_row < half, turned, turned_ref[...])
    else:
        mixed = jnp.where(in_row < EDGE, turned_ref[...], turned)
    for window in each:
        result = adjoint_edge(fields[1, window, spot(2, RADIUS, GROUP), :], window, mixed)
        field = fields.at[2, window]
        if side == 0:
            field[8:16] = jnp.zeros((8, LANES), jnp.float32)
        else:
            field[48:56] = jnp.zeros((8, LANES), jnp.float32)
        field[near] = early[window][2][own]
        field[spot(2), :] = jnp.where(in_image(2, window), result[:EDGE], 0.0)
        outs[2][:, cols(window)] = field[out]

    yield
    results = forward_edge([fields[2, window, spot(3, RADIUS, GROUP), :] for window in each], plain_ref[...])
    for window in each:
        rest = COUNT - EDGE
        if side == 0:
            outs[3][EDGE:, cols(window)] = early[window][3][EDGE:COUNT]
            outs[3][:EDGE, cols(window)] = results[window][:EDGE]
        else:
            outs[3][:rest, cols(window)] = early[window][3][TILE - COUNT : TILE - EDGE]
            outs[3][rest:, cols(window)] = results[window][:EDGE]
    yield


INNER = slice(COUNT, TILE - COUNT)


def record_of(values, position):
    lane = lanes_of((1, LANES))
    bounds = ((24, 108), (20, 108), (20, 104))

    def total(pieces):
        sums = [
            jnp.where((lane >= low) & (lane < high), jnp.sum(piece, axis=0, keepdims=True), 0.0)
            for piece, (low, high) in zip(pieces, bounds)
        ]
        return jnp.sum(sums[0] + sums[1] + sums[2], axis=1, keepdims=True)

    def best(first, second):
        size = total([b * b for b in second])
        cross = total([a * b for a, b in zip(first, second)])
        ratio = jnp.where(size > 0.0, cross / jnp.where(size > 0.0, size, 1.0), 0.0)
        rest = total([(a - ratio * b) ** 2 for a, b in zip(first, second)])
        return total([a * a for a in first]), size, ratio, rest

    grad, image, grad2, image2 = values
    line = jnp.zeros((1, LANES), jnp.float32)
    for index, value in enumerate(best(grad, grad2) + best(image, image2)):
        line = jnp.where(lane == position + index, value, line)
    return line


def edge_kernel(*refs):
    early = [refs[4 * window : 4 * window + 4] for window in (1, 0, 2)]
    two_ref, one_ref, plain_ref, turned_ref, inner_ref = refs[12:17]
    tops, lows, record_ref, edge, fields = refs[17:21], refs[21:25], *refs[25:]
    odd = is_odd("rng")
    one, two = one_ref[...], two_ref[...]
    above, below = jnp.where(odd, one, two), jnp.where(odd, two, one)
    top = edge_rows(0, above, plain_ref, turned_ref, early, tops, edge.at[0], fields.at[0])
    low = edge_rows(1, below, plain_ref, turned_ref, early, lows, edge.at[1], fields.at[1])
    for _ in zip(top, low):
        pass

    def windows(i):
        both = jnp.concatenate([tops[i][...], lows[i][...]], axis=0)
        return [both[:, w * LANES : (w + 1) * LANES] for w in range(WINDOWS)]

    line = inner_ref[:1] + record_of([windows(i) for i in range(4)], 8)
    record_ref[...] = jnp.broadcast_to(line[None], record_ref.shape)


def combine_kernel(records_ref, block_ref, *refs):
    early = [refs[4 * window : 4 * window + 4] for window in (1, 0, 2)]
    tops, lows, (estimate_ref, residual_ref) = refs[12:16], refs[16:20], refs[20:]
    records = records_ref[:, 0, :]
    lane = lanes_of((1, LANES))

    def total(value, place):
        wanted = (lane % 8 == place) & (lane < 24)
        return jnp.sum(jnp.where(wanted, jnp.sum(value, axis=0, keepdims=True), 0.0), axis=1, keepdims=True)

    gamma = total(records, 0)
    delta = total(records, 4)
    alpha = gamma / delta
    apart = records + (alpha - pltpu.roll(records, 1, 1)) ** 2 * pltpu.roll(records, 2, 1)
    gamma_new = total(apart, 3)
    bent = total(apart, 7)
    factor = gamma_new / gamma
    delta_new = bent - factor * factor * delta
    alpha_new = gamma_new / delta_new
    first = alpha + alpha_new * (1.0 + factor)
    second = -alpha_new * alpha

    def own(a, b):
        parts = [first * a[w] + second * b[w] for w in range(WINDOWS)]
        lanes = lanes_of(parts[0].shape)
        middle = pltpu.roll(parts[1], 64, 1)
        left = jnp.where(lanes < 84, pltpu.roll(parts[0], LANES - HALO, 1), middle)
        right = jnp.where(lanes < 44, middle, pltpu.roll(parts[2], HALO, 1))
        return left, right

    def windows(ref):
        return [ref[:, w * LANES : (w + 1) * LANES] for w in range(WINDOWS)]

    for rows, pieces in (
        (slice(0, COUNT), lambda i: windows(tops[i])),
        (INNER, lambda i: [early[w][i][slice(8 + COUNT, 8 + TILE - COUNT) if i == 0 else INNER] for w in range(WINDOWS)]),
        (slice(TILE - COUNT, TILE), lambda i: windows(lows[i])),
    ):
        left, right = own(pieces(0), pieces(2))
        estimate_ref[rows, :LANES] = left
        estimate_ref[rows, LANES:] = right
        left, right = own(pieces(1), pieces(3))
        residual_ref[rows, :LANES] = block_ref[rows, :LANES] - left
        residual_ref[rows, LANES:] = block_ref[rows, LANES:] - right


def neighbours(axis):
    count = lax.axis_size(axis)
    near = [(i, i + 1) for i in range(0, count - 1, 2)]
    far = [(i, i + 1) for i in range(1, count - 1, 2)]
    return [pairs + [(b, a) for a, b in pairs] for pairs in (near, far)]


def body(observed, psf_tiles):
    devices = lax.axis_size("rng") * lax.axis_size("azi")
    wide = WINDOWS * LANES
    block, own, far, near = call(
        load_kernel,
        [f32(TILE, 2 * LANES), f32(8, LANES), f32(40, LANES), f32(40, LANES)],
        [pltpu.VMEM((1, 2, TAPS), jnp.float32), pltpu.SemaphoreType.DMA((3,))],
        inputs=[pl.BlockSpec(memory_space=pltpu.HBM)] * 2,
    )(
        pltpu.with_memory_space_constraint(observed, pltpu.HBM),
        pltpu.with_memory_space_constraint(psf_tiles, pltpu.HBM),
    )
    near_pairs, far_pairs = neighbours("azi")
    far = lax.ppermute(far, "azi", far_pairs)
    near = lax.ppermute(near, "azi", near_pairs)
    early = [f32(MAIN, LANES)] + [f32(TILE, LANES)] * 3
    rest = [jax.ShapeDtypeStruct((SLOTS * REST, 2 * LANES), jnp.bfloat16)] * 4

    def scratch(windows):
        return [
            pltpu.VMEM((windows, 4, ROWS, LANES), jnp.float32),
            pltpu.VMEM((windows, 4, MAIN + 8, LANES), jnp.float32),
        ]

    *middle, high0, low0, high2, low2 = call(
        middle_kernel, early + rest, [pltpu.VMEM((DEPTH, 2 * LANES), jnp.bfloat16)] * 2 + scratch(1), limit=8
    )(block, own)
    wide_block, taps, two, one = call(
        rows_kernel,
        [f32(TILE, wide), f32(8, LANES), f32(HALO, wide), f32(HALO, wide)],
        [pltpu.VMEM((HALO, wide), jnp.float32)] * 2,
    )(block, own, far, near, middle[0])
    one_pairs, two_pairs = neighbours("rng")
    two = lax.ppermute(two, "rng", two_pairs)
    one = lax.ppermute(one, "rng", one_pairs)
    *sides, plain, turned, inner = call(
        sides_kernel,
        early * 2 + [f32(4 * COUNT, wide)] * 2 + [f32(8, LANES)],
        [pltpu.VMEM((2, 2, SLOTS * PATCH, 2 * LANES), jnp.bfloat16)] + scratch(2),
        limit=8,
    )(wide_block, taps, high0, low0, high2, low2, *middle)
    *edges, record = call(
        edge_kernel,
        [f32(COUNT, wide)] * 8 + [f32(devices, 1, LANES)],
        [pltpu.VMEM((2, 40, wide), jnp.float32), pltpu.VMEM((2, 3, WINDOWS, 72, LANES), jnp.float32)],
        limit=8,
    )(*middle, *sides, two, one, plain, turned, inner)
    records = lax.all_to_all(record, ("rng", "azi"), 0, 0, tiled=True)
    estimate, residual = call(combine_kernel, [f32(TILE, 2 * LANES)] * 2)(
        records, block, *middle, *sides, *edges
    )
    return estimate, residual


def solution(mesh):
    return jax.shard_map(
        body,
        mesh=mesh,
        in_specs=(P("rng", "azi"), P("rng", "azi", None)),
        out_specs=(P("rng", "azi"), P("rng", "azi")),
        check_vma=False,
    )
```

```python
import jax
import jax.numpy as jnp
from jax import lax
from jax.experimental import pallas as pl
from jax.experimental.pallas import tpu as pltpu
from jax.sharding import PartitionSpec as P

TILE = 128
KSIZE = 11
RADIUS = 5
TAPS = KSIZE * KSIZE
LANES = 128
HALO = 24
REACH = 20
WINDOWS = 3
ROWS = TILE + 2 * HALO
SLOTS = (KSIZE + 1) // 2
DEPTH = SLOTS * LANES
MAIN = 144
REGIONS = ((0, 1, 24), (1, 2, 64), (2, 3, 104))
VMEM = pl.BlockSpec(memory_space=pltpu.VMEM)


def call(kernel, out_shape, scratch=(), limit=4, inputs=None):
    given = {} if inputs is None else {"in_specs": inputs}
    return pl.pallas_call(
        kernel,
        out_shape=out_shape,
        out_specs=[VMEM] * len(out_shape),
        **given,
        scratch_shapes=list(scratch),
        compiler_params=pltpu.CompilerParams(vmem_limit_bytes=limit * 2**20),
    )


def f32(*shape):
    return jax.ShapeDtypeStruct(shape, jnp.float32)


def lanes_of(shape):
    return lax.broadcasted_iota(jnp.int32, shape, len(shape) - 1)


def is_odd(axis):
    return lax.axis_index(axis) % 2 == 1


def load_kernel(observed_ref, psf_ref, block_ref, taps_ref, far_ref, near_ref, psf, sems):
    half = TILE // 2
    loads = [
        pltpu.make_async_copy(observed_ref.at[pl.ds(half * i, half)], block_ref.at[pl.ds(half * i, half)], sems.at[i])
        for i in range(2)
    ]
    loads.append(pltpu.make_async_copy(psf_ref, psf, sems.at[2]))
    for load in loads:
        load.start()
    taps_ref[...] = jnp.zeros((8, LANES), jnp.float32)
    for load in loads:
        load.wait()
    taps_ref[1:2, :TAPS] = psf[0, 0:1, :]
    taps_ref[2:3, :TAPS] = psf[0, 1:2, :]
    columns_kernel(block_ref, taps_ref, far_ref, near_ref)


def columns_kernel(block_ref, taps_ref, far_ref, near_ref):
    lane = lanes_of((32, LANES))

    def packed(side, first):
        out = jnp.zeros((32, LANES), jnp.float32)
        for part in range(4):
            rows = block_ref[32 * part : 32 * part + 32, LANES * side : LANES * side + LANES]
            moved = pltpu.roll(rows, (32 * part - first) % LANES, 1)
            out = jnp.where((lane >= 32 * part) & (lane < 32 * part + HALO), moved, out)
        return out

    left, right = packed(0, 0), packed(1, LANES - HALO)
    odd = is_odd("azi")
    near_ref[:32] = jnp.where(odd, left, right)
    far_ref[:32] = jnp.where(odd, right, left)
    first, second = taps_ref[...], pltpu.roll(taps_ref[...], 7, 0)
    near_ref[32:] = jnp.where(odd, first, second)
    far_ref[32:] = jnp.where(odd, second, first)


def rows_kernel(block_ref, own_ref, far_ref, near_ref, _, wide_ref, taps_ref, two_ref, one_ref, top, low):
    odd = is_odd("azi")
    lane = lanes_of((32, LANES))
    near, far = near_ref[:32], far_ref[:32]
    has_left = lax.axis_index("azi") > 0
    has_right = lax.axis_index("azi") < lax.axis_size("azi") - 1
    left = jnp.where(has_left, jnp.where(odd, near, far), 0.0)
    right = jnp.where(has_right, jnp.where(odd, far, near), 0.0)
    for part in range(4):
        rows = slice(32 * part, 32 * part + 32)
        first = block_ref[rows, :LANES]
        second = block_ref[rows, LANES:]
        halo_left = pltpu.roll(left, (-32 * part) % LANES, 1)
        halo_right = pltpu.roll(right, (LANES - HALO - 32 * part) % LANES, 1)
        wide_ref[rows, :LANES] = jnp.where(lane < HALO, halo_left, pltpu.roll(first, HALO, 1))
        wide_ref[rows, LANES : 2 * LANES] = middle_window(first, second)
        wide_ref[rows, 2 * LANES :] = jnp.where(
            lane < LANES - HALO, pltpu.roll(second, LANES - HALO, 1), halo_right
        )
    near_taps, far_taps = near_ref[33:34], far_ref[33:34]
    taps_ref[...] = own_ref[...]
    taps_ref[0:1] = jnp.where(has_left, jnp.where(odd, near_taps, far_taps), 0.0)
    taps_ref[3:4] = jnp.where(has_right, jnp.where(odd, far_taps, near_taps), 0.0)
    top[...] = wide_ref[:HALO]
    low[...] = wide_ref[TILE - HALO :]
    top[REACH:, :LANES] = taps_ref[0:4]
    low[: HALO - REACH, :LANES] = taps_ref[0:4]
    odd_row = is_odd("rng")
    one_ref[...] = jnp.where(odd_row, top[...], low[...])
    two_ref[...] = jnp.where(odd_row, low[...], top[...])


def middle_window(first, second):
    lane = lanes_of(first.shape)
    return jnp.where(lane < 64, pltpu.roll(first, 64, 1), pltpu.roll(second, 64, 1))


def split(value):
    high = value.astype(jnp.bfloat16)
    return high, (value - high.astype(jnp.float32)).astype(jnp.bfloat16)


def product(parts, high, low, dims):
    rows = parts[0].shape[0]

    def dot(a, b):
        return lax.dot_general(a, b, (dims, ((), ())), preferred_element_type=jnp.float32)

    both = dot(jnp.concatenate(parts, axis=0), high)
    return both[:rows] + both[rows:] + dot(parts[0], low)


def stacked_rows(field_ref, first, count, offsets):
    pieces = [split(field_ref[pl.ds(HALO + first + offset, count), :]) for offset in offsets]
    return [jnp.concatenate([piece[part] for piece in pieces], axis=1) for part in range(2)]


def adjoint_rows(field_ref, block, pair, first, count, lead):
    offsets = [RADIUS - 2 * slot for slot in range(SLOTS)]
    parts = stacked_rows(field_ref, first - lead, count + lead, offsets)
    high, low = [jnp.concatenate([block(part, slot) for slot in range(SLOTS)], axis=0) for part in range(2)]
    both = product(parts, high, low, ((1,), (0,)))
    if lead == 0:
        pair[:8, :] = jnp.zeros((8, LANES), jnp.float32)
    pair[pl.ds(8 if lead == 0 else 0, count + lead), :] = both[:, LANES:]
    return both[lead:, :LANES] + pair[pl.ds(7 if lead == 0 else lead - 1, count), :]


def forward_rows(field_ref, block, pair):
    offsets = [2 * slot - RADIUS for slot in range(SLOTS)]
    parts = stacked_rows(field_ref, 0, MAIN, offsets)

    def turned(part):
        blocks = [block(part, slot) for slot in range(SLOTS)]
        halves = [
            jnp.concatenate([value[:, half * LANES : (half + 1) * LANES] for value in blocks], axis=1)
            for half in range(2)
        ]
        return jnp.concatenate(halves, axis=0)

    both = product(parts, turned(0), turned(1), ((1,), (1,)))
    pair[:MAIN, :] = both[:, LANES:]
    return both[:TILE, :LANES] + pair[pl.ds(1, TILE), :]


def tap_lines(taps):
    spot = (lanes_of((8, LANES)) + RADIUS) % LANES
    return [
        jnp.where(spot < KSIZE, jnp.take_along_axis(taps, jnp.minimum(KSIZE * u + spot, LANES - 1), axis=1), 0.0)
        for u in range(KSIZE)
    ]


def put_band(lines, offset, window, first, count, refs):
    slot, half = offset // 2, offset % 2
    place = (slice(slot * count, (slot + 1) * count), slice(half * LANES, (half + 1) * LANES))
    if offset >= KSIZE:
        for ref in refs:
            ref[place] = jnp.zeros((count, LANES), jnp.bfloat16)
        return
    before, after, bound = REGIONS[window]
    row = first + lax.broadcasted_iota(jnp.int32, (count, LANES), 0)
    left, right = [jnp.broadcast_to(lines[offset][tile : tile + 1], (count, LANES)) for tile in (before, after)]
    base = left if first + count <= bound else right if first >= bound else jnp.where(row < bound, left, right)
    refs[0][place], refs[1][place] = split(pltpu.roll(base, first, 1, stride=1, stride_axis=0))


def inside(window):
    lane = lanes_of((1, LANES))
    if window == 0:
        return (lane >= HALO) | (lax.axis_index("azi") > 0)
    if window == 2:
        return (lane < LANES - HALO) | (lax.axis_index("azi") < lax.axis_size("azi") - 1)
    return lane >= 0


def early_rows(rows, windows, blocks, outs, fields, pairs, between=lambda stage: None):
    own = slice(HALO, HALO + TILE)
    each = range(len(windows))
    keep = [inside(window) for window in windows]
    for i in each:
        for stage in range(4):
            fields[i, stage, :HALO] = jnp.zeros((HALO, LANES), jnp.float32)
            fields[i, stage, HALO + TILE :] = jnp.zeros((HALO, LANES), jnp.float32)
        fields[i, 0, own] = rows[i]
    for i in each:
        main = adjoint_rows(fields.at[i, 0], blocks[i], pairs.at[i, 0], -8, MAIN, 0)
        main = jnp.where(keep[i], main, 0.0)
        outs[i][0][...] = main
        fields[i, 1, HALO - 8 : HALO + TILE + 8] = main
    between(0)
    for i in each:
        image = forward_rows(fields.at[i, 1], blocks[i], pairs.at[i, 1])
        outs[i][1][...] = image
        fields[i, 2, own] = image
    between(1)
    for i in each:
        grad = adjoint_rows(fields.at[i, 2], blocks[i], pairs.at[i, 2], 0, TILE, 16)
        grad = jnp.where(keep[i], grad, 0.0)
        outs[i][2][...] = grad
        fields[i, 3, own] = grad
    between(2)
    for i in each:
        outs[i][3][...] = forward_rows(fields.at[i, 3], blocks[i], pairs.at[i, 3])
    between(3)


PATCH = 32
REST = LANES - PATCH


def middle_kernel(block_ref, taps_ref, *refs):
    outs, sides = refs[:4], (refs[4:6], refs[6:8])
    high, low, fields, pairs = refs[8:]
    lines = tap_lines(taps_ref[...])
    for offset in range(2 * SLOTS):
        put_band(lines, offset, 1, 0, LANES, (high, low))

    def between(stage):
        for offset in range(3 * stage, 3 * stage + 3):
            put_band(lines, offset, 0, PATCH, REST, sides[0])
            put_band(lines, offset, 2, 0, REST, sides[1])

    def block(part, slot):
        return (high, low)[part][slot * LANES : (slot + 1) * LANES, :]

    rows = middle_window(block_ref[:, :LANES], block_ref[:, LANES:])
    early_rows([rows], (1,), [block], [outs], fields, pairs, between)


def sides_kernel(wide_ref, taps_ref, *refs):
    rest, middle = (refs[:2], refs[2:4]), refs[4:8]
    outs, refs = (refs[8:12], refs[12:16]), refs[16:]
    plain_ref, turned_ref, inner_ref, patches, fields, pairs = refs
    taps = taps_ref[...]
    lines = tap_lines(taps)
    for offset in range(2 * SLOTS):
        put_band(lines, offset, 0, 0, PATCH, (patches.at[0, 0], patches.at[0, 1]))
        put_band(lines, offset, 2, REST, PATCH, (patches.at[1, 0], patches.at[1, 1]))

    def piece(side, part, slot):
        whole = rest[side][part][slot * REST : (slot + 1) * REST, :]
        patch = patches[side, part, slot * PATCH : (slot + 1) * PATCH, :]
        return jnp.concatenate([patch, whole] if side == 0 else [whole, patch], axis=0)

    blocks = [lambda part, slot: piece(0, part, slot), lambda part, slot: piece(1, part, slot)]

    def between(stage):
        if stage == 0:
            plain_ref[...] = jnp.concatenate(row_weights(taps, range(4), False), axis=0)
        if stage == 1:
            turned_ref[...] = jnp.concatenate(row_weights(taps, range(4), True), axis=0)

    rows = [wide_ref[:, :LANES], wide_ref[:, 2 * LANES :]]
    early_rows(rows, (0, 2), blocks, outs, fields, pairs, between)
    early = (outs[0], middle, outs[1])
    inner = [[window[0][8 + INNER.start : 8 + INNER.stop] for window in early]]
    inner += [[window[i][INNER] for window in early] for i in range(1, 4)]
    inner_ref[...] = jnp.broadcast_to(record_of(inner, 0), (8, LANES))


GROUP = 32
GROUPS = 3 * LANES // GROUP
EDGE = 4 * RADIUS
COUNT = 24


def row_weights(taps, tiles, turned):
    lane = lanes_of((8, LANES))
    pieces = [[] for _ in tiles]
    for part in range(3):
        u = lane % GROUP
        if turned:
            u = KSIZE - 1 - u
        v = part * (LANES // GROUP) + lane // GROUP
        base = jnp.take_along_axis(taps, jnp.clip(u * KSIZE + v, 0, LANES - 1), axis=1)
        base = jnp.where((u >= 0) & (u < KSIZE) & (v < KSIZE), base, 0.0)
        for piece, tile in zip(pieces, tiles):
            row = jnp.broadcast_to(base[tile : tile + 1], (COUNT, LANES))
            piece.append(pltpu.roll(row, 0, 1, stride=1, stride_axis=0))
    return [jnp.concatenate(piece, axis=1) for piece in pieces]


def spread(rows, sign):
    moved = [rows if v == RADIUS else pltpu.roll(rows, (sign * (v - RADIUS)) % LANES, 1) for v in range(KSIZE)]
    moved.append(jnp.zeros((GROUP * (GROUPS - KSIZE), LANES), rows.dtype))
    return jnp.concatenate(moved, axis=0)


def forward_edge(rows, weights):
    lane = lanes_of((COUNT, LANES))
    parts = [split(value) for value in rows]
    high, low = [jnp.concatenate([spread(part[i], -1) for part in parts], axis=1) for i in range(2)]
    result = product(split(weights), high, low, ((1,), (0,)))
    out = []
    for window, (before, after, bound) in enumerate(REGIONS):
        cols = slice(window * LANES, (window + 1) * LANES)
        left, right = [result[COUNT * tile : COUNT * tile + COUNT, cols] for tile in (before, after)]
        out.append(jnp.where(lane < bound, left, right))
    return out


def adjoint_edge(rows, window, weights):
    before, after, bound = REGIONS[window]
    lane = lanes_of((GROUP, LANES))
    high, low = [
        jnp.concatenate(
            [
                spread(jnp.where(lane < bound, part, jnp.zeros_like(part)), 1),
                spread(jnp.where(lane < bound, jnp.zeros_like(part), part), 1),
            ],
            axis=0,
        )
        for part in split(rows)
    ]
    both = [weights[COUNT * tile : COUNT * tile + COUNT] for tile in (before, after)]
    return product(split(jnp.concatenate(both, axis=1)), high, low, ((1,), (0,)))


def edge_rows(side, message, plain_ref, turned_ref, early, outs, edge, fields):
    wide = WINDOWS * LANES
    each = range(WINDOWS)
    base = 16 if side == 0 else -80
    near = slice(16, 64) if side == 0 else slice(0, 48)
    own = slice(0, 48) if side == 0 else slice(80, 128)
    out = slice(16, 40) if side == 0 else slice(24, 48)
    start = (-15, -10, -5, 0) if side == 0 else (123, 118, 113, 108)
    beyond = lax.axis_index("rng") > 0 if side == 0 else lax.axis_index("rng") < lax.axis_size("rng") - 1
    keep = [inside(window) for window in each]
    row = lax.broadcasted_iota(jnp.int32, (EDGE, LANES), 0)
    half = EDGE // 2

    def cols(window):
        return pl.ds(window * LANES, LANES)

    def spot(stage, reach=0, count=EDGE):
        return pl.ds(start[stage] - reach + base, count)

    def in_image(stage, window):
        inner = row >= -start[stage] if side == 0 else row < TILE - start[stage]
        return keep[window] & (beyond | inner)

    tiles = range(4) if side == 0 else range(4, 8)
    taps = message[:8, :LANES] if side == 0 else message[HALO - 8 :, :LANES]
    turned = jnp.concatenate(row_weights(taps, tiles, True), axis=0)
    plain = jnp.concatenate(row_weights(taps, tiles, False), axis=0)

    row24 = lax.broadcasted_iota(jnp.int32, (HALO, 1), 0)
    if side == 0:
        edge[:HALO] = jnp.where(row24 < HALO - REACH, 0.0, message)
        edge[HALO:] = jnp.zeros((16, wide), jnp.float32)
        strip = slice(4, 36)
    else:
        edge[:16] = jnp.zeros((16, wide), jnp.float32)
        edge[16:] = jnp.where(row24 >= REACH, 0.0, message)
        strip = slice(6, 38)
    for window in each:
        main = early[window][0]
        field = fields.at[0, window]
        if side == 0:
            field[:8] = jnp.zeros((8, LANES), jnp.float32)
            field[8:16] = jnp.where(beyond, main[:8], 0.0)
            field[16:64] = main[8:56]
        else:
            field[:48] = main[88:136]
            field[48:56] = jnp.where(beyond, main[136:], 0.0)
            field[56:] = jnp.zeros((16, LANES), jnp.float32)
        result = adjoint_edge(edge[strip, cols(window)], window, turned)
        field[spot(0), :] += jnp.where(in_image(0, window), result[:EDGE], 0.0)
        outs[0][:, cols(window)] = field[out]

    yield
    out_row = lax.broadcasted_iota(jnp.int32, (4 * COUNT, wide), 0) % COUNT
    mixed = (plain, plain_ref[...]) if side == 0 else (plain_ref[...], plain)
    results = forward_edge(
        [fields[0, window, spot(1, RADIUS, GROUP), :] for window in each], jnp.where(out_row < half, *mixed)
    )
    for window in each:
        field = fields.at[1, window]
        if side == 0:
            field[:16] = jnp.zeros((16, LANES), jnp.float32)
        else:
            field[48:] = jnp.zeros((24, LANES), jnp.float32)
        field[near] = early[window][1][own]
        field[spot(1), :] = results[window][:EDGE]
        outs[1][:, cols(window)] = field[out]

    yield
    in_row = lanes_of((4 * COUNT, wide)) % GROUP
    if side == 0:
        mixed = jnp.where(in_row < half, turned, turned_ref[...])
    else:
        mixed = jnp.where(in_row < EDGE, turned_ref[...], turned)
    for window in each:
        result = adjoint_edge(fields[1, window, spot(2, RADIUS, GROUP), :], window, mixed)
        field = fields.at[2, window]
        if side == 0:
            field[8:16] = jnp.zeros((8, LANES), jnp.float32)
        else:
            field[48:56] = jnp.zeros((8, LANES), jnp.float32)
        field[near] = early[window][2][own]
        field[spot(2), :] = jnp.where(in_image(2, window), result[:EDGE], 0.0)
        outs[2][:, cols(window)] = field[out]

    yield
    results = forward_edge([fields[2, window, spot(3, RADIUS, GROUP), :] for window in each], plain_ref[...])
    for window in each:
        rest = COUNT - EDGE
        if side == 0:
            outs[3][EDGE:, cols(window)] = early[window][3][EDGE:COUNT]
            outs[3][:EDGE, cols(window)] = results[window][:EDGE]
        else:
            outs[3][:rest, cols(window)] = early[window][3][TILE - COUNT : TILE - EDGE]
            outs[3][rest:, cols(window)] = results[window][:EDGE]
    yield


INNER = slice(COUNT, TILE - COUNT)


def record_of(values, position):
    lane = lanes_of((1, LANES))
    bounds = ((24, 108), (20, 108), (20, 104))

    def total(pieces):
        sums = [
            jnp.where((lane >= low) & (lane < high), jnp.sum(piece, axis=0, keepdims=True), 0.0)
            for piece, (low, high) in zip(pieces, bounds)
        ]
        return jnp.sum(sums[0] + sums[1] + sums[2], axis=1, keepdims=True)

    def best(first, second):
        size = total([b * b for b in second])
        cross = total([a * b for a, b in zip(first, second)])
        ratio = jnp.where(size > 0.0, cross / jnp.where(size > 0.0, size, 1.0), 0.0)
        rest = total([(a - ratio * b) ** 2 for a, b in zip(first, second)])
        return total([a * a for a in first]), size, ratio, rest

    grad, image, grad2, image2 = values
    line = jnp.zeros((1, LANES), jnp.float32)
    for index, value in enumerate(best(grad, grad2) + best(image, image2)):
        line = jnp.where(lane == position + index, value, line)
    return line


def edge_kernel(*refs):
    early = [refs[4 * window : 4 * window + 4] for window in (1, 0, 2)]
    two_ref, one_ref, plain_ref, turned_ref, inner_ref = refs[12:17]
    tops, lows, record_ref, edge, fields = refs[17:21], refs[21:25], *refs[25:]
    odd = is_odd("rng")
    one, two = one_ref[...], two_ref[...]
    has_above = lax.axis_index("rng") > 0
    has_below = lax.axis_index("rng") < lax.axis_size("rng") - 1
    above = jnp.where(has_above, jnp.where(odd, one, two), 0.0)
    below = jnp.where(has_below, jnp.where(odd, two, one), 0.0)
    top = edge_rows(0, above, plain_ref, turned_ref, early, tops, edge.at[0], fields.at[0])
    low = edge_rows(1, below, plain_ref, turned_ref, early, lows, edge.at[1], fields.at[1])
    for _ in zip(top, low):
        pass

    def windows(i):
        both = jnp.concatenate([tops[i][...], lows[i][...]], axis=0)
        return [both[:, w * LANES : (w + 1) * LANES] for w in range(WINDOWS)]

    line = inner_ref[:1] + record_of([windows(i) for i in range(4)], 8)
    record_ref[...] = jnp.broadcast_to(line[None], record_ref.shape)


def combine_kernel(records_ref, block_ref, *refs):
    early = [refs[4 * window : 4 * window + 4] for window in (1, 0, 2)]
    tops, lows, (estimate_ref, residual_ref) = refs[12:16], refs[16:20], refs[20:]
    records = records_ref[:, 0, :]
    lane = lanes_of((1, LANES))

    def total(value, place):
        wanted = (lane % 8 == place) & (lane < 24)
        return jnp.sum(jnp.where(wanted, jnp.sum(value, axis=0, keepdims=True), 0.0), axis=1, keepdims=True)

    gamma = total(records, 0)
    delta = total(records, 4)
    alpha = gamma / delta
    apart = records + (alpha - pltpu.roll(records, 1, 1)) ** 2 * pltpu.roll(records, 2, 1)
    gamma_new = total(apart, 3)
    bent = total(apart, 7)
    factor = gamma_new / gamma
    delta_new = bent - factor * factor * delta
    alpha_new = gamma_new / delta_new
    first = alpha + alpha_new * (1.0 + factor)
    second = -alpha_new * alpha

    def own(a, b):
        parts = [first * a[w] + second * b[w] for w in range(WINDOWS)]
        lanes = lanes_of(parts[0].shape)
        middle = pltpu.roll(parts[1], 64, 1)
        left = jnp.where(lanes < 84, pltpu.roll(parts[0], LANES - HALO, 1), middle)
        right = jnp.where(lanes < 44, middle, pltpu.roll(parts[2], HALO, 1))
        return left, right

    def windows(ref):
        return [ref[:, w * LANES : (w + 1) * LANES] for w in range(WINDOWS)]

    for rows, pieces in (
        (slice(0, COUNT), lambda i: windows(tops[i])),
        (INNER, lambda i: [early[w][i][slice(8 + COUNT, 8 + TILE - COUNT) if i == 0 else INNER] for w in range(WINDOWS)]),
        (slice(TILE - COUNT, TILE), lambda i: windows(lows[i])),
    ):
        left, right = own(pieces(0), pieces(2))
        estimate_ref[rows, :LANES] = left
        estimate_ref[rows, LANES:] = right
        left, right = own(pieces(1), pieces(3))
        residual_ref[rows, :LANES] = block_ref[rows, :LANES] - left
        residual_ref[rows, LANES:] = block_ref[rows, LANES:] - right


def partners(axis, other):
    count, across = lax.axis_size(axis), lax.axis_size(other)

    def number(i, j):
        return i * across + j if axis == "rng" else j * count + i

    near, far = [], []
    for i in range(count):
        for j in range(across):
            near.append((number(i, j), number(i ^ 1, j)))
            beside = i + 1 if i % 2 else i - 1
            far.append((number(i, j), number(beside, j) if 0 <= beside < count else number(i, j ^ 1)))
    return near, far


BOTH = ("rng", "azi")


def body(observed, psf_tiles):
    devices = lax.axis_size("rng") * lax.axis_size("azi")
    wide = WINDOWS * LANES
    block, own, far, near = call(
        load_kernel,
        [f32(TILE, 2 * LANES), f32(8, LANES), f32(40, LANES), f32(40, LANES)],
        [pltpu.VMEM((1, 2, TAPS), jnp.float32), pltpu.SemaphoreType.DMA((3,))],
        inputs=[pl.BlockSpec(memory_space=pltpu.HBM)] * 2,
    )(
        pltpu.with_memory_space_constraint(observed, pltpu.HBM),
        pltpu.with_memory_space_constraint(psf_tiles, pltpu.HBM),
    )
    near_pairs, far_pairs = partners("azi", "rng")
    far = lax.ppermute(far, BOTH, far_pairs)
    near = lax.ppermute(near, BOTH, near_pairs)
    early = [f32(MAIN, LANES)] + [f32(TILE, LANES)] * 3
    rest = [jax.ShapeDtypeStruct((SLOTS * REST, 2 * LANES), jnp.bfloat16)] * 4

    def scratch(windows):
        return [
            pltpu.VMEM((windows, 4, ROWS, LANES), jnp.float32),
            pltpu.VMEM((windows, 4, MAIN + 8, LANES), jnp.float32),
        ]

    *middle, high0, low0, high2, low2 = call(
        middle_kernel, early + rest, [pltpu.VMEM((DEPTH, 2 * LANES), jnp.bfloat16)] * 2 + scratch(1), limit=8
    )(block, own)
    wide_block, taps, two, one = call(
        rows_kernel,
        [f32(TILE, wide), f32(8, LANES), f32(HALO, wide), f32(HALO, wide)],
        [pltpu.VMEM((HALO, wide), jnp.float32)] * 2,
    )(block, own, far, near, middle[0])
    one_pairs, two_pairs = partners("rng", "azi")
    two = lax.ppermute(two, BOTH, two_pairs)
    one = lax.ppermute(one, BOTH, one_pairs)
    *sides, plain, turned, inner = call(
        sides_kernel,
        early * 2 + [f32(4 * COUNT, wide)] * 2 + [f32(8, LANES)],
        [pltpu.VMEM((2, 2, SLOTS * PATCH, 2 * LANES), jnp.bfloat16)] + scratch(2),
        limit=8,
    )(wide_block, taps, high0, low0, high2, low2, *middle)
    *edges, record = call(
        edge_kernel,
        [f32(COUNT, wide)] * 8 + [f32(devices, 1, LANES)],
        [pltpu.VMEM((2, 40, wide), jnp.float32), pltpu.VMEM((2, 3, WINDOWS, 72, LANES), jnp.float32)],
        limit=8,
    )(*middle, *sides, two, one, plain, turned, inner)
    records = lax.all_to_all(record, BOTH, 0, 0, tiled=True)
    estimate, residual = call(combine_kernel, [f32(TILE, 2 * LANES)] * 2)(
        records, block, *middle, *sides, *edges
    )
    return estimate, residual


def solution(mesh):
    return jax.shard_map(
        body,
        mesh=mesh,
        in_specs=(P("rng", "azi"), P("rng", "azi", None)),
        out_specs=(P("rng", "azi"), P("rng", "azi")),
        check_vma=False,
    )
```

```python
import jax
import jax.numpy as jnp
from jax import lax
from jax.experimental import pallas as pl
from jax.experimental.pallas import tpu as pltpu
from jax.sharding import PartitionSpec as P

TILE = 128
KSIZE = 11
RADIUS = 5
TAPS = KSIZE * KSIZE
LANES = 128
HALO = 24
REACH = 20
WINDOWS = 3
ROWS = TILE + 2 * HALO
SLOTS = (KSIZE + 1) // 2
DEPTH = SLOTS * LANES
MAIN = 144
REGIONS = ((0, 1, 24), (1, 2, 64), (2, 3, 104))
VMEM = pl.BlockSpec(memory_space=pltpu.VMEM)


def call(kernel, out_shape, scratch=(), limit=4, inputs=None):
    given = {} if inputs is None else {"in_specs": inputs}
    return pl.pallas_call(
        kernel,
        out_shape=out_shape,
        out_specs=[VMEM] * len(out_shape),
        **given,
        scratch_shapes=list(scratch),
        compiler_params=pltpu.CompilerParams(vmem_limit_bytes=limit * 2**20),
    )


def f32(*shape):
    return jax.ShapeDtypeStruct(shape, jnp.float32)


def lanes_of(shape):
    return lax.broadcasted_iota(jnp.int32, shape, len(shape) - 1)


def is_odd(axis):
    return lax.axis_index(axis) % 2 == 1


CHUNKS = 4


def load_kernel(observed_ref, psf_ref, block_ref, taps_ref, far_ref, near_ref, psf, sems):
    part = TILE // CHUNKS
    loads = [
        pltpu.make_async_copy(observed_ref.at[pl.ds(part * i, part)], block_ref.at[pl.ds(part * i, part)], sems.at[i])
        for i in range(CHUNKS)
    ]
    loads.append(pltpu.make_async_copy(psf_ref, psf, sems.at[CHUNKS]))
    for load in loads:
        load.start()
    taps_ref[...] = jnp.zeros((8, LANES), jnp.float32)
    for load in loads:
        load.wait()
    taps_ref[1:2, :TAPS] = psf[0, 0:1, :]
    taps_ref[2:3, :TAPS] = psf[0, 1:2, :]
    columns_kernel(block_ref, taps_ref, far_ref, near_ref)


def columns_kernel(block_ref, taps_ref, far_ref, near_ref):
    lane = lanes_of((32, LANES))

    def packed(side, first):
        out = jnp.zeros((32, LANES), jnp.float32)
        for part in range(4):
            rows = block_ref[32 * part : 32 * part + 32, LANES * side : LANES * side + LANES]
            moved = pltpu.roll(rows, (32 * part - first) % LANES, 1)
            out = jnp.where((lane >= 32 * part) & (lane < 32 * part + HALO), moved, out)
        return out

    left, right = packed(0, 0), packed(1, LANES - HALO)
    odd = is_odd("azi")
    near_ref[:32] = jnp.where(odd, left, right)
    far_ref[:32] = jnp.where(odd, right, left)
    first, second = taps_ref[...], pltpu.roll(taps_ref[...], 7, 0)
    near_ref[32:] = jnp.where(odd, first, second)
    far_ref[32:] = jnp.where(odd, second, first)


def rows_kernel(block_ref, own_ref, far_ref, near_ref, _, wide_ref, taps_ref, two_ref, one_ref, top, low):
    odd = is_odd("azi")
    lane = lanes_of((32, LANES))
    near, far = near_ref[:32], far_ref[:32]
    has_left = lax.axis_index("azi") > 0
    has_right = lax.axis_index("azi") < lax.axis_size("azi") - 1
    left = jnp.where(has_left, jnp.where(odd, near, far), 0.0)
    right = jnp.where(has_right, jnp.where(odd, far, near), 0.0)
    for part in range(4):
        rows = slice(32 * part, 32 * part + 32)
        first = block_ref[rows, :LANES]
        second = block_ref[rows, LANES:]
        halo_left = pltpu.roll(left, (-32 * part) % LANES, 1)
        halo_right = pltpu.roll(right, (LANES - HALO - 32 * part) % LANES, 1)
        wide_ref[rows, :LANES] = jnp.where(lane < HALO, halo_left, pltpu.roll(first, HALO, 1))
        wide_ref[rows, LANES : 2 * LANES] = middle_window(first, second)
        wide_ref[rows, 2 * LANES :] = jnp.where(
            lane < LANES - HALO, pltpu.roll(second, LANES - HALO, 1), halo_right
        )
    near_taps, far_taps = near_ref[33:34], far_ref[33:34]
    taps_ref[...] = own_ref[...]
    taps_ref[0:1] = jnp.where(has_left, jnp.where(odd, near_taps, far_taps), 0.0)
    taps_ref[3:4] = jnp.where(has_right, jnp.where(odd, far_taps, near_taps), 0.0)
    top[...] = wide_ref[:HALO]
    low[...] = wide_ref[TILE - HALO :]
    top[REACH:, :LANES] = taps_ref[0:4]
    low[: HALO - REACH, :LANES] = taps_ref[0:4]
    odd_row = is_odd("rng")
    one_ref[...] = jnp.where(odd_row, top[...], low[...])
    two_ref[...] = jnp.where(odd_row, low[...], top[...])


def middle_window(first, second):
    lane = lanes_of(first.shape)
    return jnp.where(lane < 64, pltpu.roll(first, 64, 1), pltpu.roll(second, 64, 1))


def split(value):
    high = value.astype(jnp.bfloat16)
    return high, (value - high.astype(jnp.float32)).astype(jnp.bfloat16)


def product(parts, high, low, dims):
    rows = parts[0].shape[0]

    def dot(a, b):
        return lax.dot_general(a, b, (dims, ((), ())), preferred_element_type=jnp.float32)

    both = dot(jnp.concatenate(parts, axis=0), high)
    return both[:rows] + both[rows:] + dot(parts[0], low)


def stacked_rows(field_ref, first, count, offsets):
    pieces = [split(field_ref[pl.ds(HALO + first + offset, count), :]) for offset in offsets]
    return [jnp.concatenate([piece[part] for piece in pieces], axis=1) for part in range(2)]


def adjoint_rows(field_ref, block, pair, first, count, lead):
    offsets = [RADIUS - 2 * slot for slot in range(SLOTS)]
    parts = stacked_rows(field_ref, first - lead, count + lead, offsets)
    high, low = [jnp.concatenate([block(part, slot) for slot in range(SLOTS)], axis=0) for part in range(2)]
    both = product(parts, high, low, ((1,), (0,)))
    if lead == 0:
        pair[:8, :] = jnp.zeros((8, LANES), jnp.float32)
    pair[pl.ds(8 if lead == 0 else 0, count + lead), :] = both[:, LANES:]
    return both[lead:, :LANES] + pair[pl.ds(7 if lead == 0 else lead - 1, count), :]


def forward_rows(field_ref, block, pair):
    offsets = [2 * slot - RADIUS for slot in range(SLOTS)]
    parts = stacked_rows(field_ref, 0, MAIN, offsets)

    def turned(part):
        blocks = [block(part, slot) for slot in range(SLOTS)]
        halves = [
            jnp.concatenate([value[:, half * LANES : (half + 1) * LANES] for value in blocks], axis=1)
            for half in range(2)
        ]
        return jnp.concatenate(halves, axis=0)

    both = product(parts, turned(0), turned(1), ((1,), (1,)))
    pair[:MAIN, :] = both[:, LANES:]
    return both[:TILE, :LANES] + pair[pl.ds(1, TILE), :]


def tap_lines(taps):
    spot = (lanes_of((8, LANES)) + RADIUS) % LANES
    return [
        jnp.where(spot < KSIZE, jnp.take_along_axis(taps, jnp.minimum(KSIZE * u + spot, LANES - 1), axis=1), 0.0)
        for u in range(KSIZE)
    ]


def put_band(lines, offset, window, first, count, refs):
    slot, half = offset // 2, offset % 2
    place = (slice(slot * count, (slot + 1) * count), slice(half * LANES, (half + 1) * LANES))
    if offset >= KSIZE:
        for ref in refs:
            ref[place] = jnp.zeros((count, LANES), jnp.bfloat16)
        return
    before, after, bound = REGIONS[window]
    row = first + lax.broadcasted_iota(jnp.int32, (count, LANES), 0)
    left, right = [jnp.broadcast_to(lines[offset][tile : tile + 1], (count, LANES)) for tile in (before, after)]
    base = left if first + count <= bound else right if first >= bound else jnp.where(row < bound, left, right)
    refs[0][place], refs[1][place] = split(pltpu.roll(base, first, 1, stride=1, stride_axis=0))


def inside(window):
    lane = lanes_of((1, LANES))
    if window == 0:
        return (lane >= HALO) | (lax.axis_index("azi") > 0)
    if window == 2:
        return (lane < LANES - HALO) | (lax.axis_index("azi") < lax.axis_size("azi") - 1)
    return lane >= 0


def early_rows(rows, windows, blocks, outs, fields, pairs, between=lambda stage: None):
    own = slice(HALO, HALO + TILE)
    each = range(len(windows))
    keep = [inside(window) for window in windows]
    for i in each:
        for stage in range(4):
            fields[i, stage, :HALO] = jnp.zeros((HALO, LANES), jnp.float32)
            fields[i, stage, HALO + TILE :] = jnp.zeros((HALO, LANES), jnp.float32)
        fields[i, 0, own] = rows[i]
    for i in each:
        main = adjoint_rows(fields.at[i, 0], blocks[i], pairs.at[i, 0], -8, MAIN, 0)
        main = jnp.where(keep[i], main, 0.0)
        outs[i][0][...] = main
        fields[i, 1, HALO - 8 : HALO + TILE + 8] = main
    between(0)
    for i in each:
        image = forward_rows(fields.at[i, 1], blocks[i], pairs.at[i, 1])
        outs[i][1][...] = image
        fields[i, 2, own] = image
    between(1)
    for i in each:
        grad = adjoint_rows(fields.at[i, 2], blocks[i], pairs.at[i, 2], 0, TILE, 16)
        grad = jnp.where(keep[i], grad, 0.0)
        outs[i][2][...] = grad
        fields[i, 3, own] = grad
    between(2)
    for i in each:
        outs[i][3][...] = forward_rows(fields.at[i, 3], blocks[i], pairs.at[i, 3])
    between(3)


PATCH = 32
REST = LANES - PATCH


def middle_kernel(block_ref, taps_ref, *refs):
    outs, sides = refs[:4], (refs[4:6], refs[6:8])
    high, low, fields, pairs = refs[8:]
    lines = tap_lines(taps_ref[...])
    for offset in range(2 * SLOTS):
        put_band(lines, offset, 1, 0, LANES, (high, low))

    def between(stage):
        for offset in range(3 * stage, 3 * stage + 3):
            put_band(lines, offset, 0, PATCH, REST, sides[0])
            put_band(lines, offset, 2, 0, REST, sides[1])

    def block(part, slot):
        return (high, low)[part][slot * LANES : (slot + 1) * LANES, :]

    rows = middle_window(block_ref[:, :LANES], block_ref[:, LANES:])
    early_rows([rows], (1,), [block], [outs], fields, pairs, between)


def sides_kernel(wide_ref, taps_ref, *refs):
    rest, middle = (refs[:2], refs[2:4]), refs[4:8]
    outs, refs = (refs[8:12], refs[12:16]), refs[16:]
    plain_ref, turned_ref, inner_ref, patches, fields, pairs = refs
    taps = taps_ref[...]
    lines = tap_lines(taps)
    for offset in range(2 * SLOTS):
        put_band(lines, offset, 0, 0, PATCH, (patches.at[0, 0], patches.at[0, 1]))
        put_band(lines, offset, 2, REST, PATCH, (patches.at[1, 0], patches.at[1, 1]))

    def piece(side, part, slot):
        whole = rest[side][part][slot * REST : (slot + 1) * REST, :]
        patch = patches[side, part, slot * PATCH : (slot + 1) * PATCH, :]
        return jnp.concatenate([patch, whole] if side == 0 else [whole, patch], axis=0)

    blocks = [lambda part, slot: piece(0, part, slot), lambda part, slot: piece(1, part, slot)]

    def between(stage):
        if stage == 0:
            plain_ref[...] = jnp.concatenate(row_weights(taps, range(4), False), axis=0)
        if stage == 1:
            turned_ref[...] = jnp.concatenate(row_weights(taps, range(4), True), axis=0)

    rows = [wide_ref[:, :LANES], wide_ref[:, 2 * LANES :]]
    early_rows(rows, (0, 2), blocks, outs, fields, pairs, between)
    early = (outs[0], middle, outs[1])
    inner = [[window[0][8 + INNER.start : 8 + INNER.stop] for window in early]]
    inner += [[window[i][INNER] for window in early] for i in range(1, 4)]
    inner_ref[...] = jnp.broadcast_to(record_of(inner, 0), (8, LANES))


GROUP = 32
GROUPS = 3 * LANES // GROUP
EDGE = 4 * RADIUS
COUNT = 24


def row_weights(taps, tiles, turned):
    lane = lanes_of((8, LANES))
    pieces = [[] for _ in tiles]
    for part in range(3):
        u = lane % GROUP
        if turned:
            u = KSIZE - 1 - u
        v = part * (LANES // GROUP) + lane // GROUP
        base = jnp.take_along_axis(taps, jnp.clip(u * KSIZE + v, 0, LANES - 1), axis=1)
        base = jnp.where((u >= 0) & (u < KSIZE) & (v < KSIZE), base, 0.0)
        for piece, tile in zip(pieces, tiles):
            row = jnp.broadcast_to(base[tile : tile + 1], (COUNT, LANES))
            piece.append(pltpu.roll(row, 0, 1, stride=1, stride_axis=0))
    return [jnp.concatenate(piece, axis=1) for piece in pieces]


def spread(rows, sign):
    moved = [rows if v == RADIUS else pltpu.roll(rows, (sign * (v - RADIUS)) % LANES, 1) for v in range(KSIZE)]
    moved.append(jnp.zeros((GROUP * (GROUPS - KSIZE), LANES), rows.dtype))
    return jnp.concatenate(moved, axis=0)


def forward_edge(rows, weights):
    lane = lanes_of((COUNT, LANES))
    parts = [split(value) for value in rows]
    high, low = [jnp.concatenate([spread(part[i], -1) for part in parts], axis=1) for i in range(2)]
    result = product(split(weights), high, low, ((1,), (0,)))
    out = []
    for window, (before, after, bound) in enumerate(REGIONS):
        cols = slice(window * LANES, (window + 1) * LANES)
        left, right = [result[COUNT * tile : COUNT * tile + COUNT, cols] for tile in (before, after)]
        out.append(jnp.where(lane < bound, left, right))
    return out


def adjoint_edge(rows, window, weights):
    before, after, bound = REGIONS[window]
    lane = lanes_of((GROUP, LANES))
    whole = [spread(part, 1) for part in split(rows)]
    high, low = [
        jnp.concatenate(
            [part]
            + [
                jnp.where(lane < bound + v - RADIUS, moved, jnp.zeros_like(moved))
                for v, moved in enumerate(part[GROUP * v : GROUP * v + GROUP] for v in range(KSIZE))
            ]
            + [part[GROUP * KSIZE :]],
            axis=0,
        )
        for part in whole
    ]
    left, right = [weights[COUNT * tile : COUNT * tile + COUNT] for tile in (before, after)]
    return product(split(jnp.concatenate([right, left - right], axis=1)), high, low, ((1,), (0,)))


def edge_rows(side, message, plain, turned, plain_ref, turned_ref, early, outs, edge, fields):
    wide = WINDOWS * LANES
    each = range(WINDOWS)
    base = 16 if side == 0 else -80
    near = slice(16, 64) if side == 0 else slice(0, 48)
    own = slice(0, 48) if side == 0 else slice(80, 128)
    out = slice(16, 40) if side == 0 else slice(24, 48)
    start = (-15, -10, -5, 0) if side == 0 else (123, 118, 113, 108)
    beyond = lax.axis_index("rng") > 0 if side == 0 else lax.axis_index("rng") < lax.axis_size("rng") - 1
    keep = [inside(window) for window in each]
    row = lax.broadcasted_iota(jnp.int32, (EDGE, LANES), 0)
    half = EDGE // 2

    def cols(window):
        return pl.ds(window * LANES, LANES)

    def spot(stage, reach=0, count=EDGE):
        return pl.ds(start[stage] - reach + base, count)

    def in_image(stage, window):
        inner = row >= -start[stage] if side == 0 else row < TILE - start[stage]
        return keep[window] & (beyond | inner)

    row24 = lax.broadcasted_iota(jnp.int32, (HALO, 1), 0)
    if side == 0:
        edge[:HALO] = jnp.where(row24 < HALO - REACH, 0.0, message)
        edge[HALO:] = jnp.zeros((16, wide), jnp.float32)
        strip = slice(4, 36)
    else:
        edge[:16] = jnp.zeros((16, wide), jnp.float32)
        edge[16:] = jnp.where(row24 >= REACH, 0.0, message)
        strip = slice(6, 38)
    for window in each:
        main = early[window][0]
        field = fields.at[0, window]
        if side == 0:
            field[:8] = jnp.zeros((8, LANES), jnp.float32)
            field[8:16] = jnp.where(beyond, main[:8], 0.0)
            field[16:64] = main[8:56]
        else:
            field[:48] = main[88:136]
            field[48:56] = jnp.where(beyond, main[136:], 0.0)
            field[56:] = jnp.zeros((16, LANES), jnp.float32)
        result = adjoint_edge(edge[strip, cols(window)], window, turned)
        field[spot(0), :] += jnp.where(in_image(0, window), result[:EDGE], 0.0)
        outs[0][:, cols(window)] = field[out]

    yield
    out_row = lax.broadcasted_iota(jnp.int32, (4 * COUNT, wide), 0) % COUNT
    mixed = (plain, plain_ref[...]) if side == 0 else (plain_ref[...], plain)
    results = forward_edge(
        [fields[0, window, spot(1, RADIUS, GROUP), :] for window in each], jnp.where(out_row < half, *mixed)
    )
    for window in each:
        field = fields.at[1, window]
        if side == 0:
            field[:16] = jnp.zeros((16, LANES), jnp.float32)
        else:
            field[48:] = jnp.zeros((24, LANES), jnp.float32)
        field[near] = early[window][1][own]
        field[spot(1), :] = results[window][:EDGE]
        outs[1][:, cols(window)] = field[out]

    yield
    in_row = lanes_of((4 * COUNT, wide)) % GROUP
    if side == 0:
        mixed = jnp.where(in_row < half, turned, turned_ref[...])
    else:
        mixed = jnp.where(in_row < EDGE, turned_ref[...], turned)
    for window in each:
        result = adjoint_edge(fields[1, window, spot(2, RADIUS, GROUP), :], window, mixed)
        field = fields.at[2, window]
        if side == 0:
            field[8:16] = jnp.zeros((8, LANES), jnp.float32)
        else:
            field[48:56] = jnp.zeros((8, LANES), jnp.float32)
        field[near] = early[window][2][own]
        field[spot(2), :] = jnp.where(in_image(2, window), result[:EDGE], 0.0)
        outs[2][:, cols(window)] = field[out]

    yield
    results = forward_edge([fields[2, window, spot(3, RADIUS, GROUP), :] for window in each], plain_ref[...])
    for window in each:
        rest = COUNT - EDGE
        if side == 0:
            outs[3][EDGE:, cols(window)] = early[window][3][EDGE:COUNT]
            outs[3][:EDGE, cols(window)] = results[window][:EDGE]
        else:
            outs[3][:rest, cols(window)] = early[window][3][TILE - COUNT : TILE - EDGE]
            outs[3][rest:, cols(window)] = results[window][:EDGE]
    yield


INNER = slice(COUNT, TILE - COUNT)


def record_of(values, position):
    lane = lanes_of((1, LANES))
    bounds = ((24, 108), (20, 108), (20, 104))

    def total(pieces):
        sums = [
            jnp.where((lane >= low) & (lane < high), jnp.sum(piece, axis=0, keepdims=True), 0.0)
            for piece, (low, high) in zip(pieces, bounds)
        ]
        return jnp.sum(sums[0] + sums[1] + sums[2], axis=1, keepdims=True)

    def best(first, second):
        size = total([b * b for b in second])
        cross = total([a * b for a, b in zip(first, second)])
        ratio = jnp.where(size > 0.0, cross / jnp.where(size > 0.0, size, 1.0), 0.0)
        rest = total([(a - ratio * b) ** 2 for a, b in zip(first, second)])
        return total([a * a for a in first]), size, ratio, rest

    grad, image, grad2, image2 = values
    line = jnp.zeros((1, LANES), jnp.float32)
    for index, value in enumerate(best(grad, grad2) + best(image, image2)):
        line = jnp.where(lane == position + index, value, line)
    return line


def edge_kernel(*refs):
    early = [refs[4 * window : 4 * window + 4] for window in (1, 0, 2)]
    two_ref, one_ref, plain_ref, turned_ref, inner_ref = refs[12:17]
    tops, lows, record_ref, edge, fields = refs[17:21], refs[21:25], *refs[25:]
    odd = is_odd("rng")
    one, two = one_ref[...], two_ref[...]
    has_above = lax.axis_index("rng") > 0
    has_below = lax.axis_index("rng") < lax.axis_size("rng") - 1
    above = jnp.where(has_above, jnp.where(odd, one, two), 0.0)
    below = jnp.where(has_below, jnp.where(odd, two, one), 0.0)
    row = lax.broadcasted_iota(jnp.int32, (8, LANES), 0)
    taps = jnp.where(row < 4, above[:8, :LANES], below[HALO - 8 :, :LANES])
    turned, plain = row_weights(taps, range(8), True), row_weights(taps, range(8), False)
    (turned, turned_low), (plain, plain_low) = [
        [jnp.concatenate(weights[side : side + 4], axis=0) for side in (0, 4)] for weights in (turned, plain)
    ]
    top = edge_rows(0, above, plain, turned, plain_ref, turned_ref, early, tops, edge.at[0], fields.at[0])
    low = edge_rows(1, below, plain_low, turned_low, plain_ref, turned_ref, early, lows, edge.at[1], fields.at[1])
    for _ in zip(top, low):
        pass

    def windows(i):
        both = jnp.concatenate([tops[i][...], lows[i][...]], axis=0)
        return [both[:, w * LANES : (w + 1) * LANES] for w in range(WINDOWS)]

    line = inner_ref[:1] + record_of([windows(i) for i in range(4)], 8)
    record_ref[...] = jnp.broadcast_to(line[None], record_ref.shape)


def combine_kernel(records_ref, block_ref, *refs):
    early = [refs[4 * window : 4 * window + 4] for window in (1, 0, 2)]
    tops, lows, (estimate_ref, residual_ref) = refs[12:16], refs[16:20], refs[20:]
    records = records_ref[:, 0, :]
    lane = lanes_of((1, LANES))

    def total(value, place):
        wanted = (lane % 8 == place) & (lane < 24)
        return jnp.sum(jnp.where(wanted, jnp.sum(value, axis=0, keepdims=True), 0.0), axis=1, keepdims=True)

    gamma = total(records, 0)
    delta = total(records, 4)
    alpha = gamma / delta
    apart = records + (alpha - pltpu.roll(records, 1, 1)) ** 2 * pltpu.roll(records, 2, 1)
    gamma_new = total(apart, 3)
    bent = total(apart, 7)
    factor = gamma_new / gamma
    delta_new = bent - factor * factor * delta
    alpha_new = gamma_new / delta_new
    first = alpha + alpha_new * (1.0 + factor)
    second = -alpha_new * alpha

    def own(a, b):
        parts = [first * a[w] + second * b[w] for w in range(WINDOWS)]
        lanes = lanes_of(parts[0].shape)
        middle = pltpu.roll(parts[1], 64, 1)
        left = jnp.where(lanes < 84, pltpu.roll(parts[0], LANES - HALO, 1), middle)
        right = jnp.where(lanes < 44, middle, pltpu.roll(parts[2], HALO, 1))
        return left, right

    def windows(ref):
        return [ref[:, w * LANES : (w + 1) * LANES] for w in range(WINDOWS)]

    for rows, pieces in (
        (slice(0, COUNT), lambda i: windows(tops[i])),
        (INNER, lambda i: [early[w][i][slice(8 + COUNT, 8 + TILE - COUNT) if i == 0 else INNER] for w in range(WINDOWS)]),
        (slice(TILE - COUNT, TILE), lambda i: windows(lows[i])),
    ):
        left, right = own(pieces(0), pieces(2))
        estimate_ref[rows, :LANES] = left
        estimate_ref[rows, LANES:] = right
        left, right = own(pieces(1), pieces(3))
        residual_ref[rows, :LANES] = block_ref[rows, :LANES] - left
        residual_ref[rows, LANES:] = block_ref[rows, LANES:] - right


def partners(axis, other):
    count, across = lax.axis_size(axis), lax.axis_size(other)

    def number(i, j):
        return i * across + j if axis == "rng" else j * count + i

    near, far = [], []
    for i in range(count):
        for j in range(across):
            near.append((number(i, j), number(i ^ 1, j)))
            beside = i + 1 if i % 2 else i - 1
            far.append((number(i, j), number(beside, j) if 0 <= beside < count else number(i, j ^ 1)))
    return near, far


BOTH = ("rng", "azi")


def body(observed, psf_tiles):
    devices = lax.axis_size("rng") * lax.axis_size("azi")
    wide = WINDOWS * LANES
    block, own, far, near = call(
        load_kernel,
        [f32(TILE, 2 * LANES), f32(8, LANES), f32(40, LANES), f32(40, LANES)],
        [pltpu.VMEM((1, 2, TAPS), jnp.float32), pltpu.SemaphoreType.DMA((CHUNKS + 1,))],
        inputs=[pl.BlockSpec(memory_space=pltpu.HBM)] * 2,
    )(
        pltpu.with_memory_space_constraint(observed, pltpu.HBM),
        pltpu.with_memory_space_constraint(psf_tiles, pltpu.HBM),
    )
    near_pairs, far_pairs = partners("azi", "rng")
    far = lax.ppermute(far, BOTH, far_pairs)
    near = lax.ppermute(near, BOTH, near_pairs)
    early = [f32(MAIN, LANES)] + [f32(TILE, LANES)] * 3
    rest = [jax.ShapeDtypeStruct((SLOTS * REST, 2 * LANES), jnp.bfloat16)] * 4

    def scratch(windows):
        return [
            pltpu.VMEM((windows, 4, ROWS, LANES), jnp.float32),
            pltpu.VMEM((windows, 4, MAIN + 8, LANES), jnp.float32),
        ]

    *middle, high0, low0, high2, low2 = call(
        middle_kernel, early + rest, [pltpu.VMEM((DEPTH, 2 * LANES), jnp.bfloat16)] * 2 + scratch(1), limit=8
    )(block, own)
    wide_block, taps, two, one = call(
        rows_kernel,
        [f32(TILE, wide), f32(8, LANES), f32(HALO, wide), f32(HALO, wide)],
        [pltpu.VMEM((HALO, wide), jnp.float32)] * 2,
    )(block, own, far, near, middle[0])
    one_pairs, two_pairs = partners("rng", "azi")
    two = lax.ppermute(two, BOTH, two_pairs)
    one = lax.ppermute(one, BOTH, one_pairs)
    *sides, plain, turned, inner = call(
        sides_kernel,
        early * 2 + [f32(4 * COUNT, wide)] * 2 + [f32(8, LANES)],
        [pltpu.VMEM((2, 2, SLOTS * PATCH, 2 * LANES), jnp.bfloat16)] + scratch(2),
        limit=8,
    )(wide_block, taps, high0, low0, high2, low2, *middle)
    *edges, record = call(
        edge_kernel,
        [f32(COUNT, wide)] * 8 + [f32(devices, 1, LANES)],
        [pltpu.VMEM((2, 40, wide), jnp.float32), pltpu.VMEM((2, 3, WINDOWS, 72, LANES), jnp.float32)],
        limit=8,
    )(*middle, *sides, two, one, plain, turned, inner)
    records = lax.all_to_all(record, BOTH, 0, 0, tiled=True)
    estimate, residual = call(combine_kernel, [f32(TILE, 2 * LANES)] * 2)(
        records, block, *middle, *sides, *edges
    )
    return estimate, residual


def solution(mesh):
    return jax.shard_map(
        body,
        mesh=mesh,
        in_specs=(P("rng", "azi"), P("rng", "azi", None)),
        out_specs=(P("rng", "azi"), P("rng", "azi")),
        check_vma=False,
    )
```

```python
import jax
import jax.numpy as jnp
from jax import lax
from jax.experimental import pallas as pl
from jax.experimental.pallas import tpu as pltpu
from jax.sharding import PartitionSpec as P

TILE = 128
KSIZE = 11
RADIUS = 5
TAPS = KSIZE * KSIZE
LANES = 128
HALO = 24
REACH = 20
WINDOWS = 3
ROWS = TILE + 2 * HALO
SLOTS = (KSIZE + 1) // 2
DEPTH = SLOTS * LANES
MAIN = 144
REGIONS = ((0, 1, 24), (1, 2, 64), (2, 3, 104))
VMEM = pl.BlockSpec(memory_space=pltpu.VMEM)


def call(kernel, out_shape, scratch=(), limit=4, inputs=None):
    given = {} if inputs is None else {"in_specs": inputs}
    return pl.pallas_call(
        kernel,
        out_shape=out_shape,
        out_specs=[VMEM] * len(out_shape),
        **given,
        scratch_shapes=list(scratch),
        compiler_params=pltpu.CompilerParams(vmem_limit_bytes=limit * 2**20),
    )


def f32(*shape):
    return jax.ShapeDtypeStruct(shape, jnp.float32)


def lanes_of(shape):
    return lax.broadcasted_iota(jnp.int32, shape, len(shape) - 1)


def is_odd(axis):
    return lax.axis_index(axis) % 2 == 1


CHUNKS = 4


def load_kernel(observed_ref, psf_ref, block_ref, taps_ref, far_ref, near_ref, psf, sems):
    part = TILE // CHUNKS
    loads = [
        pltpu.make_async_copy(observed_ref.at[pl.ds(part * i, part)], block_ref.at[pl.ds(part * i, part)], sems.at[i])
        for i in range(CHUNKS)
    ]
    loads.append(pltpu.make_async_copy(psf_ref, psf, sems.at[CHUNKS]))
    for load in loads:
        load.start()
    taps_ref[...] = jnp.zeros((8, LANES), jnp.float32)
    for load in loads:
        load.wait()
    taps_ref[1:2, :TAPS] = psf[0, 0:1, :]
    taps_ref[2:3, :TAPS] = psf[0, 1:2, :]
    columns_kernel(block_ref, taps_ref, far_ref, near_ref)


def columns_kernel(block_ref, taps_ref, far_ref, near_ref):
    lane = lanes_of((32, LANES))

    def packed(side, first):
        out = jnp.zeros((32, LANES), jnp.float32)
        for part in range(4):
            rows = block_ref[32 * part : 32 * part + 32, LANES * side : LANES * side + LANES]
            moved = pltpu.roll(rows, (32 * part - first) % LANES, 1)
            out = jnp.where((lane >= 32 * part) & (lane < 32 * part + HALO), moved, out)
        return out

    left, right = packed(0, 0), packed(1, LANES - HALO)
    odd = is_odd("azi")
    near_ref[:32] = jnp.where(odd, left, right)
    far_ref[:32] = jnp.where(odd, right, left)
    first, second = taps_ref[...], pltpu.roll(taps_ref[...], 7, 0)
    near_ref[32:] = jnp.where(odd, first, second)
    far_ref[32:] = jnp.where(odd, second, first)


def rows_kernel(block_ref, own_ref, far_ref, near_ref, _, wide_ref, taps_ref, two_ref, one_ref, top, low):
    odd = is_odd("azi")
    lane = lanes_of((32, LANES))
    near, far = near_ref[:32], far_ref[:32]
    has_left = lax.axis_index("azi") > 0
    has_right = lax.axis_index("azi") < lax.axis_size("azi") - 1
    left = jnp.where(has_left, jnp.where(odd, near, far), 0.0)
    right = jnp.where(has_right, jnp.where(odd, far, near), 0.0)
    for part in range(4):
        rows = slice(32 * part, 32 * part + 32)
        first = block_ref[rows, :LANES]
        second = block_ref[rows, LANES:]
        halo_left = pltpu.roll(left, (-32 * part) % LANES, 1)
        halo_right = pltpu.roll(right, (LANES - HALO - 32 * part) % LANES, 1)
        wide_ref[rows, :LANES] = jnp.where(lane < HALO, halo_left, pltpu.roll(first, HALO, 1))
        wide_ref[rows, LANES : 2 * LANES] = middle_window(first, second)
        wide_ref[rows, 2 * LANES :] = jnp.where(
            lane < LANES - HALO, pltpu.roll(second, LANES - HALO, 1), halo_right
        )
    near_taps, far_taps = near_ref[33:34], far_ref[33:34]
    taps_ref[...] = own_ref[...]
    taps_ref[0:1] = jnp.where(has_left, jnp.where(odd, near_taps, far_taps), 0.0)
    taps_ref[3:4] = jnp.where(has_right, jnp.where(odd, far_taps, near_taps), 0.0)
    top[...] = wide_ref[:HALO]
    low[...] = wide_ref[TILE - HALO :]
    top[REACH:, :LANES] = taps_ref[0:4]
    low[: HALO - REACH, :LANES] = taps_ref[0:4]
    odd_row = is_odd("rng")
    one_ref[...] = jnp.where(odd_row, top[...], low[...])
    two_ref[...] = jnp.where(odd_row, low[...], top[...])


def middle_window(first, second):
    lane = lanes_of(first.shape)
    return jnp.where(lane < 64, pltpu.roll(first, 64, 1), pltpu.roll(second, 64, 1))


def split(value):
    high = value.astype(jnp.bfloat16)
    return high, (value - high.astype(jnp.float32)).astype(jnp.bfloat16)


def product(parts, high, low, dims):
    rows = parts[0].shape[0]

    def dot(a, b):
        return lax.dot_general(a, b, (dims, ((), ())), preferred_element_type=jnp.float32)

    both = dot(jnp.concatenate(parts, axis=0), high)
    return both[:rows] + both[rows:] + dot(parts[0], low)


def stacked_rows(field_ref, first, count, offsets):
    pieces = [split(field_ref[pl.ds(HALO + first + offset, count), :]) for offset in offsets]
    return [jnp.concatenate([piece[part] for piece in pieces], axis=1) for part in range(2)]


def adjoint_rows(field_ref, block, pair, first, count, lead):
    offsets = [RADIUS - 2 * slot for slot in range(SLOTS)]
    parts = stacked_rows(field_ref, first - lead, count + lead, offsets)
    high, low = [jnp.concatenate([block(part, slot) for slot in range(SLOTS)], axis=0) for part in range(2)]
    both = product(parts, high, low, ((1,), (0,)))
    if lead == 0:
        pair[:8, :] = jnp.zeros((8, LANES), jnp.float32)
    pair[pl.ds(8 if lead == 0 else 0, count + lead), :] = both[:, LANES:]
    return both[lead:, :LANES] + pair[pl.ds(7 if lead == 0 else lead - 1, count), :]


def forward_rows(field_ref, block, pair, first, count):
    offsets = [2 * slot - RADIUS for slot in range(SLOTS)]
    parts = stacked_rows(field_ref, first, count + 16, offsets)

    def turned(part):
        blocks = [block(part, slot) for slot in range(SLOTS)]
        halves = [
            jnp.concatenate([value[:, half * LANES : (half + 1) * LANES] for value in blocks], axis=1)
            for half in range(2)
        ]
        return jnp.concatenate(halves, axis=0)

    both = product(parts, turned(0), turned(1), ((1,), (1,)))
    pair[: count + 16, :] = both[:, LANES:]
    return both[:count, :LANES] + pair[pl.ds(1, count), :]


def tap_lines(taps):
    spot = (lanes_of((8, LANES)) + RADIUS) % LANES
    return [
        jnp.where(spot < KSIZE, jnp.take_along_axis(taps, jnp.minimum(KSIZE * u + spot, LANES - 1), axis=1), 0.0)
        for u in range(KSIZE)
    ]


def put_band(lines, offset, window, first, count, refs):
    slot, half = offset // 2, offset % 2
    place = (slice(slot * count, (slot + 1) * count), slice(half * LANES, (half + 1) * LANES))
    if offset >= KSIZE:
        for ref in refs:
            ref[place] = jnp.zeros((count, LANES), jnp.bfloat16)
        return
    before, after, bound = REGIONS[window]
    row = first + lax.broadcasted_iota(jnp.int32, (count, LANES), 0)
    left, right = [jnp.broadcast_to(lines[offset][tile : tile + 1], (count, LANES)) for tile in (before, after)]
    base = left if first + count <= bound else right if first >= bound else jnp.where(row < bound, left, right)
    refs[0][place], refs[1][place] = split(pltpu.roll(base, first, 1, stride=1, stride_axis=0))


def inside(window):
    lane = lanes_of((1, LANES))
    if window == 0:
        return (lane >= HALO) | (lax.axis_index("azi") > 0)
    if window == 2:
        return (lane < LANES - HALO) | (lax.axis_index("azi") < lax.axis_size("azi") - 1)
    return lane >= 0


def early_rows(rows, windows, blocks, outs, fields, pairs, between=lambda stage: None):
    own = slice(HALO, HALO + TILE)
    most, fewer = slice(8, TILE - 8), slice(16, TILE - 16)
    each = range(len(windows))
    keep = [inside(window) for window in windows]
    for i in each:
        for stage in range(4):
            fields[i, stage, : HALO + 8] = jnp.zeros((HALO + 8, LANES), jnp.float32)
            fields[i, stage, HALO + TILE - 8 :] = jnp.zeros((HALO + 8, LANES), jnp.float32)
        fields[i, 0, own] = rows[i]
    for i in each:
        main = adjoint_rows(fields.at[i, 0], blocks[i], pairs.at[i, 0], -8, MAIN, 0)
        main = jnp.where(keep[i], main, 0.0)
        outs[i][0][...] = main
        fields[i, 1, HALO - 8 : HALO + TILE + 8] = main
    between(0)
    for i in each:
        image = forward_rows(fields.at[i, 1], blocks[i], pairs.at[i, 1], most.start, TILE - 16)
        outs[i][1][most] = image
        fields[i, 2, HALO + most.start : HALO + most.stop] = image
    between(1)
    for i in each:
        grad = adjoint_rows(fields.at[i, 2], blocks[i], pairs.at[i, 2], most.start, TILE - 16, 16)
        grad = jnp.where(keep[i], grad, 0.0)
        outs[i][2][most] = grad
        fields[i, 3, HALO + most.start : HALO + most.stop] = grad
    between(2)
    for i in each:
        outs[i][3][fewer] = forward_rows(fields.at[i, 3], blocks[i], pairs.at[i, 3], fewer.start, TILE - 32)
    between(3)


PATCH = 32
REST = LANES - PATCH


def middle_kernel(block_ref, taps_ref, *refs):
    outs, sides = refs[:4], (refs[4:6], refs[6:8])
    high, low, fields, pairs = refs[8:]
    lines = tap_lines(taps_ref[...])
    for offset in range(2 * SLOTS):
        put_band(lines, offset, 1, 0, LANES, (high, low))

    def between(stage):
        for offset in range(3 * stage, 3 * stage + 3):
            put_band(lines, offset, 0, PATCH, REST, sides[0])
            put_band(lines, offset, 2, 0, REST, sides[1])

    def block(part, slot):
        return (high, low)[part][slot * LANES : (slot + 1) * LANES, :]

    rows = middle_window(block_ref[:, :LANES], block_ref[:, LANES:])
    early_rows([rows], (1,), [block], [outs], fields, pairs, between)


def sides_kernel(wide_ref, taps_ref, *refs):
    rest, middle = (refs[:2], refs[2:4]), refs[4:8]
    outs, refs = (refs[8:12], refs[12:16]), refs[16:]
    plain_ref, turned_ref, inner_ref, patches, fields, pairs = refs
    taps = taps_ref[...]
    lines = tap_lines(taps)
    for offset in range(2 * SLOTS):
        put_band(lines, offset, 0, 0, PATCH, (patches.at[0, 0], patches.at[0, 1]))
        put_band(lines, offset, 2, REST, PATCH, (patches.at[1, 0], patches.at[1, 1]))

    def piece(side, part, slot):
        whole = rest[side][part][slot * REST : (slot + 1) * REST, :]
        patch = patches[side, part, slot * PATCH : (slot + 1) * PATCH, :]
        return jnp.concatenate([patch, whole] if side == 0 else [whole, patch], axis=0)

    blocks = [lambda part, slot: piece(0, part, slot), lambda part, slot: piece(1, part, slot)]

    def between(stage):
        if stage == 0:
            plain_ref[...] = jnp.concatenate(row_weights(taps, range(4), False), axis=0)
        if stage == 1:
            turned_ref[...] = jnp.concatenate(row_weights(taps, range(4), True), axis=0)

    rows = [wide_ref[:, :LANES], wide_ref[:, 2 * LANES :]]
    early_rows(rows, (0, 2), blocks, outs, fields, pairs, between)
    early = (outs[0], middle, outs[1])
    inner = [[window[0][8 + INNER.start : 8 + INNER.stop] for window in early]]
    inner += [[window[i][INNER] for window in early] for i in range(1, 4)]
    inner_ref[...] = jnp.broadcast_to(record_of(inner, 0), (8, LANES))


GROUP = 32
GROUPS = 3 * LANES // GROUP
EDGE = 4 * RADIUS
COUNT = 24


def row_weights(taps, tiles, turned):
    lane = lanes_of((8, LANES))
    pieces = [[] for _ in tiles]
    for part in range(3):
        u = lane % GROUP
        if turned:
            u = KSIZE - 1 - u
        v = part * (LANES // GROUP) + lane // GROUP
        base = jnp.take_along_axis(taps, jnp.clip(u * KSIZE + v, 0, LANES - 1), axis=1)
        base = jnp.where((u >= 0) & (u < KSIZE) & (v < KSIZE), base, 0.0)
        for piece, tile in zip(pieces, tiles):
            row = jnp.broadcast_to(base[tile : tile + 1], (COUNT, LANES))
            piece.append(pltpu.roll(row, 0, 1, stride=1, stride_axis=0))
    return [jnp.concatenate(piece, axis=1) for piece in pieces]


def spread(rows, sign):
    moved = [rows if v == RADIUS else pltpu.roll(rows, (sign * (v - RADIUS)) % LANES, 1) for v in range(KSIZE)]
    moved.append(jnp.zeros((GROUP * (GROUPS - KSIZE), LANES), rows.dtype))
    return jnp.concatenate(moved, axis=0)


def forward_edge(rows, window, weights):
    before, after, bound = REGIONS[window]
    high, low = [spread(part, -1) for part in split(rows)]
    both = [weights[COUNT * tile : COUNT * tile + COUNT] for tile in (before, after)]
    result = product(split(jnp.concatenate(both, axis=0)), high, low, ((1,), (0,)))
    return jnp.where(lanes_of((COUNT, LANES)) < bound, result[:COUNT], result[COUNT:])


def adjoint_edge(rows, window, weights):
    before, after, bound = REGIONS[window]
    lane = lanes_of((GROUP, LANES))
    whole = [spread(part, 1) for part in split(rows)]
    high, low = [
        jnp.concatenate(
            [part]
            + [
                jnp.where(lane < bound + v - RADIUS, moved, jnp.zeros_like(moved))
                for v, moved in enumerate(part[GROUP * v : GROUP * v + GROUP] for v in range(KSIZE))
            ]
            + [part[GROUP * KSIZE :]],
            axis=0,
        )
        for part in whole
    ]
    left, right = [weights[COUNT * tile : COUNT * tile + COUNT] for tile in (before, after)]
    return product(split(jnp.concatenate([right, left - right], axis=1)), high, low, ((1,), (0,)))


def edge_rows(side, message, plain, turned, plain_ref, turned_ref, early, outs, edge, fields):
    wide = WINDOWS * LANES
    each = range(WINDOWS)
    base = 16 if side == 0 else -80
    near = slice(24, 64) if side == 0 else slice(0, 40)
    own = slice(8, 48) if side == 0 else slice(80, 120)
    out = slice(16, 40) if side == 0 else slice(24, 48)
    start = (-15, -10, -5, 0) if side == 0 else (123, 118, 113, 108)
    beyond = lax.axis_index("rng") > 0 if side == 0 else lax.axis_index("rng") < lax.axis_size("rng") - 1
    keep = [inside(window) for window in each]
    row = lax.broadcasted_iota(jnp.int32, (EDGE, LANES), 0)
    half = EDGE // 2

    def cols(window):
        return pl.ds(window * LANES, LANES)

    def spot(stage, reach=0, count=EDGE):
        return pl.ds(start[stage] - reach + base, count)

    def in_image(stage, window):
        inner = row >= -start[stage] if side == 0 else row < TILE - start[stage]
        return keep[window] & (beyond | inner)

    row24 = lax.broadcasted_iota(jnp.int32, (HALO, 1), 0)
    if side == 0:
        edge[:HALO] = jnp.where(row24 < HALO - REACH, 0.0, message)
        edge[HALO:] = jnp.zeros((16, wide), jnp.float32)
        strip = slice(4, 36)
    else:
        edge[:16] = jnp.zeros((16, wide), jnp.float32)
        edge[16:] = jnp.where(row24 >= REACH, 0.0, message)
        strip = slice(6, 38)
    for window in each:
        main = early[window][0]
        field = fields.at[0, window]
        if side == 0:
            field[:8] = jnp.zeros((8, LANES), jnp.float32)
            field[8:16] = jnp.where(beyond, main[:8], 0.0)
            field[16:64] = main[8:56]
        else:
            field[:48] = main[88:136]
            field[48:56] = jnp.where(beyond, main[136:], 0.0)
            field[56:] = jnp.zeros((16, LANES), jnp.float32)
        result = adjoint_edge(edge[strip, cols(window)], window, turned)
        field[spot(0), :] += jnp.where(in_image(0, window), result[:EDGE], 0.0)
        outs[0][:, cols(window)] = field[out]

    yield
    out_row = lax.broadcasted_iota(jnp.int32, (4 * COUNT, wide), 0) % COUNT
    mixed = (plain, plain_ref[...]) if side == 0 else (plain_ref[...], plain)
    mixed = jnp.where(out_row < half, *mixed)
    results = [forward_edge(fields[0, window, spot(1, RADIUS, GROUP), :], window, mixed) for window in each]
    for window in each:
        field = fields.at[1, window]
        if side == 0:
            field[:24] = jnp.zeros((24, LANES), jnp.float32)
        else:
            field[40:] = jnp.zeros((32, LANES), jnp.float32)
        field[near] = early[window][1][own]
        field[spot(1), :] = results[window][:EDGE]
        outs[1][:, cols(window)] = field[out]

    yield
    in_row = lanes_of((4 * COUNT, wide)) % GROUP
    if side == 0:
        mixed = jnp.where(in_row < half, turned, turned_ref[...])
    else:
        mixed = jnp.where(in_row < EDGE, turned_ref[...], turned)
    for window in each:
        result = adjoint_edge(fields[1, window, spot(2, RADIUS, GROUP), :], window, mixed)
        field = fields.at[2, window]
        if side == 0:
            field[8:24] = jnp.zeros((16, LANES), jnp.float32)
        else:
            field[40:56] = jnp.zeros((16, LANES), jnp.float32)
        field[near] = early[window][2][own]
        field[spot(2), :] = jnp.where(in_image(2, window), result[:EDGE], 0.0)
        outs[2][:, cols(window)] = field[out]

    yield
    results = [forward_edge(fields[2, window, spot(3, RADIUS, GROUP), :], window, plain_ref[...]) for window in each]
    for window in each:
        rest = COUNT - EDGE
        if side == 0:
            outs[3][EDGE:, cols(window)] = early[window][3][EDGE:COUNT]
            outs[3][:EDGE, cols(window)] = results[window][:EDGE]
        else:
            outs[3][:rest, cols(window)] = early[window][3][TILE - COUNT : TILE - EDGE]
            outs[3][rest:, cols(window)] = results[window][:EDGE]
    yield


INNER = slice(COUNT, TILE - COUNT)


def record_of(values, position):
    lane = lanes_of((1, LANES))
    bounds = ((24, 108), (20, 108), (20, 104))

    def total(pieces):
        sums = [
            jnp.where((lane >= low) & (lane < high), jnp.sum(piece, axis=0, keepdims=True), 0.0)
            for piece, (low, high) in zip(pieces, bounds)
        ]
        return jnp.sum(sums[0] + sums[1] + sums[2], axis=1, keepdims=True)

    def best(first, second):
        size = total([b * b for b in second])
        cross = total([a * b for a, b in zip(first, second)])
        ratio = jnp.where(size > 0.0, cross / jnp.where(size > 0.0, size, 1.0), 0.0)
        rest = total([(a - ratio * b) ** 2 for a, b in zip(first, second)])
        return total([a * a for a in first]), size, ratio, rest

    grad, image, grad2, image2 = values
    line = jnp.zeros((1, LANES), jnp.float32)
    for index, value in enumerate(best(grad, grad2) + best(image, image2)):
        line = jnp.where(lane == position + index, value, line)
    return line


def edge_kernel(*refs):
    early = [refs[4 * window : 4 * window + 4] for window in (1, 0, 2)]
    two_ref, one_ref, plain_ref, turned_ref, inner_ref = refs[12:17]
    tops, lows, record_ref, edge, fields = refs[17:21], refs[21:25], *refs[25:]
    odd = is_odd("rng")
    one, two = one_ref[...], two_ref[...]
    has_above = lax.axis_index("rng") > 0
    has_below = lax.axis_index("rng") < lax.axis_size("rng") - 1
    above = jnp.where(has_above, jnp.where(odd, one, two), 0.0)
    below = jnp.where(has_below, jnp.where(odd, two, one), 0.0)
    row = lax.broadcasted_iota(jnp.int32, (8, LANES), 0)
    taps = jnp.where(row < 4, above[:8, :LANES], below[HALO - 8 :, :LANES])
    turned, plain = row_weights(taps, range(8), True), row_weights(taps, range(8), False)
    (turned, turned_low), (plain, plain_low) = [
        [jnp.concatenate(weights[side : side + 4], axis=0) for side in (0, 4)] for weights in (turned, plain)
    ]
    top = edge_rows(0, above, plain, turned, plain_ref, turned_ref, early, tops, edge.at[0], fields.at[0])
    low = edge_rows(1, below, plain_low, turned_low, plain_ref, turned_ref, early, lows, edge.at[1], fields.at[1])
    for _ in zip(top, low):
        pass

    def windows(i):
        both = jnp.concatenate([tops[i][...], lows[i][...]], axis=0)
        return [both[:, w * LANES : (w + 1) * LANES] for w in range(WINDOWS)]

    line = inner_ref[:1] + record_of([windows(i) for i in range(4)], 8)
    record_ref[...] = jnp.broadcast_to(line[None], record_ref.shape)


def combine_kernel(records_ref, block_ref, *refs):
    early = [refs[4 * window : 4 * window + 4] for window in (1, 0, 2)]
    tops, lows, (estimate_ref, residual_ref) = refs[12:16], refs[16:20], refs[20:]
    records = records_ref[:, 0, :]
    lane = lanes_of((1, LANES))

    def total(value, place):
        wanted = (lane % 8 == place) & (lane < 24)
        return jnp.sum(jnp.where(wanted, jnp.sum(value, axis=0, keepdims=True), 0.0), axis=1, keepdims=True)

    gamma = total(records, 0)
    delta = total(records, 4)
    alpha = gamma / delta
    apart = records + (alpha - pltpu.roll(records, 1, 1)) ** 2 * pltpu.roll(records, 2, 1)
    gamma_new = total(apart, 3)
    bent = total(apart, 7)
    factor = gamma_new / gamma
    delta_new = bent - factor * factor * delta
    alpha_new = gamma_new / delta_new
    first = alpha + alpha_new * (1.0 + factor)
    second = -alpha_new * alpha

    def own(a, b):
        parts = [first * a[w] + second * b[w] for w in range(WINDOWS)]
        lanes = lanes_of(parts[0].shape)
        middle = pltpu.roll(parts[1], 64, 1)
        left = jnp.where(lanes < 84, pltpu.roll(parts[0], LANES - HALO, 1), middle)
        right = jnp.where(lanes < 44, middle, pltpu.roll(parts[2], HALO, 1))
        return left, right

    def windows(ref):
        return [ref[:, w * LANES : (w + 1) * LANES] for w in range(WINDOWS)]

    for rows, pieces in (
        (slice(0, COUNT), lambda i: windows(tops[i])),
        (INNER, lambda i: [early[w][i][slice(8 + COUNT, 8 + TILE - COUNT) if i == 0 else INNER] for w in range(WINDOWS)]),
        (slice(TILE - COUNT, TILE), lambda i: windows(lows[i])),
    ):
        left, right = own(pieces(0), pieces(2))
        estimate_ref[rows, :LANES] = left
        estimate_ref[rows, LANES:] = right
        left, right = own(pieces(1), pieces(3))
        residual_ref[rows, :LANES] = block_ref[rows, :LANES] - left
        residual_ref[rows, LANES:] = block_ref[rows, LANES:] - right


def partners(axis, other):
    count, across = lax.axis_size(axis), lax.axis_size(other)

    def number(i, j):
        return i * across + j if axis == "rng" else j * count + i

    near, far = [], []
    for i in range(count):
        for j in range(across):
            near.append((number(i, j), number(i ^ 1, j)))
            beside = i + 1 if i % 2 else i - 1
            far.append((number(i, j), number(beside, j) if 0 <= beside < count else number(i, j ^ 1)))
    return near, far


BOTH = ("rng", "azi")


def body(observed, psf_tiles):
    devices = lax.axis_size("rng") * lax.axis_size("azi")
    wide = WINDOWS * LANES
    block, own, far, near = call(
        load_kernel,
        [f32(TILE, 2 * LANES), f32(8, LANES), f32(40, LANES), f32(40, LANES)],
        [pltpu.VMEM((1, 2, TAPS), jnp.float32), pltpu.SemaphoreType.DMA((CHUNKS + 1,))],
        inputs=[pl.BlockSpec(memory_space=pltpu.HBM)] * 2,
    )(
        pltpu.with_memory_space_constraint(observed, pltpu.HBM),
        pltpu.with_memory_space_constraint(psf_tiles, pltpu.HBM),
    )
    near_pairs, far_pairs = partners("azi", "rng")
    far = lax.ppermute(far, BOTH, far_pairs)
    near = lax.ppermute(near, BOTH, near_pairs)
    early = [f32(MAIN, LANES)] + [f32(TILE, LANES)] * 3
    rest = [jax.ShapeDtypeStruct((SLOTS * REST, 2 * LANES), jnp.bfloat16)] * 4

    def scratch(windows):
        return [
            pltpu.VMEM((windows, 4, ROWS, LANES), jnp.float32),
            pltpu.VMEM((windows, 4, MAIN + 8, LANES), jnp.float32),
        ]

    *middle, high0, low0, high2, low2 = call(
        middle_kernel, early + rest, [pltpu.VMEM((DEPTH, 2 * LANES), jnp.bfloat16)] * 2 + scratch(1), limit=8
    )(block, own)
    wide_block, taps, two, one = call(
        rows_kernel,
        [f32(TILE, wide), f32(8, LANES), f32(HALO, wide), f32(HALO, wide)],
        [pltpu.VMEM((HALO, wide), jnp.float32)] * 2,
    )(block, own, far, near, middle[0])
    one_pairs, two_pairs = partners("rng", "azi")
    two = lax.ppermute(two, BOTH, two_pairs)
    one = lax.ppermute(one, BOTH, one_pairs)
    *sides, plain, turned, inner = call(
        sides_kernel,
        early * 2 + [f32(4 * COUNT, wide)] * 2 + [f32(8, LANES)],
        [pltpu.VMEM((2, 2, SLOTS * PATCH, 2 * LANES), jnp.bfloat16)] + scratch(2),
        limit=8,
    )(wide_block, taps, high0, low0, high2, low2, *middle)
    *edges, record = call(
        edge_kernel,
        [f32(COUNT, wide)] * 8 + [f32(devices, 1, LANES)],
        [pltpu.VMEM((2, 40, wide), jnp.float32), pltpu.VMEM((2, 3, WINDOWS, 72, LANES), jnp.float32)],
        limit=8,
    )(*middle, *sides, two, one, plain, turned, inner)
    records = lax.all_to_all(record, BOTH, 0, 0, tiled=True)
    estimate, residual = call(combine_kernel, [f32(TILE, 2 * LANES)] * 2)(
        records, block, *middle, *sides, *edges
    )
    return estimate, residual


def solution(mesh):
    return jax.shard_map(
        body,
        mesh=mesh,
        in_specs=(P("rng", "azi"), P("rng", "azi", None)),
        out_specs=(P("rng", "azi"), P("rng", "azi")),
        check_vma=False,
    )
```

```python
import jax
import jax.numpy as jnp
from jax import lax
from jax.experimental import pallas as pl
from jax.experimental.pallas import tpu as pltpu
from jax.sharding import PartitionSpec as P

TILE = 128
KSIZE = 11
RADIUS = 5
TAPS = KSIZE * KSIZE
LANES = 128
HALO = 24
REACH = 20
WINDOWS = 3
ROWS = TILE + 2 * HALO
SLOTS = (KSIZE + 1) // 2
DEPTH = SLOTS * LANES
MAIN = 144
REGIONS = ((0, 1, 24), (1, 2, 64), (2, 3, 104))
VMEM = pl.BlockSpec(memory_space=pltpu.VMEM)


def call(kernel, out_shape, scratch=(), limit=4, inputs=None):
    given = {} if inputs is None else {"in_specs": inputs}
    return pl.pallas_call(
        kernel,
        out_shape=out_shape,
        out_specs=[VMEM] * len(out_shape),
        **given,
        scratch_shapes=list(scratch),
        compiler_params=pltpu.CompilerParams(vmem_limit_bytes=limit * 2**20),
    )


def f32(*shape):
    return jax.ShapeDtypeStruct(shape, jnp.float32)


def lanes_of(shape):
    return lax.broadcasted_iota(jnp.int32, shape, len(shape) - 1)


def is_odd(axis):
    return lax.axis_index(axis) % 2 == 1


CHUNKS = 4


def load_kernel(observed_ref, psf_ref, block_ref, taps_ref, far_ref, near_ref, psf, sems):
    part = TILE // CHUNKS
    loads = [
        pltpu.make_async_copy(observed_ref.at[pl.ds(part * i, part)], block_ref.at[pl.ds(part * i, part)], sems.at[i])
        for i in range(CHUNKS)
    ]
    loads.append(pltpu.make_async_copy(psf_ref, psf, sems.at[CHUNKS]))
    for load in loads:
        load.start()
    taps_ref[...] = jnp.zeros((8, LANES), jnp.float32)
    for load in loads:
        load.wait()
    taps_ref[1:2, :TAPS] = psf[0, 0:1, :]
    taps_ref[2:3, :TAPS] = psf[0, 1:2, :]
    columns_kernel(block_ref, taps_ref, far_ref, near_ref)


def columns_kernel(block_ref, taps_ref, far_ref, near_ref):
    lane = lanes_of((32, LANES))

    def packed(side, first):
        out = jnp.zeros((32, LANES), jnp.float32)
        for part in range(4):
            rows = block_ref[32 * part : 32 * part + 32, LANES * side : LANES * side + LANES]
            moved = pltpu.roll(rows, (32 * part - first) % LANES, 1)
            out = jnp.where((lane >= 32 * part) & (lane < 32 * part + HALO), moved, out)
        return out

    left, right = packed(0, 0), packed(1, LANES - HALO)
    odd = is_odd("azi")
    near_ref[:32] = jnp.where(odd, left, right)
    far_ref[:32] = jnp.where(odd, right, left)
    first, second = taps_ref[...], pltpu.roll(taps_ref[...], 7, 0)
    near_ref[32:] = jnp.where(odd, first, second)
    far_ref[32:] = jnp.where(odd, second, first)


def side_halos(near_ref, far_ref):
    odd = is_odd("azi")
    near, far = near_ref[:32], far_ref[:32]
    has_left = lax.axis_index("azi") > 0
    has_right = lax.axis_index("azi") < lax.axis_size("azi") - 1
    return jnp.where(has_left, jnp.where(odd, near, far), 0.0), jnp.where(has_right, jnp.where(odd, far, near), 0.0)


def side_windows(block_ref, halos, part):
    rows = slice(32 * part, 32 * part + 32)
    lane = lanes_of((32, LANES))
    left = pltpu.roll(halos[0], (-32 * part) % LANES, 1)
    right = pltpu.roll(halos[1], (LANES - HALO - 32 * part) % LANES, 1)
    first = jnp.where(lane < HALO, left, pltpu.roll(block_ref[rows, :LANES], HALO, 1))
    second = jnp.where(lane < LANES - HALO, pltpu.roll(block_ref[rows, LANES:], LANES - HALO, 1), right)
    return first, second


def rows_kernel(block_ref, own_ref, far_ref, near_ref, _, taps_ref, two_ref, one_ref, top, low):
    halos = side_halos(near_ref, far_ref)
    odd = is_odd("azi")
    has_left = lax.axis_index("azi") > 0
    has_right = lax.axis_index("azi") < lax.axis_size("azi") - 1
    near_taps, far_taps = near_ref[33:34], far_ref[33:34]
    taps_ref[...] = own_ref[...]
    taps_ref[0:1] = jnp.where(has_left, jnp.where(odd, near_taps, far_taps), 0.0)
    taps_ref[3:4] = jnp.where(has_right, jnp.where(odd, far_taps, near_taps), 0.0)
    for ref, part, rows in ((top, 0, slice(0, HALO)), (low, 3, slice(TILE - HALO, TILE))):
        inner = slice(0, HALO) if part == 0 else slice(8, 32)
        first, second = side_windows(block_ref, halos, part)
        ref[:, :LANES] = first[inner]
        ref[:, LANES : 2 * LANES] = middle_window(block_ref[rows, :LANES], block_ref[rows, LANES:])
        ref[:, 2 * LANES :] = second[inner]
    top[REACH:, :LANES] = taps_ref[0:4]
    low[: HALO - REACH, :LANES] = taps_ref[0:4]
    odd_row = is_odd("rng")
    one_ref[...] = jnp.where(odd_row, top[...], low[...])
    two_ref[...] = jnp.where(odd_row, low[...], top[...])


def middle_window(first, second):
    lane = lanes_of(first.shape)
    return jnp.where(lane < 64, pltpu.roll(first, 64, 1), pltpu.roll(second, 64, 1))


def split(value):
    high = value.astype(jnp.bfloat16)
    return high, (value - high.astype(jnp.float32)).astype(jnp.bfloat16)


def product(parts, high, low, dims):
    rows = parts[0].shape[0]

    def dot(a, b):
        return lax.dot_general(a, b, (dims, ((), ())), preferred_element_type=jnp.float32)

    both = dot(jnp.concatenate(parts, axis=0), high)
    return both[:rows] + both[rows:] + dot(parts[0], low)


def put_parts(field_ref, rows, value):
    high = value.astype(jnp.bfloat16).astype(jnp.float32)
    field_ref[0, rows] = high
    field_ref[1, rows] = value - high


def stacked_rows(field_ref, first, count, offsets):
    return [
        jnp.concatenate(
            [field_ref[part, pl.ds(HALO + first + offset, count), :].astype(jnp.bfloat16) for offset in offsets],
            axis=1,
        )
        for part in range(2)
    ]


def adjoint_rows(field_ref, block, pair, first, count, lead):
    offsets = [RADIUS - 2 * slot for slot in range(SLOTS)]
    parts = stacked_rows(field_ref, first - lead, count + lead, offsets)
    high, low = [jnp.concatenate([block(part, slot) for slot in range(SLOTS)], axis=0) for part in range(2)]
    both = product(parts, high, low, ((1,), (0,)))
    if lead == 0:
        pair[:8, :] = jnp.zeros((8, LANES), jnp.float32)
    pair[pl.ds(8 if lead == 0 else 0, count + lead), :] = both[:, LANES:]
    return both[lead:, :LANES] + pair[pl.ds(7 if lead == 0 else lead - 1, count), :]


def forward_rows(field_ref, block, pair, first, count):
    offsets = [2 * slot - RADIUS for slot in range(SLOTS)]
    parts = stacked_rows(field_ref, first, count + 16, offsets)

    def turned(part):
        blocks = [block(part, slot) for slot in range(SLOTS)]
        halves = [
            jnp.concatenate([value[:, half * LANES : (half + 1) * LANES] for value in blocks], axis=1)
            for half in range(2)
        ]
        return jnp.concatenate(halves, axis=0)

    both = product(parts, turned(0), turned(1), ((1,), (1,)))
    pair[: count + 16, :] = both[:, LANES:]
    return both[:count, :LANES] + pair[pl.ds(1, count), :]


def tap_lines(taps):
    spot = (lanes_of((8, LANES)) + RADIUS) % LANES
    return [
        jnp.where(spot < KSIZE, jnp.take_along_axis(taps, jnp.minimum(KSIZE * u + spot, LANES - 1), axis=1), 0.0)
        for u in range(KSIZE)
    ]


def put_band(lines, offset, window, first, count, refs):
    slot, half = offset // 2, offset % 2
    place = (slice(slot * count, (slot + 1) * count), slice(half * LANES, (half + 1) * LANES))
    if offset >= KSIZE:
        for ref in refs:
            ref[place] = jnp.zeros((count, LANES), jnp.bfloat16)
        return
    before, after, bound = REGIONS[window]
    row = first + lax.broadcasted_iota(jnp.int32, (count, LANES), 0)
    left, right = [jnp.broadcast_to(lines[offset][tile : tile + 1], (count, LANES)) for tile in (before, after)]
    base = left if first + count <= bound else right if first >= bound else jnp.where(row < bound, left, right)
    refs[0][place], refs[1][place] = split(pltpu.roll(base, first, 1, stride=1, stride_axis=0))


def inside(window):
    lane = lanes_of((1, LANES))
    if window == 0:
        return (lane >= HALO) | (lax.axis_index("azi") > 0)
    if window == 2:
        return (lane < LANES - HALO) | (lax.axis_index("azi") < lax.axis_size("azi") - 1)
    return lane >= 0


def early_rows(rows, windows, blocks, outs, fields, pairs, between=lambda stage: None):
    own = slice(HALO, HALO + TILE)
    most, fewer = slice(8, TILE - 8), slice(16, TILE - 16)
    each = range(len(windows))
    keep = [inside(window) for window in windows]
    for i in each:
        for stage in range(4):
            for part in range(2):
                fields[i, stage, part, : HALO + 8] = jnp.zeros((HALO + 8, LANES), jnp.float32)
                fields[i, stage, part, HALO + TILE - 8 :] = jnp.zeros((HALO + 8, LANES), jnp.float32)
        put_parts(fields.at[i, 0], own, rows[i])
    for i in each:
        main = adjoint_rows(fields.at[i, 0], blocks[i], pairs.at[i, 0], -8, MAIN, 0)
        main = jnp.where(keep[i], main, 0.0)
        outs[i][0][...] = main
        put_parts(fields.at[i, 1], slice(HALO - 8, HALO + TILE + 8), main)
    between(0)
    for i in each:
        image = forward_rows(fields.at[i, 1], blocks[i], pairs.at[i, 1], most.start, TILE - 16)
        outs[i][1][most] = image
        put_parts(fields.at[i, 2], slice(HALO + most.start, HALO + most.stop), image)
    between(1)
    for i in each:
        grad = adjoint_rows(fields.at[i, 2], blocks[i], pairs.at[i, 2], most.start, TILE - 16, 16)
        grad = jnp.where(keep[i], grad, 0.0)
        outs[i][2][most] = grad
        put_parts(fields.at[i, 3], slice(HALO + most.start, HALO + most.stop), grad)
    between(2)
    for i in each:
        outs[i][3][fewer] = forward_rows(fields.at[i, 3], blocks[i], pairs.at[i, 3], fewer.start, TILE - 32)
    between(3)


PATCH = 32
REST = LANES - PATCH


def middle_kernel(block_ref, taps_ref, *refs):
    outs, sides = refs[:4], (refs[4:6], refs[6:8])
    high, low, fields, pairs = refs[8:]
    lines = tap_lines(taps_ref[...])
    for offset in range(2 * SLOTS):
        put_band(lines, offset, 1, 0, LANES, (high, low))

    def between(stage):
        for offset in range(3 * stage, 3 * stage + 3):
            put_band(lines, offset, 0, PATCH, REST, sides[0])
            put_band(lines, offset, 2, 0, REST, sides[1])

    def block(part, slot):
        return (high, low)[part][slot * LANES : (slot + 1) * LANES, :]

    rows = middle_window(block_ref[:, :LANES], block_ref[:, LANES:])
    early_rows([rows], (1,), [block], [outs], fields, pairs, between)


def sides_kernel(block_ref, far_ref, near_ref, taps_ref, *refs):
    rest, middle = (refs[:2], refs[2:4]), refs[4:8]
    outs, refs = (refs[8:12], refs[12:16]), refs[16:]
    plain_ref, turned_ref, inner_ref, patches, fields, pairs = refs
    taps = taps_ref[...]
    lines = tap_lines(taps)
    for offset in range(2 * SLOTS):
        put_band(lines, offset, 0, 0, PATCH, (patches.at[0, 0], patches.at[0, 1]))
        put_band(lines, offset, 2, REST, PATCH, (patches.at[1, 0], patches.at[1, 1]))

    def piece(side, part, slot):
        whole = rest[side][part][slot * REST : (slot + 1) * REST, :]
        patch = patches[side, part, slot * PATCH : (slot + 1) * PATCH, :]
        return jnp.concatenate([patch, whole] if side == 0 else [whole, patch], axis=0)

    blocks = [lambda part, slot: piece(0, part, slot), lambda part, slot: piece(1, part, slot)]

    def between(stage):
        if stage == 0:
            plain_ref[...] = jnp.concatenate(row_weights(taps, range(4), False), axis=0)
        if stage == 1:
            turned_ref[...] = jnp.concatenate(row_weights(taps, range(4), True), axis=0)

    halos = side_halos(near_ref, far_ref)
    parts = [side_windows(block_ref, halos, part) for part in range(4)]
    rows = [jnp.concatenate([part[side] for part in parts], axis=0) for side in range(2)]
    early_rows(rows, (0, 2), blocks, outs, fields, pairs, between)
    early = (outs[0], middle, outs[1])
    inner = [[window[0][8 + INNER.start : 8 + INNER.stop] for window in early]]
    inner += [[window[i][INNER] for window in early] for i in range(1, 4)]
    inner_ref[...] = jnp.broadcast_to(record_of(inner, 0), (8, LANES))


GROUP = 32
GROUPS = 3 * LANES // GROUP
EDGE = 4 * RADIUS
COUNT = 24


def row_weights(taps, tiles, turned):
    lane = lanes_of((8, LANES))
    pieces = [[] for _ in tiles]
    for part in range(3):
        u = lane % GROUP
        if turned:
            u = KSIZE - 1 - u
        v = part * (LANES // GROUP) + lane // GROUP
        base = jnp.take_along_axis(taps, jnp.clip(u * KSIZE + v, 0, LANES - 1), axis=1)
        base = jnp.where((u >= 0) & (u < KSIZE) & (v < KSIZE), base, 0.0)
        for piece, tile in zip(pieces, tiles):
            row = jnp.broadcast_to(base[tile : tile + 1], (COUNT, LANES))
            piece.append(pltpu.roll(row, 0, 1, stride=1, stride_axis=0))
    return [jnp.concatenate(piece, axis=1) for piece in pieces]


def spread(rows, sign):
    moved = [rows if v == RADIUS else pltpu.roll(rows, (sign * (v - RADIUS)) % LANES, 1) for v in range(KSIZE)]
    moved.append(jnp.zeros((GROUP * (GROUPS - KSIZE), LANES), rows.dtype))
    return jnp.concatenate(moved, axis=0)


def forward_edge(rows, window, weights):
    before, after, bound = REGIONS[window]
    high, low = [spread(part, -1) for part in split(rows)]
    both = [weights[COUNT * tile : COUNT * tile + COUNT] for tile in (before, after)]
    result = product(split(jnp.concatenate(both, axis=0)), high, low, ((1,), (0,)))
    return jnp.where(lanes_of((COUNT, LANES)) < bound, result[:COUNT], result[COUNT:])


def adjoint_edge(rows, window, weights):
    before, after, bound = REGIONS[window]
    lane = lanes_of((GROUP, LANES))
    whole = [spread(part, 1) for part in split(rows)]
    high, low = [
        jnp.concatenate(
            [part]
            + [
                jnp.where(lane < bound + v - RADIUS, moved, jnp.zeros_like(moved))
                for v, moved in enumerate(part[GROUP * v : GROUP * v + GROUP] for v in range(KSIZE))
            ]
            + [part[GROUP * KSIZE :]],
            axis=0,
        )
        for part in whole
    ]
    left, right = [weights[COUNT * tile : COUNT * tile + COUNT] for tile in (before, after)]
    return product(split(jnp.concatenate([right, left - right], axis=1)), high, low, ((1,), (0,)))


def edge_rows(side, message, plain, turned, plain_ref, turned_ref, early, outs, edge, fields):
    wide = WINDOWS * LANES
    each = range(WINDOWS)
    base = 16 if side == 0 else -80
    near = slice(24, 64) if side == 0 else slice(0, 40)
    own = slice(8, 48) if side == 0 else slice(80, 120)
    out = slice(16, 40) if side == 0 else slice(24, 48)
    start = (-15, -10, -5, 0) if side == 0 else (123, 118, 113, 108)
    beyond = lax.axis_index("rng") > 0 if side == 0 else lax.axis_index("rng") < lax.axis_size("rng") - 1
    keep = [inside(window) for window in each]
    row = lax.broadcasted_iota(jnp.int32, (EDGE, LANES), 0)
    half = EDGE // 2

    def cols(window):
        return pl.ds(window * LANES, LANES)

    def spot(stage, reach=0, count=EDGE):
        return pl.ds(start[stage] - reach + base, count)

    def in_image(stage, window):
        inner = row >= -start[stage] if side == 0 else row < TILE - start[stage]
        return keep[window] & (beyond | inner)

    row24 = lax.broadcasted_iota(jnp.int32, (HALO, 1), 0)
    if side == 0:
        edge[:HALO] = jnp.where(row24 < HALO - REACH, 0.0, message)
        edge[HALO:] = jnp.zeros((16, wide), jnp.float32)
        strip = slice(4, 36)
    else:
        edge[:16] = jnp.zeros((16, wide), jnp.float32)
        edge[16:] = jnp.where(row24 >= REACH, 0.0, message)
        strip = slice(6, 38)
    for window in each:
        main = early[window][0]
        field = fields.at[0, window]
        if side == 0:
            field[:8] = jnp.zeros((8, LANES), jnp.float32)
            field[8:16] = jnp.where(beyond, main[:8], 0.0)
            field[16:64] = main[8:56]
        else:
            field[:48] = main[88:136]
            field[48:56] = jnp.where(beyond, main[136:], 0.0)
            field[56:] = jnp.zeros((16, LANES), jnp.float32)
        result = adjoint_edge(edge[strip, cols(window)], window, turned)
        field[spot(0), :] += jnp.where(in_image(0, window), result[:EDGE], 0.0)
        outs[0][:, cols(window)] = field[out]

    yield
    out_row = lax.broadcasted_iota(jnp.int32, (4 * COUNT, wide), 0) % COUNT
    mixed = (plain, plain_ref[...]) if side == 0 else (plain_ref[...], plain)
    mixed = jnp.where(out_row < half, *mixed)
    results = [forward_edge(fields[0, window, spot(1, RADIUS, GROUP), :], window, mixed) for window in each]
    for window in each:
        field = fields.at[1, window]
        if side == 0:
            field[:24] = jnp.zeros((24, LANES), jnp.float32)
        else:
            field[40:] = jnp.zeros((32, LANES), jnp.float32)
        field[near] = early[window][1][own]
        field[spot(1), :] = results[window][:EDGE]
        outs[1][:, cols(window)] = field[out]

    yield
    in_row = lanes_of((4 * COUNT, wide)) % GROUP
    if side == 0:
        mixed = jnp.where(in_row < half, turned, turned_ref[...])
    else:
        mixed = jnp.where(in_row < EDGE, turned_ref[...], turned)
    for window in each:
        result = adjoint_edge(fields[1, window, spot(2, RADIUS, GROUP), :], window, mixed)
        field = fields.at[2, window]
        if side == 0:
            field[8:24] = jnp.zeros((16, LANES), jnp.float32)
        else:
            field[40:56] = jnp.zeros((16, LANES), jnp.float32)
        field[near] = early[window][2][own]
        field[spot(2), :] = jnp.where(in_image(2, window), result[:EDGE], 0.0)
        outs[2][:, cols(window)] = field[out]

    yield
    results = [forward_edge(fields[2, window, spot(3, RADIUS, GROUP), :], window, plain_ref[...]) for window in each]
    for window in each:
        rest = COUNT - EDGE
        if side == 0:
            outs[3][EDGE:, cols(window)] = early[window][3][EDGE:COUNT]
            outs[3][:EDGE, cols(window)] = results[window][:EDGE]
        else:
            outs[3][:rest, cols(window)] = early[window][3][TILE - COUNT : TILE - EDGE]
            outs[3][rest:, cols(window)] = results[window][:EDGE]
    yield


INNER = slice(COUNT, TILE - COUNT)


def record_of(values, position):
    lane = lanes_of((1, LANES))
    bounds = ((24, 108), (20, 108), (20, 104))

    def total(pieces):
        sums = [
            jnp.where((lane >= low) & (lane < high), jnp.sum(piece, axis=0, keepdims=True), 0.0)
            for piece, (low, high) in zip(pieces, bounds)
        ]
        return jnp.sum(sums[0] + sums[1] + sums[2], axis=1, keepdims=True)

    def best(first, second):
        size = total([b * b for b in second])
        cross = total([a * b for a, b in zip(first, second)])
        ratio = jnp.where(size > 0.0, cross / jnp.where(size > 0.0, size, 1.0), 0.0)
        rest = total([(a - ratio * b) ** 2 for a, b in zip(first, second)])
        return total([a * a for a in first]), size, ratio, rest

    grad, image, grad2, image2 = values
    line = jnp.zeros((1, LANES), jnp.float32)
    for index, value in enumerate(best(grad, grad2) + best(image, image2)):
        line = jnp.where(lane == position + index, value, line)
    return line


def edge_kernel(*refs):
    early = [refs[4 * window : 4 * window + 4] for window in (1, 0, 2)]
    two_ref, one_ref, plain_ref, turned_ref, inner_ref = refs[12:17]
    tops, lows, record_ref, edge, fields = refs[17:21], refs[21:25], *refs[25:]
    odd = is_odd("rng")
    one, two = one_ref[...], two_ref[...]
    has_above = lax.axis_index("rng") > 0
    has_below = lax.axis_index("rng") < lax.axis_size("rng") - 1
    above = jnp.where(has_above, jnp.where(odd, one, two), 0.0)
    below = jnp.where(has_below, jnp.where(odd, two, one), 0.0)
    row = lax.broadcasted_iota(jnp.int32, (8, LANES), 0)
    taps = jnp.where(row < 4, above[:8, :LANES], below[HALO - 8 :, :LANES])
    turned, plain = row_weights(taps, range(8), True), row_weights(taps, range(8), False)
    (turned, turned_low), (plain, plain_low) = [
        [jnp.concatenate(weights[side : side + 4], axis=0) for side in (0, 4)] for weights in (turned, plain)
    ]
    top = edge_rows(0, above, plain, turned, plain_ref, turned_ref, early, tops, edge.at[0], fields.at[0])
    low = edge_rows(1, below, plain_low, turned_low, plain_ref, turned_ref, early, lows, edge.at[1], fields.at[1])
    for _ in zip(top, low):
        pass

    def windows(i):
        both = jnp.concatenate([tops[i][...], lows[i][...]], axis=0)
        return [both[:, w * LANES : (w + 1) * LANES] for w in range(WINDOWS)]

    line = inner_ref[:1] + record_of([windows(i) for i in range(4)], 8)
    record_ref[...] = jnp.broadcast_to(line[None], record_ref.shape)


def combine_kernel(records_ref, block_ref, *refs):
    early = [refs[4 * window : 4 * window + 4] for window in (1, 0, 2)]
    tops, lows, (estimate_ref, residual_ref) = refs[12:16], refs[16:20], refs[20:]
    records = records_ref[:, 0, :]
    lane = lanes_of((1, LANES))

    def total(value, place):
        wanted = (lane % 8 == place) & (lane < 24)
        return jnp.sum(jnp.where(wanted, jnp.sum(value, axis=0, keepdims=True), 0.0), axis=1, keepdims=True)

    gamma = total(records, 0)
    delta = total(records, 4)
    alpha = gamma / delta
    apart = records + (alpha - pltpu.roll(records, 1, 1)) ** 2 * pltpu.roll(records, 2, 1)
    gamma_new = total(apart, 3)
    bent = total(apart, 7)
    factor = gamma_new / gamma
    delta_new = bent - factor * factor * delta
    alpha_new = gamma_new / delta_new
    first = alpha + alpha_new * (1.0 + factor)
    second = -alpha_new * alpha

    def own(a, b):
        parts = [first * a[w] + second * b[w] for w in range(WINDOWS)]
        lanes = lanes_of(parts[0].shape)
        middle = pltpu.roll(parts[1], 64, 1)
        left = jnp.where(lanes < 84, pltpu.roll(parts[0], LANES - HALO, 1), middle)
        right = jnp.where(lanes < 44, middle, pltpu.roll(parts[2], HALO, 1))
        return left, right

    def windows(ref):
        return [ref[:, w * LANES : (w + 1) * LANES] for w in range(WINDOWS)]

    for rows, pieces in (
        (slice(0, COUNT), lambda i: windows(tops[i])),
        (INNER, lambda i: [early[w][i][slice(8 + COUNT, 8 + TILE - COUNT) if i == 0 else INNER] for w in range(WINDOWS)]),
        (slice(TILE - COUNT, TILE), lambda i: windows(lows[i])),
    ):
        left, right = own(pieces(0), pieces(2))
        estimate_ref[rows, :LANES] = left
        estimate_ref[rows, LANES:] = right
        left, right = own(pieces(1), pieces(3))
        residual_ref[rows, :LANES] = block_ref[rows, :LANES] - left
        residual_ref[rows, LANES:] = block_ref[rows, LANES:] - right


def partners(axis, other):
    count, across = lax.axis_size(axis), lax.axis_size(other)

    def number(i, j):
        return i * across + j if axis == "rng" else j * count + i

    near, far = [], []
    for i in range(count):
        for j in range(across):
            near.append((number(i, j), number(i ^ 1, j)))
            beside = i + 1 if i % 2 else i - 1
            far.append((number(i, j), number(beside, j) if 0 <= beside < count else number(i, j ^ 1)))
    return near, far


BOTH = ("rng", "azi")


def body(observed, psf_tiles):
    devices = lax.axis_size("rng") * lax.axis_size("azi")
    wide = WINDOWS * LANES
    block, own, far, near = call(
        load_kernel,
        [f32(TILE, 2 * LANES), f32(8, LANES), f32(40, LANES), f32(40, LANES)],
        [pltpu.VMEM((1, 2, TAPS), jnp.float32), pltpu.SemaphoreType.DMA((CHUNKS + 1,))],
        inputs=[pl.BlockSpec(memory_space=pltpu.HBM)] * 2,
    )(
        pltpu.with_memory_space_constraint(observed, pltpu.HBM),
        pltpu.with_memory_space_constraint(psf_tiles, pltpu.HBM),
    )
    near_pairs, far_pairs = partners("azi", "rng")
    far = lax.ppermute(far, BOTH, far_pairs)
    near = lax.ppermute(near, BOTH, near_pairs)
    early = [f32(MAIN, LANES)] + [f32(TILE, LANES)] * 3
    rest = [jax.ShapeDtypeStruct((SLOTS * REST, 2 * LANES), jnp.bfloat16)] * 4

    def scratch(windows):
        return [
            pltpu.VMEM((windows, 4, 2, ROWS, LANES), jnp.float32),
            pltpu.VMEM((windows, 4, MAIN + 8, LANES), jnp.float32),
        ]

    *middle, high0, low0, high2, low2 = call(
        middle_kernel, early + rest, [pltpu.VMEM((DEPTH, 2 * LANES), jnp.bfloat16)] * 2 + scratch(1), limit=8
    )(block, own)
    taps, two, one = call(
        rows_kernel,
        [f32(8, LANES), f32(HALO, wide), f32(HALO, wide)],
        [pltpu.VMEM((HALO, wide), jnp.float32)] * 2,
    )(block, own, far, near, middle[0])
    one_pairs, two_pairs = partners("rng", "azi")
    two = lax.ppermute(two, BOTH, two_pairs)
    one = lax.ppermute(one, BOTH, one_pairs)
    *sides, plain, turned, inner = call(
        sides_kernel,
        early * 2 + [f32(4 * COUNT, wide)] * 2 + [f32(8, LANES)],
        [pltpu.VMEM((2, 2, SLOTS * PATCH, 2 * LANES), jnp.bfloat16)] + scratch(2),
        limit=8,
    )(block, far, near, taps, high0, low0, high2, low2, *middle)
    *edges, record = call(
        edge_kernel,
        [f32(COUNT, wide)] * 8 + [f32(devices, 1, LANES)],
        [pltpu.VMEM((2, 40, wide), jnp.float32), pltpu.VMEM((2, 3, WINDOWS, 72, LANES), jnp.float32)],
        limit=8,
    )(*middle, *sides, two, one, plain, turned, inner)
    records = lax.all_to_all(record, BOTH, 0, 0, tiled=True)
    estimate, residual = call(combine_kernel, [f32(TILE, 2 * LANES)] * 2)(
        records, block, *middle, *sides, *edges
    )
    return estimate, residual


def solution(mesh):
    return jax.shard_map(
        body,
        mesh=mesh,
        in_specs=(P("rng", "azi"), P("rng", "azi", None)),
        out_specs=(P("rng", "azi"), P("rng", "azi")),
        check_vma=False,
    )
```

```python
import jax
import jax.numpy as jnp
from jax import lax
from jax.experimental import pallas as pl
from jax.experimental.pallas import tpu as pltpu
from jax.sharding import PartitionSpec as P

TILE = 128
KSIZE = 11
RADIUS = 5
TAPS = KSIZE * KSIZE
LANES = 128
HALO = 24
REACH = 20
WINDOWS = 3
ROWS = TILE + 2 * HALO
SLOTS = (KSIZE + 1) // 2
DEPTH = SLOTS * LANES
MAIN = 144
REGIONS = ((0, 1, 24), (1, 2, 64), (2, 3, 104))
VMEM = pl.BlockSpec(memory_space=pltpu.VMEM)


def call(kernel, out_shape, scratch=(), limit=4, inputs=None):
    given = {} if inputs is None else {"in_specs": inputs}
    return pl.pallas_call(
        kernel,
        out_shape=out_shape,
        out_specs=[VMEM] * len(out_shape),
        **given,
        scratch_shapes=list(scratch),
        compiler_params=pltpu.CompilerParams(vmem_limit_bytes=limit * 2**20),
    )


def f32(*shape):
    return jax.ShapeDtypeStruct(shape, jnp.float32)


def lanes_of(shape):
    return lax.broadcasted_iota(jnp.int32, shape, len(shape) - 1)


def is_odd(axis):
    return lax.axis_index(axis) % 2 == 1


CHUNKS = 4


def load_kernel(observed_ref, psf_ref, block_ref, taps_ref, far_ref, near_ref, psf, sems):
    part = TILE // CHUNKS
    loads = [
        pltpu.make_async_copy(observed_ref.at[pl.ds(part * i, part)], block_ref.at[pl.ds(part * i, part)], sems.at[i])
        for i in range(CHUNKS)
    ]
    loads.append(pltpu.make_async_copy(psf_ref, psf, sems.at[CHUNKS]))
    for load in loads:
        load.start()
    taps_ref[...] = jnp.zeros((8, LANES), jnp.float32)
    for load in loads:
        load.wait()
    taps_ref[1:2, :TAPS] = psf[0, 0:1, :]
    taps_ref[2:3, :TAPS] = psf[0, 1:2, :]
    columns_kernel(block_ref, taps_ref, far_ref, near_ref)


def columns_kernel(block_ref, taps_ref, far_ref, near_ref):
    lane = lanes_of((32, LANES))

    def packed(side, first):
        out = jnp.zeros((32, LANES), jnp.float32)
        for part in range(4):
            rows = block_ref[32 * part : 32 * part + 32, LANES * side : LANES * side + LANES]
            moved = pltpu.roll(rows, (32 * part - first) % LANES, 1)
            out = jnp.where((lane >= 32 * part) & (lane < 32 * part + HALO), moved, out)
        return out

    left, right = packed(0, 0), packed(1, LANES - HALO)
    odd = is_odd("azi")
    near_ref[:32] = jnp.where(odd, left, right)
    far_ref[:32] = jnp.where(odd, right, left)
    first, second = taps_ref[...], pltpu.roll(taps_ref[...], 7, 0)
    near_ref[32:] = jnp.where(odd, first, second)
    far_ref[32:] = jnp.where(odd, second, first)


def side_halos(near_ref, far_ref):
    odd = is_odd("azi")
    near, far = near_ref[:32], far_ref[:32]
    has_left = lax.axis_index("azi") > 0
    has_right = lax.axis_index("azi") < lax.axis_size("azi") - 1
    return jnp.where(has_left, jnp.where(odd, near, far), 0.0), jnp.where(has_right, jnp.where(odd, far, near), 0.0)


def side_windows(block_ref, halos, part):
    rows = slice(32 * part, 32 * part + 32)
    lane = lanes_of((32, LANES))
    left = pltpu.roll(halos[0], (-32 * part) % LANES, 1)
    right = pltpu.roll(halos[1], (LANES - HALO - 32 * part) % LANES, 1)
    first = jnp.where(lane < HALO, left, pltpu.roll(block_ref[rows, :LANES], HALO, 1))
    second = jnp.where(lane < LANES - HALO, pltpu.roll(block_ref[rows, LANES:], LANES - HALO, 1), right)
    return first, second


def rows_kernel(block_ref, own_ref, far_ref, near_ref, _, taps_ref, two_ref, one_ref, top, low):
    halos = side_halos(near_ref, far_ref)
    odd = is_odd("azi")
    has_left = lax.axis_index("azi") > 0
    has_right = lax.axis_index("azi") < lax.axis_size("azi") - 1
    near_taps, far_taps = near_ref[33:34], far_ref[33:34]
    taps_ref[...] = own_ref[...]
    taps_ref[0:1] = jnp.where(has_left, jnp.where(odd, near_taps, far_taps), 0.0)
    taps_ref[3:4] = jnp.where(has_right, jnp.where(odd, far_taps, near_taps), 0.0)
    for ref, part, rows in ((top, 0, slice(0, HALO)), (low, 3, slice(TILE - HALO, TILE))):
        inner = slice(0, HALO) if part == 0 else slice(8, 32)
        first, second = side_windows(block_ref, halos, part)
        ref[:, :LANES] = first[inner]
        ref[:, LANES : 2 * LANES] = middle_window(block_ref[rows, :LANES], block_ref[rows, LANES:])
        ref[:, 2 * LANES :] = second[inner]
    top[REACH:, :LANES] = taps_ref[0:4]
    low[: HALO - REACH, :LANES] = taps_ref[0:4]
    odd_row = is_odd("rng")
    one_ref[...] = jnp.where(odd_row, top[...], low[...])
    two_ref[...] = jnp.where(odd_row, low[...], top[...])


def middle_window(first, second):
    lane = lanes_of(first.shape)
    return jnp.where(lane < 64, pltpu.roll(first, 64, 1), pltpu.roll(second, 64, 1))


def split(value):
    high = value.astype(jnp.bfloat16)
    return high, (value - high.astype(jnp.float32)).astype(jnp.bfloat16)


def product(parts, high, low, dims):
    rows = parts[0].shape[0]

    def dot(a, b):
        return lax.dot_general(a, b, (dims, ((), ())), preferred_element_type=jnp.float32)

    both = dot(jnp.concatenate(parts, axis=0), high)
    return both[:rows] + both[rows:] + dot(parts[0], low)


def put_parts(field_ref, rows, value):
    high = value.astype(jnp.bfloat16).astype(jnp.float32)
    field_ref[0, rows] = high
    field_ref[1, rows] = value - high


def stacked_rows(field_ref, first, count, offsets):
    return [
        jnp.concatenate(
            [field_ref[part, pl.ds(HALO + first + offset, count), :].astype(jnp.bfloat16) for offset in offsets],
            axis=1,
        )
        for part in range(2)
    ]


def adjoint_rows(field_ref, block, pair, first, count, lead):
    offsets = [RADIUS - 2 * slot for slot in range(SLOTS)]
    parts = stacked_rows(field_ref, first - lead, count + lead, offsets)
    high, low = [jnp.concatenate([block(part, slot) for slot in range(SLOTS)], axis=0) for part in range(2)]
    both = product(parts, high, low, ((1,), (0,)))
    if lead == 0:
        pair[:8, :] = jnp.zeros((8, LANES), jnp.float32)
    pair[pl.ds(8 if lead == 0 else 0, count + lead), :] = both[:, LANES:]
    return both[lead:, :LANES] + pair[pl.ds(7 if lead == 0 else lead - 1, count), :]


def forward_rows(field_ref, block, pair, first, count):
    offsets = [2 * slot - RADIUS for slot in range(SLOTS)]
    parts = stacked_rows(field_ref, first, count + 16, offsets)

    def turned(part):
        blocks = [block(part, slot) for slot in range(SLOTS)]
        halves = [
            jnp.concatenate([value[:, half * LANES : (half + 1) * LANES] for value in blocks], axis=1)
            for half in range(2)
        ]
        return jnp.concatenate(halves, axis=0)

    both = product(parts, turned(0), turned(1), ((1,), (1,)))
    pair[: count + 16, :] = both[:, LANES:]
    return both[:count, :LANES] + pair[pl.ds(1, count), :]


def tap_lines(taps):
    spot = (lanes_of((8, LANES)) + RADIUS) % LANES
    return [
        jnp.where(spot < KSIZE, jnp.take_along_axis(taps, jnp.minimum(KSIZE * u + spot, LANES - 1), axis=1), 0.0)
        for u in range(KSIZE)
    ]


def put_band(lines, offset, window, first, count, refs):
    slot, half = offset // 2, offset % 2
    place = (slice(slot * count, (slot + 1) * count), slice(half * LANES, (half + 1) * LANES))
    if offset >= KSIZE:
        for ref in refs:
            ref[place] = jnp.zeros((count, LANES), jnp.bfloat16)
        return
    before, after, bound = REGIONS[window]
    row = first + lax.broadcasted_iota(jnp.int32, (count, LANES), 0)
    left, right = [jnp.broadcast_to(lines[offset][tile : tile + 1], (count, LANES)) for tile in (before, after)]
    base = left if first + count <= bound else right if first >= bound else jnp.where(row < bound, left, right)
    refs[0][place], refs[1][place] = split(pltpu.roll(base, first, 1, stride=1, stride_axis=0))


def inside(window):
    lane = lanes_of((1, LANES))
    if window == 0:
        return (lane >= HALO) | (lax.axis_index("azi") > 0)
    if window == 2:
        return (lane < LANES - HALO) | (lax.axis_index("azi") < lax.axis_size("azi") - 1)
    return lane >= 0


def early_rows(rows, windows, blocks, outs, fields, pairs, between=lambda stage: None):
    own = slice(HALO, HALO + TILE)
    most, fewer = slice(8, TILE - 8), slice(16, TILE - 16)
    each = range(len(windows))
    keep = [inside(window) for window in windows]
    for i in each:
        for stage in range(4):
            for part in range(2):
                fields[i, stage, part, : HALO + 8] = jnp.zeros((HALO + 8, LANES), jnp.float32)
                fields[i, stage, part, HALO + TILE - 8 :] = jnp.zeros((HALO + 8, LANES), jnp.float32)
        put_parts(fields.at[i, 0], own, rows[i])
    for i in each:
        main = adjoint_rows(fields.at[i, 0], blocks[i], pairs.at[i, 0], -8, MAIN, 0)
        main = jnp.where(keep[i], main, 0.0)
        outs[i][0][...] = main
        put_parts(fields.at[i, 1], slice(HALO - 8, HALO + TILE + 8), main)
    between(0)
    for i in each:
        image = forward_rows(fields.at[i, 1], blocks[i], pairs.at[i, 1], most.start, TILE - 16)
        outs[i][1][most] = image
        put_parts(fields.at[i, 2], slice(HALO + most.start, HALO + most.stop), image)
    between(1)
    for i in each:
        grad = adjoint_rows(fields.at[i, 2], blocks[i], pairs.at[i, 2], most.start, TILE - 16, 16)
        grad = jnp.where(keep[i], grad, 0.0)
        outs[i][2][most] = grad
        put_parts(fields.at[i, 3], slice(HALO + most.start, HALO + most.stop), grad)
    between(2)
    for i in each:
        outs[i][3][fewer] = forward_rows(fields.at[i, 3], blocks[i], pairs.at[i, 3], fewer.start, TILE - 32)
    between(3)


PATCH = 32
REST = LANES - PATCH


def middle_kernel(block_ref, taps_ref, *refs):
    outs, sides = refs[:4], (refs[4:6], refs[6:8])
    high, low, fields, pairs = refs[8:]
    lines = tap_lines(taps_ref[...])
    for offset in range(2 * SLOTS):
        put_band(lines, offset, 1, 0, LANES, (high, low))

    def between(stage):
        for offset in range(3 * stage, 3 * stage + 3):
            put_band(lines, offset, 0, PATCH, REST, sides[0])
            put_band(lines, offset, 2, 0, REST, sides[1])

    def block(part, slot):
        return (high, low)[part][slot * LANES : (slot + 1) * LANES, :]

    rows = middle_window(block_ref[:, :LANES], block_ref[:, LANES:])
    early_rows([rows], (1,), [block], [outs], fields, pairs, between)


def sides_kernel(block_ref, far_ref, near_ref, taps_ref, *refs):
    rest, middle = (refs[:2], refs[2:4]), refs[4:8]
    outs, refs = (refs[8:12], refs[12:16]), refs[16:]
    plain_ref, turned_ref, inner_ref, patches, fields, pairs = refs
    taps = taps_ref[...]
    lines = tap_lines(taps)
    for offset in range(2 * SLOTS):
        put_band(lines, offset, 0, 0, PATCH, (patches.at[0, 0], patches.at[0, 1]))
        put_band(lines, offset, 2, REST, PATCH, (patches.at[1, 0], patches.at[1, 1]))

    def piece(side, part, slot):
        whole = rest[side][part][slot * REST : (slot + 1) * REST, :]
        patch = patches[side, part, slot * PATCH : (slot + 1) * PATCH, :]
        return jnp.concatenate([patch, whole] if side == 0 else [whole, patch], axis=0)

    blocks = [lambda part, slot: piece(0, part, slot), lambda part, slot: piece(1, part, slot)]

    def between(stage):
        if stage == 0:
            plain_ref[...] = jnp.concatenate(row_weights(taps, range(4), False), axis=0)
        if stage == 1:
            turned_ref[...] = jnp.concatenate(row_weights(taps, range(4), True), axis=0)

    halos = side_halos(near_ref, far_ref)
    parts = [side_windows(block_ref, halos, part) for part in range(4)]
    rows = [jnp.concatenate([part[side] for part in parts], axis=0) for side in range(2)]
    early_rows(rows, (0, 2), blocks, outs, fields, pairs, between)
    early = (outs[0], middle, outs[1])
    inner = [[window[0][8 + INNER.start : 8 + INNER.stop] for window in early]]
    inner += [[window[i][INNER] for window in early] for i in range(1, 4)]
    inner_ref[...] = jnp.broadcast_to(record_of(inner, 0), (8, LANES))


GROUP = 32
GROUPS = 3 * LANES // GROUP
EDGE = 4 * RADIUS
COUNT = 24


def row_weights(taps, tiles, turned):
    lane = lanes_of((8, LANES))
    pieces = [[] for _ in tiles]
    for part in range(3):
        u = lane % GROUP
        if turned:
            u = KSIZE - 1 - u
        v = part * (LANES // GROUP) + lane // GROUP
        base = jnp.take_along_axis(taps, jnp.clip(u * KSIZE + v, 0, LANES - 1), axis=1)
        base = jnp.where((u >= 0) & (u < KSIZE) & (v < KSIZE), base, 0.0)
        for piece, tile in zip(pieces, tiles):
            row = jnp.broadcast_to(base[tile : tile + 1], (COUNT, LANES))
            piece.append(pltpu.roll(row, 0, 1, stride=1, stride_axis=0))
    return [jnp.concatenate(piece, axis=1) for piece in pieces]


def spread(rows, sign):
    moved = [rows if v == RADIUS else pltpu.roll(rows, (sign * (v - RADIUS)) % LANES, 1) for v in range(KSIZE)]
    moved.append(jnp.zeros((GROUP * (GROUPS - KSIZE), LANES), rows.dtype))
    return jnp.concatenate(moved, axis=0)


def forward_edge(rows, window, weights):
    before, after, bound = REGIONS[window]
    high, low = [spread(part, -1)[: GROUP * KSIZE] for part in split(rows)]
    both = [weights[COUNT * tile : COUNT * tile + COUNT] for tile in (before, after)]
    result = product(split(jnp.concatenate(both, axis=0)[:, : GROUP * KSIZE]), high, low, ((1,), (0,)))
    return jnp.where(lanes_of((COUNT, LANES)) < bound, result[:COUNT], result[COUNT:])


def adjoint_edge(rows, window, weights):
    before, after, bound = REGIONS[window]
    lane = lanes_of((GROUP, LANES))
    whole = [spread(part, 1) for part in split(rows)]
    high, low = [
        jnp.concatenate(
            [part]
            + [
                jnp.where(lane < bound + v - RADIUS, moved, jnp.zeros_like(moved))
                for v, moved in enumerate(part[GROUP * v : GROUP * v + GROUP] for v in range(KSIZE))
            ]
            + [part[GROUP * KSIZE :]],
            axis=0,
        )
        for part in whole
    ]
    left, right = [weights[COUNT * tile : COUNT * tile + COUNT] for tile in (before, after)]
    return product(split(jnp.concatenate([right, left - right], axis=1)), high, low, ((1,), (0,)))


def edge_rows(side, message, plain, turned, plain_ref, turned_ref, early, outs, edge, fields):
    wide = WINDOWS * LANES
    each = range(WINDOWS)
    base = 16 if side == 0 else -80
    near = slice(24, 64) if side == 0 else slice(0, 40)
    own = slice(8, 48) if side == 0 else slice(80, 120)
    out = slice(16, 40) if side == 0 else slice(24, 48)
    start = (-15, -10, -5, 0) if side == 0 else (123, 118, 113, 108)
    beyond = lax.axis_index("rng") > 0 if side == 0 else lax.axis_index("rng") < lax.axis_size("rng") - 1
    keep = [inside(window) for window in each]
    row = lax.broadcasted_iota(jnp.int32, (EDGE, LANES), 0)
    half = EDGE // 2

    def cols(window):
        return pl.ds(window * LANES, LANES)

    def spot(stage, reach=0, count=EDGE):
        return pl.ds(start[stage] - reach + base, count)

    def in_image(stage, window):
        inner = row >= -start[stage] if side == 0 else row < TILE - start[stage]
        return keep[window] & (beyond | inner)

    row24 = lax.broadcasted_iota(jnp.int32, (HALO, 1), 0)
    if side == 0:
        edge[:HALO] = jnp.where(row24 < HALO - REACH, 0.0, message)
        edge[HALO:] = jnp.zeros((16, wide), jnp.float32)
        strip = slice(4, 36)
    else:
        edge[:16] = jnp.zeros((16, wide), jnp.float32)
        edge[16:] = jnp.where(row24 >= REACH, 0.0, message)
        strip = slice(6, 38)
    for window in each:
        main = early[window][0]
        field = fields.at[0, window]
        if side == 0:
            field[:8] = jnp.zeros((8, LANES), jnp.float32)
            field[8:16] = jnp.where(beyond, main[:8], 0.0)
            field[16:64] = main[8:56]
        else:
            field[:48] = main[88:136]
            field[48:56] = jnp.where(beyond, main[136:], 0.0)
            field[56:] = jnp.zeros((16, LANES), jnp.float32)
        result = adjoint_edge(edge[strip, cols(window)], window, turned)
        field[spot(0), :] += jnp.where(in_image(0, window), result[:EDGE], 0.0)
        outs[0][:, cols(window)] = field[out]

    yield
    out_row = lax.broadcasted_iota(jnp.int32, (4 * COUNT, wide), 0) % COUNT
    mixed = (plain, plain_ref[...]) if side == 0 else (plain_ref[...], plain)
    mixed = jnp.where(out_row < half, *mixed)
    results = [forward_edge(fields[0, window, spot(1, RADIUS, GROUP), :], window, mixed) for window in each]
    for window in each:
        field = fields.at[1, window]
        if side == 0:
            field[:24] = jnp.zeros((24, LANES), jnp.float32)
        else:
            field[40:] = jnp.zeros((32, LANES), jnp.float32)
        field[near] = early[window][1][own]
        field[spot(1), :] = results[window][:EDGE]
        outs[1][:, cols(window)] = field[out]

    yield
    in_row = lanes_of((4 * COUNT, wide)) % GROUP
    if side == 0:
        mixed = jnp.where(in_row < half, turned, turned_ref[...])
    else:
        mixed = jnp.where(in_row < EDGE, turned_ref[...], turned)
    for window in each:
        result = adjoint_edge(fields[1, window, spot(2, RADIUS, GROUP), :], window, mixed)
        field = fields.at[2, window]
        if side == 0:
            field[8:24] = jnp.zeros((16, LANES), jnp.float32)
        else:
            field[40:56] = jnp.zeros((16, LANES), jnp.float32)
        field[near] = early[window][2][own]
        field[spot(2), :] = jnp.where(in_image(2, window), result[:EDGE], 0.0)
        outs[2][:, cols(window)] = field[out]

    yield
    results = [forward_edge(fields[2, window, spot(3, RADIUS, GROUP), :], window, plain_ref[...]) for window in each]
    for window in each:
        rest = COUNT - EDGE
        if side == 0:
            outs[3][EDGE:, cols(window)] = early[window][3][EDGE:COUNT]
            outs[3][:EDGE, cols(window)] = results[window][:EDGE]
        else:
            outs[3][:rest, cols(window)] = early[window][3][TILE - COUNT : TILE - EDGE]
            outs[3][rest:, cols(window)] = results[window][:EDGE]
    yield


INNER = slice(COUNT, TILE - COUNT)


def record_of(values, position):
    lane = lanes_of((1, LANES))
    bounds = ((24, 108), (20, 108), (20, 104))

    def total(pieces):
        sums = [
            jnp.where((lane >= low) & (lane < high), jnp.sum(piece, axis=0, keepdims=True), 0.0)
            for piece, (low, high) in zip(pieces, bounds)
        ]
        return jnp.sum(sums[0] + sums[1] + sums[2], axis=1, keepdims=True)

    def best(first, second):
        size = total([b * b for b in second])
        cross = total([a * b for a, b in zip(first, second)])
        ratio = jnp.where(size > 0.0, cross / jnp.where(size > 0.0, size, 1.0), 0.0)
        rest = total([(a - ratio * b) ** 2 for a, b in zip(first, second)])
        return total([a * a for a in first]), size, ratio, rest

    grad, image, grad2, image2 = values
    line = jnp.zeros((1, LANES), jnp.float32)
    for index, value in enumerate(best(grad, grad2) + best(image, image2)):
        line = jnp.where(lane == position + index, value, line)
    return line


def edge_kernel(*refs):
    early = [refs[4 * window : 4 * window + 4] for window in (1, 0, 2)]
    two_ref, one_ref, plain_ref, turned_ref, inner_ref = refs[12:17]
    tops, lows, record_ref, edge, fields = refs[17:21], refs[21:25], *refs[25:]
    odd = is_odd("rng")
    one, two = one_ref[...], two_ref[...]
    has_above = lax.axis_index("rng") > 0
    has_below = lax.axis_index("rng") < lax.axis_size("rng") - 1
    above = jnp.where(has_above, jnp.where(odd, one, two), 0.0)
    below = jnp.where(has_below, jnp.where(odd, two, one), 0.0)
    row = lax.broadcasted_iota(jnp.int32, (8, LANES), 0)
    taps = jnp.where(row < 4, above[:8, :LANES], below[HALO - 8 :, :LANES])
    turned, plain = row_weights(taps, range(8), True), row_weights(taps, range(8), False)
    (turned, turned_low), (plain, plain_low) = [
        [jnp.concatenate(weights[side : side + 4], axis=0) for side in (0, 4)] for weights in (turned, plain)
    ]
    top = edge_rows(0, above, plain, turned, plain_ref, turned_ref, early, tops, edge.at[0], fields.at[0])
    low = edge_rows(1, below, plain_low, turned_low, plain_ref, turned_ref, early, lows, edge.at[1], fields.at[1])
    for _ in zip(top, low):
        pass

    def windows(i):
        both = jnp.concatenate([tops[i][...], lows[i][...]], axis=0)
        return [both[:, w * LANES : (w + 1) * LANES] for w in range(WINDOWS)]

    line = inner_ref[:1] + record_of([windows(i) for i in range(4)], 8)
    record_ref[...] = jnp.broadcast_to(line[None], record_ref.shape)


def combine_kernel(records_ref, block_ref, *refs):
    early = [refs[4 * window : 4 * window + 4] for window in (1, 0, 2)]
    tops, lows, (estimate_ref, residual_ref) = refs[12:16], refs[16:20], refs[20:]
    records = records_ref[:, 0, :]
    lane = lanes_of((1, LANES))

    def total(value, place):
        wanted = (lane % 8 == place) & (lane < 24)
        return jnp.sum(jnp.where(wanted, jnp.sum(value, axis=0, keepdims=True), 0.0), axis=1, keepdims=True)

    gamma = total(records, 0)
    delta = total(records, 4)
    alpha = gamma / delta
    apart = records + (alpha - pltpu.roll(records, 1, 1)) ** 2 * pltpu.roll(records, 2, 1)
    gamma_new = total(apart, 3)
    bent = total(apart, 7)
    factor = gamma_new / gamma
    delta_new = bent - factor * factor * delta
    alpha_new = gamma_new / delta_new
    first = alpha + alpha_new * (1.0 + factor)
    second = -alpha_new * alpha

    def own(a, b):
        parts = [first * a[w] + second * b[w] for w in range(WINDOWS)]
        lanes = lanes_of(parts[0].shape)
        middle = pltpu.roll(parts[1], 64, 1)
        left = jnp.where(lanes < 84, pltpu.roll(parts[0], LANES - HALO, 1), middle)
        right = jnp.where(lanes < 44, middle, pltpu.roll(parts[2], HALO, 1))
        return left, right

    def windows(ref):
        return [ref[:, w * LANES : (w + 1) * LANES] for w in range(WINDOWS)]

    for rows, pieces in (
        (slice(0, COUNT), lambda i: windows(tops[i])),
        (INNER, lambda i: [early[w][i][slice(8 + COUNT, 8 + TILE - COUNT) if i == 0 else INNER] for w in range(WINDOWS)]),
        (slice(TILE - COUNT, TILE), lambda i: windows(lows[i])),
    ):
        left, right = own(pieces(0), pieces(2))
        estimate_ref[rows, :LANES] = left
        estimate_ref[rows, LANES:] = right
        left, right = own(pieces(1), pieces(3))
        residual_ref[rows, :LANES] = block_ref[rows, :LANES] - left
        residual_ref[rows, LANES:] = block_ref[rows, LANES:] - right


def partners(axis, other):
    count, across = lax.axis_size(axis), lax.axis_size(other)

    def number(i, j):
        return i * across + j if axis == "rng" else j * count + i

    near, far = [], []
    for i in range(count):
        for j in range(across):
            near.append((number(i, j), number(i ^ 1, j)))
            beside = i + 1 if i % 2 else i - 1
            far.append((number(i, j), number(beside, j) if 0 <= beside < count else number(i, j ^ 1)))
    return near, far


BOTH = ("rng", "azi")


def body(observed, psf_tiles):
    devices = lax.axis_size("rng") * lax.axis_size("azi")
    wide = WINDOWS * LANES
    block, own, far, near = call(
        load_kernel,
        [f32(TILE, 2 * LANES), f32(8, LANES), f32(40, LANES), f32(40, LANES)],
        [pltpu.VMEM((1, 2, TAPS), jnp.float32), pltpu.SemaphoreType.DMA((CHUNKS + 1,))],
        inputs=[pl.BlockSpec(memory_space=pltpu.HBM)] * 2,
    )(
        pltpu.with_memory_space_constraint(observed, pltpu.HBM),
        pltpu.with_memory_space_constraint(psf_tiles, pltpu.HBM),
    )
    near_pairs, far_pairs = partners("azi", "rng")
    far = lax.ppermute(far, BOTH, far_pairs)
    near = lax.ppermute(near, BOTH, near_pairs)
    early = [f32(MAIN, LANES)] + [f32(TILE, LANES)] * 3
    rest = [jax.ShapeDtypeStruct((SLOTS * REST, 2 * LANES), jnp.bfloat16)] * 4

    def scratch(windows):
        return [
            pltpu.VMEM((windows, 4, 2, ROWS, LANES), jnp.float32),
            pltpu.VMEM((windows, 4, MAIN + 8, LANES), jnp.float32),
        ]

    *middle, high0, low0, high2, low2 = call(
        middle_kernel, early + rest, [pltpu.VMEM((DEPTH, 2 * LANES), jnp.bfloat16)] * 2 + scratch(1), limit=8
    )(block, own)
    taps, two, one = call(
        rows_kernel,
        [f32(8, LANES), f32(HALO, wide), f32(HALO, wide)],
        [pltpu.VMEM((HALO, wide), jnp.float32)] * 2,
    )(block, own, far, near, middle[0])
    one_pairs, two_pairs = partners("rng", "azi")
    two = lax.ppermute(two, BOTH, two_pairs)
    one = lax.ppermute(one, BOTH, one_pairs)
    *sides, plain, turned, inner = call(
        sides_kernel,
        early * 2 + [f32(4 * COUNT, wide)] * 2 + [f32(8, LANES)],
        [pltpu.VMEM((2, 2, SLOTS * PATCH, 2 * LANES), jnp.bfloat16)] + scratch(2),
        limit=8,
    )(block, far, near, taps, high0, low0, high2, low2, *middle)
    *edges, record = call(
        edge_kernel,
        [f32(COUNT, wide)] * 8 + [f32(devices, 1, LANES)],
        [pltpu.VMEM((2, 40, wide), jnp.float32), pltpu.VMEM((2, 3, WINDOWS, 72, LANES), jnp.float32)],
        limit=8,
    )(*middle, *sides, two, one, plain, turned, inner)
    records = lax.all_to_all(record, BOTH, 0, 0, tiled=True)
    estimate, residual = call(combine_kernel, [f32(TILE, 2 * LANES)] * 2)(
        records, block, *middle, *sides, *edges
    )
    return estimate, residual


def solution(mesh):
    return jax.shard_map(
        body,
        mesh=mesh,
        in_specs=(P("rng", "azi"), P("rng", "azi", None)),
        out_specs=(P("rng", "azi"), P("rng", "azi")),
        check_vma=False,
    )
```

```python
import jax
import jax.numpy as jnp
from jax import lax
from jax.experimental import pallas as pl
from jax.experimental.pallas import tpu as pltpu
from jax.sharding import PartitionSpec as P

TILE = 128
KSIZE = 11
RADIUS = 5
TAPS = KSIZE * KSIZE
LANES = 128
HALO = 24
REACH = 20
WINDOWS = 3
ROWS = TILE + 2 * HALO
SLOTS = (KSIZE + 1) // 2
DEPTH = SLOTS * LANES
MAIN = 144
REGIONS = ((0, 1, 24), (1, 2, 64), (2, 3, 104))
VMEM = pl.BlockSpec(memory_space=pltpu.VMEM)


def call(kernel, out_shape, scratch=(), limit=4, inputs=None):
    given = {} if inputs is None else {"in_specs": inputs}
    return pl.pallas_call(
        kernel,
        out_shape=out_shape,
        out_specs=[VMEM] * len(out_shape),
        **given,
        scratch_shapes=list(scratch),
        compiler_params=pltpu.CompilerParams(vmem_limit_bytes=limit * 2**20),
    )


def f32(*shape):
    return jax.ShapeDtypeStruct(shape, jnp.float32)


def lanes_of(shape):
    return lax.broadcasted_iota(jnp.int32, shape, len(shape) - 1)


def is_odd(axis):
    return lax.axis_index(axis) % 2 == 1


CHUNKS = 4


def load_kernel(observed_ref, psf_ref, block_ref, taps_ref, far_ref, near_ref, psf, sems):
    part = TILE // CHUNKS
    loads = [
        pltpu.make_async_copy(observed_ref.at[pl.ds(part * i, part)], block_ref.at[pl.ds(part * i, part)], sems.at[i])
        for i in range(CHUNKS)
    ]
    loads.append(pltpu.make_async_copy(psf_ref, psf, sems.at[CHUNKS]))
    for load in loads:
        load.start()
    taps_ref[...] = jnp.zeros((8, LANES), jnp.float32)
    for load in loads:
        load.wait()
    taps_ref[1:2, :TAPS] = psf[0, 0:1, :]
    taps_ref[2:3, :TAPS] = psf[0, 1:2, :]
    columns_kernel(block_ref, taps_ref, far_ref, near_ref)


def columns_kernel(block_ref, taps_ref, far_ref, near_ref):
    lane = lanes_of((32, LANES))

    def packed(side, first):
        out = jnp.zeros((32, LANES), jnp.float32)
        for part in range(4):
            rows = block_ref[32 * part : 32 * part + 32, LANES * side : LANES * side + LANES]
            moved = pltpu.roll(rows, (32 * part - first) % LANES, 1)
            out = jnp.where((lane >= 32 * part) & (lane < 32 * part + HALO), moved, out)
        return out

    left, right = packed(0, 0), packed(1, LANES - HALO)
    odd = is_odd("azi")
    near_ref[:32] = jnp.where(odd, left, right)
    far_ref[:32] = jnp.where(odd, right, left)
    first, second = taps_ref[...], pltpu.roll(taps_ref[...], 7, 0)
    near_ref[32:] = jnp.where(odd, first, second)
    far_ref[32:] = jnp.where(odd, second, first)


def side_halos(near_ref, far_ref):
    odd = is_odd("azi")
    near, far = near_ref[:32], far_ref[:32]
    has_left = lax.axis_index("azi") > 0
    has_right = lax.axis_index("azi") < lax.axis_size("azi") - 1
    return jnp.where(has_left, jnp.where(odd, near, far), 0.0), jnp.where(has_right, jnp.where(odd, far, near), 0.0)


def side_windows(block_ref, halos, part):
    rows = slice(32 * part, 32 * part + 32)
    lane = lanes_of((32, LANES))
    left = pltpu.roll(halos[0], (-32 * part) % LANES, 1)
    right = pltpu.roll(halos[1], (LANES - HALO - 32 * part) % LANES, 1)
    first = jnp.where(lane < HALO, left, pltpu.roll(block_ref[rows, :LANES], HALO, 1))
    second = jnp.where(lane < LANES - HALO, pltpu.roll(block_ref[rows, LANES:], LANES - HALO, 1), right)
    return first, second


def rows_kernel(own_ref, far_ref, near_ref, ends_ref, taps_ref, two_ref, one_ref, top, low):
    halos = side_halos(near_ref, far_ref)
    odd = is_odd("azi")
    has_left = lax.axis_index("azi") > 0
    has_right = lax.axis_index("azi") < lax.axis_size("azi") - 1
    near_taps, far_taps = near_ref[33:34], far_ref[33:34]
    taps_ref[...] = own_ref[...]
    taps_ref[0:1] = jnp.where(has_left, jnp.where(odd, near_taps, far_taps), 0.0)
    taps_ref[3:4] = jnp.where(has_right, jnp.where(odd, far_taps, near_taps), 0.0)
    lane = lanes_of((HALO, LANES))
    for ref, part, inner, ends in ((top, 0, slice(0, HALO), slice(0, HALO)), (low, 3, slice(8, 32), slice(HALO, 2 * HALO))):
        left = pltpu.roll(halos[0][inner], (-32 * part) % LANES, 1)
        right = pltpu.roll(halos[1][inner], (LANES - HALO - 32 * part) % LANES, 1)
        ref[:, :LANES] = jnp.where(lane < HALO, left, ends_ref[ends, :LANES])
        ref[:, LANES : 2 * LANES] = ends_ref[ends, LANES : 2 * LANES]
        ref[:, 2 * LANES :] = jnp.where(lane < LANES - HALO, ends_ref[ends, 2 * LANES :], right)
    top[REACH:, :LANES] = taps_ref[0:4]
    low[: HALO - REACH, :LANES] = taps_ref[0:4]
    odd_row = is_odd("rng")
    one_ref[...] = jnp.where(odd_row, top[...], low[...])
    two_ref[...] = jnp.where(odd_row, low[...], top[...])


def middle_window(first, second):
    lane = lanes_of(first.shape)
    return jnp.where(lane < 64, pltpu.roll(first, 64, 1), pltpu.roll(second, 64, 1))


def split(value):
    high = value.astype(jnp.bfloat16)
    return high, (value - high.astype(jnp.float32)).astype(jnp.bfloat16)


def product(parts, high, low, dims):
    rows = parts[0].shape[0]

    def dot(a, b):
        return lax.dot_general(a, b, (dims, ((), ())), preferred_element_type=jnp.float32)

    both = dot(jnp.concatenate(parts, axis=0), high)
    return both[:rows] + both[rows:] + dot(parts[0], low)


def put_parts(field_ref, rows, value):
    high = value.astype(jnp.bfloat16).astype(jnp.float32)
    field_ref[0, rows] = high
    field_ref[1, rows] = value - high


def stacked_rows(field_ref, first, count, offsets):
    return [
        jnp.concatenate(
            [field_ref[part, pl.ds(HALO + first + offset, count), :].astype(jnp.bfloat16) for offset in offsets],
            axis=1,
        )
        for part in range(2)
    ]


def adjoint_rows(field_ref, block, pair, first, count, lead):
    offsets = [RADIUS - 2 * slot for slot in range(SLOTS)]
    parts = stacked_rows(field_ref, first - lead, count + lead, offsets)
    high, low = [jnp.concatenate([block(part, slot) for slot in range(SLOTS)], axis=0) for part in range(2)]
    both = product(parts, high, low, ((1,), (0,)))
    if lead == 0:
        pair[:8, :] = jnp.zeros((8, LANES), jnp.float32)
    pair[pl.ds(8 if lead == 0 else 0, count + lead), :] = both[:, LANES:]
    return both[lead:, :LANES] + pair[pl.ds(7 if lead == 0 else lead - 1, count), :]


def forward_rows(field_ref, block, pair, first, count):
    offsets = [2 * slot - RADIUS for slot in range(SLOTS)]
    parts = stacked_rows(field_ref, first, count + 16, offsets)

    def turned(part):
        blocks = [block(part, slot) for slot in range(SLOTS)]
        halves = [
            jnp.concatenate([value[:, half * LANES : (half + 1) * LANES] for value in blocks], axis=1)
            for half in range(2)
        ]
        return jnp.concatenate(halves, axis=0)

    both = product(parts, turned(0), turned(1), ((1,), (1,)))
    pair[: count + 16, :] = both[:, LANES:]
    return both[:count, :LANES] + pair[pl.ds(1, count), :]


def tap_lines(taps):
    spot = (lanes_of((8, LANES)) + RADIUS) % LANES
    return [
        jnp.where(spot < KSIZE, jnp.take_along_axis(taps, jnp.minimum(KSIZE * u + spot, LANES - 1), axis=1), 0.0)
        for u in range(KSIZE)
    ]


def put_band(lines, offset, window, first, count, refs):
    slot, half = offset // 2, offset % 2
    place = (slice(slot * count, (slot + 1) * count), slice(half * LANES, (half + 1) * LANES))
    if offset >= KSIZE:
        for ref in refs:
            ref[place] = jnp.zeros((count, LANES), jnp.bfloat16)
        return
    before, after, bound = REGIONS[window]
    row = first + lax.broadcasted_iota(jnp.int32, (count, LANES), 0)
    left, right = [jnp.broadcast_to(lines[offset][tile : tile + 1], (count, LANES)) for tile in (before, after)]
    base = left if first + count <= bound else right if first >= bound else jnp.where(row < bound, left, right)
    refs[0][place], refs[1][place] = split(pltpu.roll(base, first, 1, stride=1, stride_axis=0))


def inside(window):
    lane = lanes_of((1, LANES))
    if window == 0:
        return (lane >= HALO) | (lax.axis_index("azi") > 0)
    if window == 2:
        return (lane < LANES - HALO) | (lax.axis_index("azi") < lax.axis_size("azi") - 1)
    return lane >= 0


def early_rows(rows, windows, blocks, outs, fields, pairs, between=lambda stage: None):
    own = slice(HALO, HALO + TILE)
    most, fewer = slice(8, TILE - 8), slice(16, TILE - 16)
    each = range(len(windows))
    keep = [inside(window) for window in windows]
    for i in each:
        for stage in range(4):
            for part in range(2):
                fields[i, stage, part, : HALO + 8] = jnp.zeros((HALO + 8, LANES), jnp.float32)
                fields[i, stage, part, HALO + TILE - 8 :] = jnp.zeros((HALO + 8, LANES), jnp.float32)
        put_parts(fields.at[i, 0], own, rows[i])
    for i in each:
        main = adjoint_rows(fields.at[i, 0], blocks[i], pairs.at[i, 0], -8, MAIN, 0)
        main = jnp.where(keep[i], main, 0.0)
        outs[i][0][...] = main
        put_parts(fields.at[i, 1], slice(HALO - 8, HALO + TILE + 8), main)
    between(0)
    for i in each:
        image = forward_rows(fields.at[i, 1], blocks[i], pairs.at[i, 1], most.start, TILE - 16)
        outs[i][1][most] = image
        put_parts(fields.at[i, 2], slice(HALO + most.start, HALO + most.stop), image)
    between(1)
    for i in each:
        grad = adjoint_rows(fields.at[i, 2], blocks[i], pairs.at[i, 2], most.start, TILE - 16, 16)
        grad = jnp.where(keep[i], grad, 0.0)
        outs[i][2][most] = grad
        put_parts(fields.at[i, 3], slice(HALO + most.start, HALO + most.stop), grad)
    between(2)
    for i in each:
        outs[i][3][fewer] = forward_rows(fields.at[i, 3], blocks[i], pairs.at[i, 3], fewer.start, TILE - 32)
    between(3)


PATCH = 32
REST = LANES - PATCH


def middle_kernel(block_ref, taps_ref, *refs):
    outs, sides, ends_ref = refs[:4], (refs[4:6], refs[6:8]), refs[8]
    high, low, fields, pairs = refs[9:]
    for side, ends in enumerate((slice(0, HALO), slice(TILE - HALO, TILE))):
        first, second = block_ref[ends, :LANES], block_ref[ends, LANES:]
        place = slice(HALO * side, HALO * side + HALO)
        ends_ref[place, :LANES] = pltpu.roll(first, HALO, 1)
        ends_ref[place, LANES : 2 * LANES] = middle_window(first, second)
        ends_ref[place, 2 * LANES :] = pltpu.roll(second, LANES - HALO, 1)
    lines = tap_lines(taps_ref[...])
    for offset in range(2 * SLOTS):
        put_band(lines, offset, 1, 0, LANES, (high, low))

    def between(stage):
        for offset in range(3 * stage, 3 * stage + 3):
            put_band(lines, offset, 0, PATCH, REST, sides[0])
            put_band(lines, offset, 2, 0, REST, sides[1])

    def block(part, slot):
        return (high, low)[part][slot * LANES : (slot + 1) * LANES, :]

    rows = middle_window(block_ref[:, :LANES], block_ref[:, LANES:])
    early_rows([rows], (1,), [block], [outs], fields, pairs, between)


def sides_kernel(block_ref, far_ref, near_ref, taps_ref, *refs):
    rest, middle = (refs[:2], refs[2:4]), refs[4:8]
    outs, refs = (refs[8:12], refs[12:16]), refs[16:]
    plain_ref, turned_ref, inner_ref, patches, fields, pairs = refs
    taps = taps_ref[...]
    lines = tap_lines(taps)
    for offset in range(2 * SLOTS):
        put_band(lines, offset, 0, 0, PATCH, (patches.at[0, 0], patches.at[0, 1]))
        put_band(lines, offset, 2, REST, PATCH, (patches.at[1, 0], patches.at[1, 1]))

    def piece(side, part, slot):
        whole = rest[side][part][slot * REST : (slot + 1) * REST, :]
        patch = patches[side, part, slot * PATCH : (slot + 1) * PATCH, :]
        return jnp.concatenate([patch, whole] if side == 0 else [whole, patch], axis=0)

    blocks = [lambda part, slot: piece(0, part, slot), lambda part, slot: piece(1, part, slot)]

    def between(stage):
        if stage == 0:
            plain_ref[...] = jnp.concatenate(row_weights(taps, range(4), False), axis=0)
        if stage == 1:
            turned_ref[...] = jnp.concatenate(row_weights(taps, range(4), True), axis=0)

    halos = side_halos(near_ref, far_ref)
    parts = [side_windows(block_ref, halos, part) for part in range(4)]
    rows = [jnp.concatenate([part[side] for part in parts], axis=0) for side in range(2)]
    early_rows(rows, (0, 2), blocks, outs, fields, pairs, between)
    early = (outs[0], middle, outs[1])
    inner = [[window[0][8 + INNER.start : 8 + INNER.stop] for window in early]]
    inner += [[window[i][INNER] for window in early] for i in range(1, 4)]
    inner_ref[...] = jnp.broadcast_to(record_of(inner, 0), (8, LANES))


GROUP = 32
GROUPS = 3 * LANES // GROUP
EDGE = 4 * RADIUS
COUNT = 24


def row_weights(taps, tiles, turned):
    lane = lanes_of((8, LANES))
    pieces = [[] for _ in tiles]
    for part in range(3):
        u = lane % GROUP
        if turned:
            u = KSIZE - 1 - u
        v = part * (LANES // GROUP) + lane // GROUP
        base = jnp.take_along_axis(taps, jnp.clip(u * KSIZE + v, 0, LANES - 1), axis=1)
        base = jnp.where((u >= 0) & (u < KSIZE) & (v < KSIZE), base, 0.0)
        for piece, tile in zip(pieces, tiles):
            row = jnp.broadcast_to(base[tile : tile + 1], (COUNT, LANES))
            piece.append(pltpu.roll(row, 0, 1, stride=1, stride_axis=0))
    return [jnp.concatenate(piece, axis=1) for piece in pieces]


def spread(rows, sign):
    moved = [rows if v == RADIUS else pltpu.roll(rows, (sign * (v - RADIUS)) % LANES, 1) for v in range(KSIZE)]
    moved.append(jnp.zeros((GROUP * (GROUPS - KSIZE), LANES), rows.dtype))
    return jnp.concatenate(moved, axis=0)


def forward_edge(rows, window, weights):
    before, after, bound = REGIONS[window]
    high, low = [spread(part, -1)[: GROUP * KSIZE] for part in split(rows)]
    both = [weights[COUNT * tile : COUNT * tile + COUNT] for tile in (before, after)]
    result = product(split(jnp.concatenate(both, axis=0)[:, : GROUP * KSIZE]), high, low, ((1,), (0,)))
    return jnp.where(lanes_of((COUNT, LANES)) < bound, result[:COUNT], result[COUNT:])


def adjoint_edge(rows, window, weights):
    before, after, bound = REGIONS[window]
    lane = lanes_of((GROUP, LANES))
    whole = [spread(part, 1) for part in split(rows)]
    high, low = [
        jnp.concatenate(
            [part]
            + [
                jnp.where(lane < bound + v - RADIUS, moved, jnp.zeros_like(moved))
                for v, moved in enumerate(part[GROUP * v : GROUP * v + GROUP] for v in range(KSIZE))
            ]
            + [part[GROUP * KSIZE :]],
            axis=0,
        )
        for part in whole
    ]
    left, right = [weights[COUNT * tile : COUNT * tile + COUNT] for tile in (before, after)]
    return product(split(jnp.concatenate([right, left - right], axis=1)), high, low, ((1,), (0,)))


def edge_rows(side, message, plain, turned, plain_ref, turned_ref, early, outs, edge, fields):
    wide = WINDOWS * LANES
    each = range(WINDOWS)
    base = 16 if side == 0 else -80
    near = slice(24, 64) if side == 0 else slice(0, 40)
    own = slice(8, 48) if side == 0 else slice(80, 120)
    out = slice(16, 40) if side == 0 else slice(24, 48)
    start = (-15, -10, -5, 0) if side == 0 else (123, 118, 113, 108)
    beyond = lax.axis_index("rng") > 0 if side == 0 else lax.axis_index("rng") < lax.axis_size("rng") - 1
    keep = [inside(window) for window in each]
    row = lax.broadcasted_iota(jnp.int32, (EDGE, LANES), 0)
    half = EDGE // 2

    def cols(window):
        return pl.ds(window * LANES, LANES)

    def spot(stage, reach=0, count=EDGE):
        return pl.ds(start[stage] - reach + base, count)

    def in_image(stage, window):
        inner = row >= -start[stage] if side == 0 else row < TILE - start[stage]
        return keep[window] & (beyond | inner)

    row24 = lax.broadcasted_iota(jnp.int32, (HALO, 1), 0)
    if side == 0:
        edge[:HALO] = jnp.where(row24 < HALO - REACH, 0.0, message)
        edge[HALO:] = jnp.zeros((16, wide), jnp.float32)
        strip = slice(4, 36)
    else:
        edge[:16] = jnp.zeros((16, wide), jnp.float32)
        edge[16:] = jnp.where(row24 >= REACH, 0.0, message)
        strip = slice(6, 38)
    for window in each:
        main = early[window][0]
        field = fields.at[0, window]
        if side == 0:
            field[:8] = jnp.zeros((8, LANES), jnp.float32)
            field[8:16] = jnp.where(beyond, main[:8], 0.0)
            field[16:64] = main[8:56]
        else:
            field[:48] = main[88:136]
            field[48:56] = jnp.where(beyond, main[136:], 0.0)
            field[56:] = jnp.zeros((16, LANES), jnp.float32)
        result = adjoint_edge(edge[strip, cols(window)], window, turned)
        field[spot(0), :] += jnp.where(in_image(0, window), result[:EDGE], 0.0)
        outs[0][:, cols(window)] = field[out]

    yield
    out_row = lax.broadcasted_iota(jnp.int32, (4 * COUNT, wide), 0) % COUNT
    mixed = (plain, plain_ref[...]) if side == 0 else (plain_ref[...], plain)
    mixed = jnp.where(out_row < half, *mixed)
    results = [forward_edge(fields[0, window, spot(1, RADIUS, GROUP), :], window, mixed) for window in each]
    for window in each:
        field = fields.at[1, window]
        if side == 0:
            field[:24] = jnp.zeros((24, LANES), jnp.float32)
        else:
            field[40:] = jnp.zeros((32, LANES), jnp.float32)
        field[near] = early[window][1][own]
        field[spot(1), :] = results[window][:EDGE]
        outs[1][:, cols(window)] = field[out]

    yield
    in_row = lanes_of((4 * COUNT, wide)) % GROUP
    if side == 0:
        mixed = jnp.where(in_row < half, turned, turned_ref[...])
    else:
        mixed = jnp.where(in_row < EDGE, turned_ref[...], turned)
    for window in each:
        result = adjoint_edge(fields[1, window, spot(2, RADIUS, GROUP), :], window, mixed)
        field = fields.at[2, window]
        if side == 0:
            field[8:24] = jnp.zeros((16, LANES), jnp.float32)
        else:
            field[40:56] = jnp.zeros((16, LANES), jnp.float32)
        field[near] = early[window][2][own]
        field[spot(2), :] = jnp.where(in_image(2, window), result[:EDGE], 0.0)
        outs[2][:, cols(window)] = field[out]

    yield
    results = [forward_edge(fields[2, window, spot(3, RADIUS, GROUP), :], window, plain_ref[...]) for window in each]
    for window in each:
        rest = COUNT - EDGE
        if side == 0:
            outs[3][EDGE:, cols(window)] = early[window][3][EDGE:COUNT]
            outs[3][:EDGE, cols(window)] = results[window][:EDGE]
        else:
            outs[3][:rest, cols(window)] = early[window][3][TILE - COUNT : TILE - EDGE]
            outs[3][rest:, cols(window)] = results[window][:EDGE]
    yield


INNER = slice(COUNT, TILE - COUNT)


def record_of(values, position):
    lane = lanes_of((1, LANES))
    bounds = ((24, 108), (20, 108), (20, 104))

    def total(pieces):
        sums = [
            jnp.where((lane >= low) & (lane < high), jnp.sum(piece, axis=0, keepdims=True), 0.0)
            for piece, (low, high) in zip(pieces, bounds)
        ]
        return jnp.broadcast_to(jnp.sum(sums[0] + sums[1] + sums[2], axis=1, keepdims=True), (1, LANES))

    def best(first, second):
        size = total([b * b for b in second])
        cross = total([a * b for a, b in zip(first, second)])
        ratio = jnp.where(size > 0.0, cross / jnp.where(size > 0.0, size, 1.0), 0.0)
        rest = total([(a - ratio * b) ** 2 for a, b in zip(first, second)])
        return total([a * a for a in first]), size, ratio, rest

    grad, image, grad2, image2 = values
    line = jnp.zeros((1, LANES), jnp.float32)
    for index, value in enumerate(best(grad, grad2) + best(image, image2)):
        line = jnp.where(lane == position + index, value, line)
    return line


def edge_kernel(*refs):
    early = [refs[4 * window : 4 * window + 4] for window in (1, 0, 2)]
    two_ref, one_ref, plain_ref, turned_ref, inner_ref = refs[12:17]
    tops, lows, record_ref, edge, fields = refs[17:21], refs[21:25], *refs[25:]
    odd = is_odd("rng")
    one, two = one_ref[...], two_ref[...]
    has_above = lax.axis_index("rng") > 0
    has_below = lax.axis_index("rng") < lax.axis_size("rng") - 1
    above = jnp.where(has_above, jnp.where(odd, one, two), 0.0)
    below = jnp.where(has_below, jnp.where(odd, two, one), 0.0)
    row = lax.broadcasted_iota(jnp.int32, (8, LANES), 0)
    taps = jnp.where(row < 4, above[:8, :LANES], below[HALO - 8 :, :LANES])
    turned, plain = row_weights(taps, range(8), True), row_weights(taps, range(8), False)
    (turned, turned_low), (plain, plain_low) = [
        [jnp.concatenate(weights[side : side + 4], axis=0) for side in (0, 4)] for weights in (turned, plain)
    ]
    top = edge_rows(0, above, plain, turned, plain_ref, turned_ref, early, tops, edge.at[0], fields.at[0])
    low = edge_rows(1, below, plain_low, turned_low, plain_ref, turned_ref, early, lows, edge.at[1], fields.at[1])
    for _ in zip(top, low):
        pass

    def windows(i):
        both = jnp.concatenate([tops[i][...], lows[i][...]], axis=0)
        return [both[:, w * LANES : (w + 1) * LANES] for w in range(WINDOWS)]

    line = inner_ref[:1] + record_of([windows(i) for i in range(4)], 8)
    record_ref[...] = jnp.broadcast_to(line[None], record_ref.shape)


def combine_kernel(records_ref, block_ref, *refs):
    early = [refs[4 * window : 4 * window + 4] for window in (1, 0, 2)]
    tops, lows, (estimate_ref, residual_ref) = refs[12:16], refs[16:20], refs[20:]
    records = records_ref[:, 0, :]
    lane = lanes_of((1, LANES))

    def total(value, place):
        wanted = (lane % 8 == place) & (lane < 24)
        one = jnp.sum(jnp.where(wanted, jnp.sum(value, axis=0, keepdims=True), 0.0), axis=1, keepdims=True)
        return jnp.broadcast_to(one, (1, LANES))

    gamma = total(records, 0)
    delta = total(records, 4)
    alpha = gamma / delta
    apart = records + (alpha - pltpu.roll(records, 1, 1)) ** 2 * pltpu.roll(records, 2, 1)
    gamma_new = total(apart, 3)
    bent = total(apart, 7)
    factor = gamma_new / gamma
    delta_new = bent - factor * factor * delta
    alpha_new = gamma_new / delta_new
    first = alpha + alpha_new * (1.0 + factor)
    second = -alpha_new * alpha

    def own(a, b):
        parts = [first * a[w] + second * b[w] for w in range(WINDOWS)]
        lanes = lanes_of(parts[0].shape)
        middle = pltpu.roll(parts[1], 64, 1)
        left = jnp.where(lanes < 84, pltpu.roll(parts[0], LANES - HALO, 1), middle)
        right = jnp.where(lanes < 44, middle, pltpu.roll(parts[2], HALO, 1))
        return left, right

    def windows(ref):
        return [ref[:, w * LANES : (w + 1) * LANES] for w in range(WINDOWS)]

    for rows, pieces in (
        (slice(0, COUNT), lambda i: windows(tops[i])),
        (INNER, lambda i: [early[w][i][slice(8 + COUNT, 8 + TILE - COUNT) if i == 0 else INNER] for w in range(WINDOWS)]),
        (slice(TILE - COUNT, TILE), lambda i: windows(lows[i])),
    ):
        left, right = own(pieces(0), pieces(2))
        estimate_ref[rows, :LANES] = left
        estimate_ref[rows, LANES:] = right
        left, right = own(pieces(1), pieces(3))
        residual_ref[rows, :LANES] = block_ref[rows, :LANES] - left
        residual_ref[rows, LANES:] = block_ref[rows, LANES:] - right


def partners(axis, other):
    count, across = lax.axis_size(axis), lax.axis_size(other)

    def number(i, j):
        return i * across + j if axis == "rng" else j * count + i

    near, far = [], []
    for i in range(count):
        for j in range(across):
            near.append((number(i, j), number(i ^ 1, j)))
            beside = i + 1 if i % 2 else i - 1
            far.append((number(i, j), number(beside, j) if 0 <= beside < count else number(i, j ^ (1 if axis == "rng" else 2))))
    return near, far


BOTH = ("rng", "azi")


def body(observed, psf_tiles):
    devices = lax.axis_size("rng") * lax.axis_size("azi")
    wide = WINDOWS * LANES
    block, own, far, near = call(
        load_kernel,
        [f32(TILE, 2 * LANES), f32(8, LANES), f32(40, LANES), f32(40, LANES)],
        [pltpu.VMEM((1, 2, TAPS), jnp.float32), pltpu.SemaphoreType.DMA((CHUNKS + 1,))],
        inputs=[pl.BlockSpec(memory_space=pltpu.HBM)] * 2,
    )(
        pltpu.with_memory_space_constraint(observed, pltpu.HBM),
        pltpu.with_memory_space_constraint(psf_tiles, pltpu.HBM),
    )
    near_pairs, far_pairs = partners("azi", "rng")
    far = lax.ppermute(far, BOTH, far_pairs)
    near = lax.ppermute(near, BOTH, near_pairs)
    early = [f32(MAIN, LANES)] + [f32(TILE, LANES)] * 3
    rest = [jax.ShapeDtypeStruct((SLOTS * REST, 2 * LANES), jnp.bfloat16)] * 4

    def scratch(windows):
        return [
            pltpu.VMEM((windows, 4, 2, ROWS, LANES), jnp.float32),
            pltpu.VMEM((windows, 4, MAIN + 8, LANES), jnp.float32),
        ]

    *middle, high0, low0, high2, low2, ends = call(
        middle_kernel, early + rest + [f32(2 * HALO, wide)], [pltpu.VMEM((DEPTH, 2 * LANES), jnp.bfloat16)] * 2 + scratch(1), limit=8
    )(block, own)
    taps, two, one = call(
        rows_kernel,
        [f32(8, LANES), f32(HALO, wide), f32(HALO, wide)],
        [pltpu.VMEM((HALO, wide), jnp.float32)] * 2,
    )(own, far, near, ends)
    one_pairs, two_pairs = partners("rng", "azi")
    two = lax.ppermute(two, BOTH, two_pairs)
    one = lax.ppermute(one, BOTH, one_pairs)
    *sides, plain, turned, inner = call(
        sides_kernel,
        early * 2 + [f32(4 * COUNT, wide)] * 2 + [f32(8, LANES)],
        [pltpu.VMEM((2, 2, SLOTS * PATCH, 2 * LANES), jnp.bfloat16)] + scratch(2),
        limit=8,
    )(block, far, near, taps, high0, low0, high2, low2, *middle)
    *edges, record = call(
        edge_kernel,
        [f32(COUNT, wide)] * 8 + [f32(devices, 1, LANES)],
        [pltpu.VMEM((2, 40, wide), jnp.float32), pltpu.VMEM((2, 3, WINDOWS, 72, LANES), jnp.float32)],
        limit=8,
    )(*middle, *sides, two, one, plain, turned, inner)
    records = lax.all_to_all(record, BOTH, 0, 0, tiled=True)
    estimate, residual = call(combine_kernel, [f32(TILE, 2 * LANES)] * 2)(
        records, block, *middle, *sides, *edges
    )
    return estimate, residual


def solution(mesh):
    return jax.shard_map(
        body,
        mesh=mesh,
        in_specs=(P("rng", "azi"), P("rng", "azi", None)),
        out_specs=(P("rng", "azi"), P("rng", "azi")),
        check_vma=False,
    )
```

```python
import jax
import jax.numpy as jnp
from jax import lax
from jax.experimental import pallas as pl
from jax.experimental.pallas import tpu as pltpu
from jax.sharding import PartitionSpec as P

TILE = 128
KSIZE = 11
RADIUS = 5
TAPS = KSIZE * KSIZE
LANES = 128
HALO = 24
REACH = 20
WINDOWS = 3
ROWS = TILE + 2 * HALO
SLOTS = (KSIZE + 1) // 2
DEPTH = SLOTS * LANES
MAIN = 144
REGIONS = ((0, 1, 24), (1, 2, 64), (2, 3, 104))
VMEM = pl.BlockSpec(memory_space=pltpu.VMEM)


def call(kernel, out_shape, scratch=(), limit=4, inputs=None):
    given = {} if inputs is None else {"in_specs": inputs}
    return pl.pallas_call(
        kernel,
        out_shape=out_shape,
        out_specs=[VMEM] * len(out_shape),
        **given,
        scratch_shapes=list(scratch),
        compiler_params=pltpu.CompilerParams(vmem_limit_bytes=limit * 2**20),
    )


def f32(*shape):
    return jax.ShapeDtypeStruct(shape, jnp.float32)


def lanes_of(shape):
    return lax.broadcasted_iota(jnp.int32, shape, len(shape) - 1)


def is_odd(axis):
    return lax.axis_index(axis) % 2 == 1


CHUNKS = 4


def load_kernel(observed_ref, psf_ref, block_ref, taps_ref, far_ref, near_ref, psf, sems):
    part = TILE // CHUNKS
    loads = [
        pltpu.make_async_copy(observed_ref.at[pl.ds(part * i, part)], block_ref.at[pl.ds(part * i, part)], sems.at[i])
        for i in range(CHUNKS)
    ]
    loads.append(pltpu.make_async_copy(psf_ref, psf, sems.at[CHUNKS]))
    for load in loads:
        load.start()
    taps_ref[...] = jnp.zeros((8, LANES), jnp.float32)
    for load in loads:
        load.wait()
    taps_ref[1:2, :TAPS] = psf[0, 0:1, :]
    taps_ref[2:3, :TAPS] = psf[0, 1:2, :]
    columns_kernel(block_ref, taps_ref, far_ref, near_ref)


def columns_kernel(block_ref, taps_ref, far_ref, near_ref):
    lane = lanes_of((32, LANES))

    def packed(side, first):
        out = jnp.zeros((32, LANES), jnp.float32)
        for part in range(4):
            rows = block_ref[32 * part : 32 * part + 32, LANES * side : LANES * side + LANES]
            moved = pltpu.roll(rows, (32 * part - first) % LANES, 1)
            out = jnp.where((lane >= 32 * part) & (lane < 32 * part + HALO), moved, out)
        return out

    left, right = packed(0, 0), packed(1, LANES - HALO)
    odd = is_odd("azi")
    near_ref[:32] = jnp.where(odd, left, right)
    far_ref[:32] = jnp.where(odd, right, left)
    first, second = taps_ref[...], pltpu.roll(taps_ref[...], 7, 0)
    near_ref[32:] = jnp.where(odd, first, second)
    far_ref[32:] = jnp.where(odd, second, first)


def side_halos(near_ref, far_ref):
    odd = is_odd("azi")
    near, far = near_ref[:32], far_ref[:32]
    has_left = lax.axis_index("azi") > 0
    has_right = lax.axis_index("azi") < lax.axis_size("azi") - 1
    return jnp.where(has_left, jnp.where(odd, near, far), 0.0), jnp.where(has_right, jnp.where(odd, far, near), 0.0)


def side_windows(block_ref, halos, part):
    rows = slice(32 * part, 32 * part + 32)
    lane = lanes_of((32, LANES))
    left = pltpu.roll(halos[0], (-32 * part) % LANES, 1)
    right = pltpu.roll(halos[1], (LANES - HALO - 32 * part) % LANES, 1)
    first = jnp.where(lane < HALO, left, pltpu.roll(block_ref[rows, :LANES], HALO, 1))
    second = jnp.where(lane < LANES - HALO, pltpu.roll(block_ref[rows, LANES:], LANES - HALO, 1), right)
    return first, second


def rows_kernel(block_ref, own_ref, far_ref, near_ref, _, taps_ref, two_ref, one_ref, top, low):
    halos = side_halos(near_ref, far_ref)
    odd = is_odd("azi")
    has_left = lax.axis_index("azi") > 0
    has_right = lax.axis_index("azi") < lax.axis_size("azi") - 1
    near_taps, far_taps = near_ref[33:34], far_ref[33:34]
    taps_ref[...] = own_ref[...]
    taps_ref[0:1] = jnp.where(has_left, jnp.where(odd, near_taps, far_taps), 0.0)
    taps_ref[3:4] = jnp.where(has_right, jnp.where(odd, far_taps, near_taps), 0.0)
    for ref, part, rows in ((top, 0, slice(0, HALO)), (low, 3, slice(TILE - HALO, TILE))):
        inner = slice(0, HALO) if part == 0 else slice(8, 32)
        first, second = side_windows(block_ref, halos, part)
        ref[:, :LANES] = first[inner]
        ref[:, LANES : 2 * LANES] = middle_window(block_ref[rows, :LANES], block_ref[rows, LANES:])
        ref[:, 2 * LANES :] = second[inner]
    top[REACH:, :LANES] = taps_ref[0:4]
    low[: HALO - REACH, :LANES] = taps_ref[0:4]
    odd_row = is_odd("rng")
    one_ref[...] = jnp.where(odd_row, top[...], low[...])
    two_ref[...] = jnp.where(odd_row, low[...], top[...])


def middle_window(first, second):
    lane = lanes_of(first.shape)
    return jnp.where(lane < 64, pltpu.roll(first, 64, 1), pltpu.roll(second, 64, 1))


def split(value):
    high = value.astype(jnp.bfloat16)
    return high, (value - high.astype(jnp.float32)).astype(jnp.bfloat16)


def product(parts, high, low, dims):
    rows = parts[0].shape[0]

    def dot(a, b):
        return lax.dot_general(a, b, (dims, ((), ())), preferred_element_type=jnp.float32)

    both = dot(jnp.concatenate(parts, axis=0), high)
    return both[:rows] + both[rows:] + dot(parts[0], low)


def put_parts(field_ref, rows, value):
    high = value.astype(jnp.bfloat16).astype(jnp.float32)
    field_ref[0, rows] = high
    field_ref[1, rows] = value - high


def stacked_rows(field_ref, first, count, offsets):
    return [
        jnp.concatenate(
            [field_ref[part, pl.ds(HALO + first + offset, count), :].astype(jnp.bfloat16) for offset in offsets],
            axis=1,
        )
        for part in range(2)
    ]


def adjoint_rows(field_ref, block, pair, first, count, lead):
    offsets = [RADIUS - 2 * slot for slot in range(SLOTS)]
    parts = stacked_rows(field_ref, first - lead, count + lead, offsets)
    high, low = [jnp.concatenate([block(part, slot) for slot in range(SLOTS)], axis=0) for part in range(2)]
    both = product(parts, high, low, ((1,), (0,)))
    if lead == 0:
        pair[:8, :] = jnp.zeros((8, LANES), jnp.float32)
    pair[pl.ds(8 if lead == 0 else 0, count + lead), :] = both[:, LANES:]
    return both[lead:, :LANES] + pair[pl.ds(7 if lead == 0 else lead - 1, count), :]


def forward_rows(field_ref, block, pair, first, count):
    offsets = [2 * slot - RADIUS for slot in range(SLOTS)]
    parts = stacked_rows(field_ref, first, count + 16, offsets)

    def turned(part):
        blocks = [block(part, slot) for slot in range(SLOTS)]
        halves = [
            jnp.concatenate([value[:, half * LANES : (half + 1) * LANES] for value in blocks], axis=1)
            for half in range(2)
        ]
        return jnp.concatenate(halves, axis=0)

    both = product(parts, turned(0), turned(1), ((1,), (1,)))
    pair[: count + 16, :] = both[:, LANES:]
    return both[:count, :LANES] + pair[pl.ds(1, count), :]


def tap_lines(taps):
    spot = (lanes_of((8, LANES)) + RADIUS) % LANES
    return [
        jnp.where(spot < KSIZE, jnp.take_along_axis(taps, jnp.minimum(KSIZE * u + spot, LANES - 1), axis=1), 0.0)
        for u in range(KSIZE)
    ]


def put_band(lines, offset, window, first, count, refs):
    slot, half = offset // 2, offset % 2
    place = (slice(slot * count, (slot + 1) * count), slice(half * LANES, (half + 1) * LANES))
    if offset >= KSIZE:
        for ref in refs:
            ref[place] = jnp.zeros((count, LANES), jnp.bfloat16)
        return
    before, after, bound = REGIONS[window]
    row = first + lax.broadcasted_iota(jnp.int32, (count, LANES), 0)
    left, right = [jnp.broadcast_to(lines[offset][tile : tile + 1], (count, LANES)) for tile in (before, after)]
    base = left if first + count <= bound else right if first >= bound else jnp.where(row < bound, left, right)
    refs[0][place], refs[1][place] = split(pltpu.roll(base, first, 1, stride=1, stride_axis=0))


def inside(window):
    lane = lanes_of((1, LANES))
    if window == 0:
        return (lane >= HALO) | (lax.axis_index("azi") > 0)
    if window == 2:
        return (lane < LANES - HALO) | (lax.axis_index("azi") < lax.axis_size("azi") - 1)
    return lane >= 0


def early_rows(rows, windows, blocks, outs, fields, pairs, between=lambda stage: None):
    own = slice(HALO, HALO + TILE)
    most, fewer = slice(8, TILE - 8), slice(16, TILE - 16)
    each = range(len(windows))
    keep = [inside(window) for window in windows]
    for i in each:
        for stage in range(4):
            for part in range(2):
                fields[i, stage, part, : HALO + 8] = jnp.zeros((HALO + 8, LANES), jnp.float32)
                fields[i, stage, part, HALO + TILE - 8 :] = jnp.zeros((HALO + 8, LANES), jnp.float32)
        put_parts(fields.at[i, 0], own, rows[i])
    for i in each:
        main = adjoint_rows(fields.at[i, 0], blocks[i], pairs.at[i, 0], -8, MAIN, 0)
        main = jnp.where(keep[i], main, 0.0)
        outs[i][0][...] = main
        put_parts(fields.at[i, 1], slice(HALO - 8, HALO + TILE + 8), main)
    between(0)
    for i in each:
        image = forward_rows(fields.at[i, 1], blocks[i], pairs.at[i, 1], most.start, TILE - 16)
        outs[i][1][most] = image
        put_parts(fields.at[i, 2], slice(HALO + most.start, HALO + most.stop), image)
    between(1)
    for i in each:
        grad = adjoint_rows(fields.at[i, 2], blocks[i], pairs.at[i, 2], most.start, TILE - 16, 16)
        grad = jnp.where(keep[i], grad, 0.0)
        outs[i][2][most] = grad
        put_parts(fields.at[i, 3], slice(HALO + most.start, HALO + most.stop), grad)
    between(2)
    for i in each:
        outs[i][3][fewer] = forward_rows(fields.at[i, 3], blocks[i], pairs.at[i, 3], fewer.start, TILE - 32)
    between(3)


PATCH = 32
REST = LANES - PATCH


def middle_kernel(block_ref, taps_ref, *refs):
    outs, sides = refs[:4], (refs[4:6], refs[6:8])
    high, low, fields, pairs = refs[8:]
    lines = tap_lines(taps_ref[...])
    for offset in range(2 * SLOTS):
        put_band(lines, offset, 1, 0, LANES, (high, low))

    def between(stage):
        for offset in range(3 * stage, 3 * stage + 3):
            put_band(lines, offset, 0, PATCH, REST, sides[0])
            put_band(lines, offset, 2, 0, REST, sides[1])

    def block(part, slot):
        return (high, low)[part][slot * LANES : (slot + 1) * LANES, :]

    rows = middle_window(block_ref[:, :LANES], block_ref[:, LANES:])
    early_rows([rows], (1,), [block], [outs], fields, pairs, between)


def sides_kernel(block_ref, far_ref, near_ref, taps_ref, *refs):
    rest, middle = (refs[:2], refs[2:4]), refs[4:8]
    outs, refs = (refs[8:12], refs[12:16]), refs[16:]
    plain_ref, turned_ref, inner_ref, patches, fields, pairs = refs
    taps = taps_ref[...]
    lines = tap_lines(taps)
    for offset in range(2 * SLOTS):
        put_band(lines, offset, 0, 0, PATCH, (patches.at[0, 0], patches.at[0, 1]))
        put_band(lines, offset, 2, REST, PATCH, (patches.at[1, 0], patches.at[1, 1]))

    def piece(side, part, slot):
        whole = rest[side][part][slot * REST : (slot + 1) * REST, :]
        patch = patches[side, part, slot * PATCH : (slot + 1) * PATCH, :]
        return jnp.concatenate([patch, whole] if side == 0 else [whole, patch], axis=0)

    blocks = [lambda part, slot: piece(0, part, slot), lambda part, slot: piece(1, part, slot)]

    def between(stage):
        if stage == 0:
            plain_ref[...] = jnp.concatenate(row_weights(taps, range(4), False), axis=0)
        if stage == 1:
            turned_ref[...] = jnp.concatenate(row_weights(taps, range(4), True), axis=0)

    halos = side_halos(near_ref, far_ref)
    parts = [side_windows(block_ref, halos, part) for part in range(4)]
    rows = [jnp.concatenate([part[side] for part in parts], axis=0) for side in range(2)]
    early_rows(rows, (0, 2), blocks, outs, fields, pairs, between)
    early = (outs[0], middle, outs[1])
    inner = [[window[0][8 + INNER.start : 8 + INNER.stop] for window in early]]
    inner += [[window[i][INNER] for window in early] for i in range(1, 4)]
    inner_ref[...] = jnp.broadcast_to(record_of(inner, 0), (8, LANES))


GROUP = 32
GROUPS = 3 * LANES // GROUP
EDGE = 4 * RADIUS
COUNT = 24


def row_weights(taps, tiles, turned):
    lane = lanes_of((8, LANES))
    pieces = [[] for _ in tiles]
    for part in range(3):
        u = lane % GROUP
        if turned:
            u = KSIZE - 1 - u
        v = part * (LANES // GROUP) + lane // GROUP
        base = jnp.take_along_axis(taps, jnp.clip(u * KSIZE + v, 0, LANES - 1), axis=1)
        base = jnp.where((u >= 0) & (u < KSIZE) & (v < KSIZE), base, 0.0)
        for piece, tile in zip(pieces, tiles):
            row = jnp.broadcast_to(base[tile : tile + 1], (COUNT, LANES))
            piece.append(pltpu.roll(row, 0, 1, stride=1, stride_axis=0))
    return [jnp.concatenate(piece, axis=1) for piece in pieces]


def spread(rows, sign):
    moved = [rows if v == RADIUS else pltpu.roll(rows, (sign * (v - RADIUS)) % LANES, 1) for v in range(KSIZE)]
    moved.append(jnp.zeros((GROUP * (GROUPS - KSIZE), LANES), rows.dtype))
    return jnp.concatenate(moved, axis=0)


def forward_edge(rows, window, weights):
    before, after, bound = REGIONS[window]
    high, low = [spread(part, -1)[: GROUP * KSIZE] for part in split(rows)]
    both = [weights[COUNT * tile : COUNT * tile + COUNT] for tile in (before, after)]
    result = product(split(jnp.concatenate(both, axis=0)[:, : GROUP * KSIZE]), high, low, ((1,), (0,)))
    return jnp.where(lanes_of((COUNT, LANES)) < bound, result[:COUNT], result[COUNT:])


def adjoint_edge(rows, window, weights):
    before, after, bound = REGIONS[window]
    lane = lanes_of((GROUP, LANES))
    whole = [spread(part, 1) for part in split(rows)]
    high, low = [
        jnp.concatenate(
            [part]
            + [
                jnp.where(lane < bound + v - RADIUS, moved, jnp.zeros_like(moved))
                for v, moved in enumerate(part[GROUP * v : GROUP * v + GROUP] for v in range(KSIZE))
            ]
            + [part[GROUP * KSIZE :]],
            axis=0,
        )
        for part in whole
    ]
    left, right = [weights[COUNT * tile : COUNT * tile + COUNT] for tile in (before, after)]
    return product(split(jnp.concatenate([right, left - right], axis=1)), high, low, ((1,), (0,)))


def edge_rows(side, message, plain, turned, plain_ref, turned_ref, early, outs, edge, fields):
    wide = WINDOWS * LANES
    each = range(WINDOWS)
    base = 16 if side == 0 else -80
    near = slice(24, 64) if side == 0 else slice(0, 40)
    own = slice(8, 48) if side == 0 else slice(80, 120)
    out = slice(16, 40) if side == 0 else slice(24, 48)
    start = (-15, -10, -5, 0) if side == 0 else (123, 118, 113, 108)
    beyond = lax.axis_index("rng") > 0 if side == 0 else lax.axis_index("rng") < lax.axis_size("rng") - 1
    keep = [inside(window) for window in each]
    row = lax.broadcasted_iota(jnp.int32, (EDGE, LANES), 0)
    half = EDGE // 2

    def cols(window):
        return pl.ds(window * LANES, LANES)

    def spot(stage, reach=0, count=EDGE):
        return pl.ds(start[stage] - reach + base, count)

    def in_image(stage, window):
        inner = row >= -start[stage] if side == 0 else row < TILE - start[stage]
        return keep[window] & (beyond | inner)

    row24 = lax.broadcasted_iota(jnp.int32, (HALO, 1), 0)
    if side == 0:
        edge[:HALO] = jnp.where(row24 < HALO - REACH, 0.0, message)
        edge[HALO:] = jnp.zeros((16, wide), jnp.float32)
        strip = slice(4, 36)
    else:
        edge[:16] = jnp.zeros((16, wide), jnp.float32)
        edge[16:] = jnp.where(row24 >= REACH, 0.0, message)
        strip = slice(6, 38)
    for window in each:
        main = early[window][0]
        field = fields.at[0, window]
        if side == 0:
            field[:8] = jnp.zeros((8, LANES), jnp.float32)
            field[8:16] = jnp.where(beyond, main[:8], 0.0)
            field[16:64] = main[8:56]
        else:
            field[:48] = main[88:136]
            field[48:56] = jnp.where(beyond, main[136:], 0.0)
            field[56:] = jnp.zeros((16, LANES), jnp.float32)
        result = adjoint_edge(edge[strip, cols(window)], window, turned)
        field[spot(0), :] += jnp.where(in_image(0, window), result[:EDGE], 0.0)
        outs[0][:, cols(window)] = field[out]
        yield

    out_row = lax.broadcasted_iota(jnp.int32, (4 * COUNT, wide), 0) % COUNT
    mixed = (plain, plain_ref[...]) if side == 0 else (plain_ref[...], plain)
    mixed = jnp.where(out_row < half, *mixed)
    results = []
    for window in each:
        results.append(forward_edge(fields[0, window, spot(1, RADIUS, GROUP), :], window, mixed))
        yield
    for window in each:
        field = fields.at[1, window]
        if side == 0:
            field[:24] = jnp.zeros((24, LANES), jnp.float32)
        else:
            field[40:] = jnp.zeros((32, LANES), jnp.float32)
        field[near] = early[window][1][own]
        field[spot(1), :] = results[window][:EDGE]
        outs[1][:, cols(window)] = field[out]

    in_row = lanes_of((4 * COUNT, wide)) % GROUP
    if side == 0:
        mixed = jnp.where(in_row < half, turned, turned_ref[...])
    else:
        mixed = jnp.where(in_row < EDGE, turned_ref[...], turned)
    for window in each:
        result = adjoint_edge(fields[1, window, spot(2, RADIUS, GROUP), :], window, mixed)
        field = fields.at[2, window]
        if side == 0:
            field[8:24] = jnp.zeros((16, LANES), jnp.float32)
        else:
            field[40:56] = jnp.zeros((16, LANES), jnp.float32)
        field[near] = early[window][2][own]
        field[spot(2), :] = jnp.where(in_image(2, window), result[:EDGE], 0.0)
        outs[2][:, cols(window)] = field[out]
        yield

    results = []
    for window in each:
        results.append(forward_edge(fields[2, window, spot(3, RADIUS, GROUP), :], window, plain_ref[...]))
        yield
    for window in each:
        rest = COUNT - EDGE
        if side == 0:
            outs[3][EDGE:, cols(window)] = early[window][3][EDGE:COUNT]
            outs[3][:EDGE, cols(window)] = results[window][:EDGE]
        else:
            outs[3][:rest, cols(window)] = early[window][3][TILE - COUNT : TILE - EDGE]
            outs[3][rest:, cols(window)] = results[window][:EDGE]
    yield


INNER = slice(COUNT, TILE - COUNT)


def record_of(values, position):
    lane = lanes_of((1, LANES))
    bounds = ((24, 108), (20, 108), (20, 104))

    def total(pieces):
        sums = [
            jnp.where((lane >= low) & (lane < high), jnp.sum(piece, axis=0, keepdims=True), 0.0)
            for piece, (low, high) in zip(pieces, bounds)
        ]
        return jnp.sum(sums[0] + sums[1] + sums[2], axis=1, keepdims=True)

    def best(first, second):
        size = total([b * b for b in second])
        cross = total([a * b for a, b in zip(first, second)])
        ratio = jnp.where(size > 0.0, cross / jnp.where(size > 0.0, size, 1.0), 0.0)
        rest = total([(a - ratio * b) ** 2 for a, b in zip(first, second)])
        return total([a * a for a in first]), size, ratio, rest

    grad, image, grad2, image2 = values
    line = jnp.zeros((1, LANES), jnp.float32)
    for index, value in enumerate(best(grad, grad2) + best(image, image2)):
        line = jnp.where(lane == position + index, value, line)
    return line


def edge_kernel(*refs):
    early = [refs[4 * window : 4 * window + 4] for window in (1, 0, 2)]
    two_ref, one_ref, plain_ref, turned_ref, inner_ref = refs[12:17]
    tops, lows, record_ref, edge, fields = refs[17:21], refs[21:25], *refs[25:]
    odd = is_odd("rng")
    one, two = one_ref[...], two_ref[...]
    has_above = lax.axis_index("rng") > 0
    has_below = lax.axis_index("rng") < lax.axis_size("rng") - 1
    above = jnp.where(has_above, jnp.where(odd, one, two), 0.0)
    below = jnp.where(has_below, jnp.where(odd, two, one), 0.0)
    row = lax.broadcasted_iota(jnp.int32, (8, LANES), 0)
    taps = jnp.where(row < 4, above[:8, :LANES], below[HALO - 8 :, :LANES])
    turned, plain = row_weights(taps, range(8), True), row_weights(taps, range(8), False)
    (turned, turned_low), (plain, plain_low) = [
        [jnp.concatenate(weights[side : side + 4], axis=0) for side in (0, 4)] for weights in (turned, plain)
    ]
    top = edge_rows(0, above, plain, turned, plain_ref, turned_ref, early, tops, edge.at[0], fields.at[0])
    low = edge_rows(1, below, plain_low, turned_low, plain_ref, turned_ref, early, lows, edge.at[1], fields.at[1])
    for _ in zip(top, low):
        pass

    def windows(i):
        both = jnp.concatenate([tops[i][...], lows[i][...]], axis=0)
        return [both[:, w * LANES : (w + 1) * LANES] for w in range(WINDOWS)]

    line = inner_ref[:1] + record_of([windows(i) for i in range(4)], 8)
    record_ref[...] = jnp.broadcast_to(line[None], record_ref.shape)


def combine_kernel(records_ref, block_ref, *refs):
    early = [refs[4 * window : 4 * window + 4] for window in (1, 0, 2)]
    tops, lows, (estimate_ref, residual_ref) = refs[12:16], refs[16:20], refs[20:]
    records = records_ref[:, 0, :]
    lane = lanes_of((1, LANES))

    def total(value, place):
        wanted = (lane % 8 == place) & (lane < 24)
        return jnp.sum(jnp.where(wanted, jnp.sum(value, axis=0, keepdims=True), 0.0), axis=1, keepdims=True)

    gamma = total(records, 0)
    delta = total(records, 4)
    alpha = gamma / delta
    apart = records + (alpha - pltpu.roll(records, 1, 1)) ** 2 * pltpu.roll(records, 2, 1)
    gamma_new = total(apart, 3)
    bent = total(apart, 7)
    factor = gamma_new / gamma
    delta_new = bent - factor * factor * delta
    alpha_new = gamma_new / delta_new
    first = alpha + alpha_new * (1.0 + factor)
    second = -alpha_new * alpha

    def own(a, b):
        parts = [first * a[w] + second * b[w] for w in range(WINDOWS)]
        lanes = lanes_of(parts[0].shape)
        middle = pltpu.roll(parts[1], 64, 1)
        left = jnp.where(lanes < 84, pltpu.roll(parts[0], LANES - HALO, 1), middle)
        right = jnp.where(lanes < 44, middle, pltpu.roll(parts[2], HALO, 1))
        return left, right

    def windows(ref):
        return [ref[:, w * LANES : (w + 1) * LANES] for w in range(WINDOWS)]

    for rows, pieces in (
        (slice(0, COUNT), lambda i: windows(tops[i])),
        (INNER, lambda i: [early[w][i][slice(8 + COUNT, 8 + TILE - COUNT) if i == 0 else INNER] for w in range(WINDOWS)]),
        (slice(TILE - COUNT, TILE), lambda i: windows(lows[i])),
    ):
        left, right = own(pieces(0), pieces(2))
        estimate_ref[rows, :LANES] = left
        estimate_ref[rows, LANES:] = right
        left, right = own(pieces(1), pieces(3))
        residual_ref[rows, :LANES] = block_ref[rows, :LANES] - left
        residual_ref[rows, LANES:] = block_ref[rows, LANES:] - right


def partners(axis, other):
    count, across = lax.axis_size(axis), lax.axis_size(other)

    def number(i, j):
        return i * across + j if axis == "rng" else j * count + i

    near, far = [], []
    for i in range(count):
        for j in range(across):
            near.append((number(i, j), number(i ^ 1, j)))
            beside = i + 1 if i % 2 else i - 1
            far.append((number(i, j), number(beside, j) if 0 <= beside < count else number(i, j ^ 1)))
    return near, far


BOTH = ("rng", "azi")


def body(observed, psf_tiles):
    devices = lax.axis_size("rng") * lax.axis_size("azi")
    wide = WINDOWS * LANES
    block, own, far, near = call(
        load_kernel,
        [f32(TILE, 2 * LANES), f32(8, LANES), f32(40, LANES), f32(40, LANES)],
        [pltpu.VMEM((1, 2, TAPS), jnp.float32), pltpu.SemaphoreType.DMA((CHUNKS + 1,))],
        inputs=[pl.BlockSpec(memory_space=pltpu.HBM)] * 2,
    )(
        pltpu.with_memory_space_constraint(observed, pltpu.HBM),
        pltpu.with_memory_space_constraint(psf_tiles, pltpu.HBM),
    )
    near_pairs, far_pairs = partners("azi", "rng")
    far = lax.ppermute(far, BOTH, far_pairs)
    near = lax.ppermute(near, BOTH, near_pairs)
    early = [f32(MAIN, LANES)] + [f32(TILE, LANES)] * 3
    rest = [jax.ShapeDtypeStruct((SLOTS * REST, 2 * LANES), jnp.bfloat16)] * 4

    def scratch(windows):
        return [
            pltpu.VMEM((windows, 4, 2, ROWS, LANES), jnp.float32),
            pltpu.VMEM((windows, 4, MAIN + 8, LANES), jnp.float32),
        ]

    *middle, high0, low0, high2, low2 = call(
        middle_kernel, early + rest, [pltpu.VMEM((DEPTH, 2 * LANES), jnp.bfloat16)] * 2 + scratch(1), limit=8
    )(block, own)
    taps, two, one = call(
        rows_kernel,
        [f32(8, LANES), f32(HALO, wide), f32(HALO, wide)],
        [pltpu.VMEM((HALO, wide), jnp.float32)] * 2,
    )(block, own, far, near, middle[0])
    one_pairs, two_pairs = partners("rng", "azi")
    two = lax.ppermute(two, BOTH, two_pairs)
    one = lax.ppermute(one, BOTH, one_pairs)
    *sides, plain, turned, inner = call(
        sides_kernel,
        early * 2 + [f32(4 * COUNT, wide)] * 2 + [f32(8, LANES)],
        [pltpu.VMEM((2, 2, SLOTS * PATCH, 2 * LANES), jnp.bfloat16)] + scratch(2),
        limit=8,
    )(block, far, near, taps, high0, low0, high2, low2, *middle)
    *edges, record = call(
        edge_kernel,
        [f32(COUNT, wide)] * 8 + [f32(devices, 1, LANES)],
        [pltpu.VMEM((2, 40, wide), jnp.float32), pltpu.VMEM((2, 3, WINDOWS, 72, LANES), jnp.float32)],
        limit=8,
    )(*middle, *sides, two, one, plain, turned, inner)
    records = lax.all_to_all(record, BOTH, 0, 0, tiled=True)
    estimate, residual = call(combine_kernel, [f32(TILE, 2 * LANES)] * 2)(
        records, block, *middle, *sides, *edges
    )
    return estimate, residual


def solution(mesh):
    return jax.shard_map(
        body,
        mesh=mesh,
        in_specs=(P("rng", "azi"), P("rng", "azi", None)),
        out_specs=(P("rng", "azi"), P("rng", "azi")),
        check_vma=False,
    )
```
